128 devices in a mesh: gz: 32 (over y, x, core), gy: 4 (over z).
Axes of the slice: x: 4, y: 4, z: 4, core: 2. Of those that a mesh axis runs over, the one named last changes fastest.
Arguments:
- flow_state: float32 [7, 768, 128, 128], P(None, 'gz', 'gy'), may hold values from -1.1 to 6, as said below
- block_tiles: int32 [32768, 4], P(('gz', 'gy')), may hold values from 0 to 98303, as said below
- bubble_place: float32 [3, 32768, 128], P(None, ('gz', 'gy')), may hold values from 0 to 1
- bubble_radius: float32 [32768, 128], P(('gz', 'gy')), may hold values from 0.2 to 0.5
- bubble_speed: float32 [32768, 128], P(('gz', 'gy')), may hold values from -3 to 3
- rest_ratio: float32 [32768, 128], P(('gz', 'gy')), may hold values from 0.8 to 1.25
Outputs:
- state_next: float32 [7, 768, 128, 128], P(None, 'gz', 'gy')
- bubble_source: float32 [768, 128, 128], P('gz', 'gy')
- bubble_motion: float32 [2, 32768, 128], P(None, ('gz', 'gy'))
The draws below stay inside these ranges and needn't reach their ends.
Inputs may be any that keep to these rules, and one draw needn't show every extreme that they name: `flow_state`: conserved variables of primitives with liquid fraction 0.4 to 0.6, liquid density 0.7 to 1.4, gas density 0.05 to 0.1, each velocity component within 1.2, pressure 0.6 to 1.2; the partial densities are those fractions times the densities. `block_tiles`: each block lists rows (z, y), (z, y + 1), (z + 1, y), (z + 1, y + 1), all on one device's cells (z % 24 < 23, y % 32 < 31). Among the 256 blocks of one device, each device whose cells are named is named by exactly 8 blocks; one device is named so by every device.
All inputs are finite; a program needn't handle non-finite values.
Results may differ from the reference program's by a relative error of at most 0.0003.
Values sent between devices are 32-bit elements; how exact they have to be, the bound alone decides.
No kernel may reach another device: no remote copies, remote signals or barrier semaphores. Data moves between devices by JAX's collectives and lax.ppermute only.
A program may use at most 128 MiB of HBM per device.

```python
import math
import jax
import jax.numpy as jnp
from jax import lax

CZ = 24
CY = 32
CX = 128
BB = 128
BPD = 256
HB = 8
NZ = 768
NY = 128
NBLK = 32768
N_GY = 4
DEVICES = 128


def mixture_drawn(fraction):
    stiffness = fraction / 3.4 + (1.0 - fraction) / 0.4
    offset_term = fraction * 4.4 * 3.0 / 3.4
    return (stiffness, offset_term)


def draw_flow_state(key, part):
    key = jax.random.fold_in(key, 5)
    subkeys = jax.random.split(key, 5)
    grid_shape = (NZ, NY, CX)
    fraction = jax.random.uniform(subkeys[0], grid_shape, jnp.float32, 0.4, 0.6)
    liquid = jax.random.uniform(subkeys[1], grid_shape, jnp.float32, 0.7, 1.4)
    gas_density = jax.random.uniform(subkeys[2], grid_shape, jnp.float32, 0.05, 0.1)
    velocity = jnp.clip(0.3 * jax.random.normal(subkeys[3], (3,) + grid_shape, jnp.float32), -1.2, 1.2)
    pressure = jax.random.uniform(subkeys[4], grid_shape, jnp.float32, 0.6, 1.2)
    liquid_part = fraction * liquid
    gas_part = (1.0 - fraction) * gas_density
    density = liquid_part + gas_part
    stiffness, offset_term = mixture_drawn(fraction)
    energy = stiffness * pressure + offset_term + 0.5 * density * jnp.sum(velocity * velocity, axis=0)
    return jnp.concatenate([liquid_part[None], gas_part[None], density[None] * velocity, energy[None], fraction[None]], axis=0).astype(jnp.float32)


def draw_block_tiles(key, part):
    key = jax.random.fold_in(key, 11)
    center_key, score_key, order_key, level_key, column_key = jax.random.split(key, 5)
    homes_each = BPD // HB
    center = jax.random.randint(center_key, (), 0, DEVICES)
    device_ids = jnp.arange(DEVICES)
    distance = (device_ids - center) % DEVICES
    home_bias = jnp.where(distance == 0, 4, jnp.where(distance < DEVICES // 4, 1, 0))
    random_noise = jax.random.randint(score_key, (DEVICES, DEVICES), 0, 4096)
    corner_bias = jnp.where((device_ids[:, None] == 0) & (device_ids[None, :] == DEVICES - 1), 8, 0)
    scores = (random_noise + (home_bias[None, :] + corner_bias) * 4096) * DEVICES + device_ids[None, :]
    chosen = lax.top_k(scores, homes_each)[1]
    home_list = jnp.repeat(chosen, HB, axis=1)
    block_order = jnp.argsort(jax.random.randint(order_key, (DEVICES, BPD), 0, 1 << 20) * BPD + jnp.arange(BPD)[None, :], axis=1)
    home_list = jnp.take_along_axis(home_list, block_order, axis=1).reshape(-1)
    local_level = jax.random.randint(level_key, (NBLK,), 0, CZ - 1)
    local_column = jax.random.randint(column_key, (NBLK,), 0, CY - 1)
    to_last = (home_list == DEVICES - 1).astype(jnp.int32)
    first_last = jnp.argmax(to_last)
    is_corner = jnp.arange(NBLK) == first_last
    local_level = jnp.where(is_corner, CZ - 2, local_level)
    local_column = jnp.where(is_corner, CY - 2, local_column)
    grid_level = home_list // N_GY * CZ + local_level
    column = home_list % N_GY * CY + local_column
    anchor = grid_level * NY + column
    return jnp.stack([anchor, anchor + 1, anchor + NY, anchor + NY + 1], axis=1).astype(jnp.int32)


def level_of(key, shape, shards, low, largest):
    gain, own = 1.0, jax.random.fold_in(key, 6)
    for dim, shards_of in shards:
        heights = jnp.exp(jax.random.uniform(jax.random.fold_in(own, dim), (shards_of,), jnp.float32, low / len(shards), largest / len(shards)))
        gain = gain * jnp.repeat(heights, shape[dim] // shards_of).reshape([-1 if axis == dim else 1 for axis in range(len(shape))])
    return gain


def noise(stream_key, extent, spread, bound, pieces=(), dtype=jnp.bfloat16):
    level = level_of(stream_key, extent, pieces, -0.22, 0.18) if pieces else 1.0
    values = jax.random.normal(stream_key, extent, jnp.float32) * spread * level
    return jnp.minimum(jnp.maximum(values, -bound), bound).astype(dtype)


def setup_inputs(seed: int = 0) -> dict:
    arg_keys = jax.random.split(jax.random.key(seed), 7)
    return {
        "flow_state": draw_flow_state(jax.random.fold_in(arg_keys[6], 71), 0),
        "block_tiles": draw_block_tiles(jax.random.fold_in(arg_keys[6], 71), 0),
        "bubble_place": jnp.clip(1.0 * jax.random.uniform(arg_keys[2], (3, NBLK, BB), jnp.float32) ** level_of(arg_keys[2], (3, NBLK, BB), ((1, 128),), -0.2, 0.2), 0.0, 1.0),
        "bubble_radius": jnp.clip(0.2 + 0.3 * jax.random.uniform(arg_keys[3], (NBLK, BB), jnp.float32) ** level_of(arg_keys[3], (NBLK, BB), ((0, 128),), -0.2, 0.2), 0.2, 0.5),
        "bubble_speed": noise(arg_keys[4], (NBLK, BB), 0.5, 3.0, ((0, 128),), jnp.float32),
        "rest_ratio": jnp.clip(jnp.exp(math.log(1.25) - 0.4462871 * jax.random.uniform(arg_keys[5], (NBLK, BB), jnp.float32) ** level_of(arg_keys[5], (NBLK, BB), ((0, 128),), -0.2, 0.2)), 0.8, 1.25),
    }


gamma_liquid = 4.4
stiff_liquid = 3.0
gamma_gas = 1.4
time_step = 0.08
liquid_sound = 20.0
surface_tension = 0.01
liquid_viscosity = 0.001
polytropic = 1.4
weno_eps = 1e-06
highest = lax.Precision.HIGHEST

def mixture(fraction):
    stiffness = fraction / (gamma_liquid - 1.0) + (1.0 - fraction) / (gamma_gas - 1.0)
    offset_term = fraction * gamma_liquid * stiff_liquid / (gamma_liquid - 1.0)
    return (stiffness, offset_term)

def primitives(flow_state):
    density = flow_state[0] + flow_state[1]
    velocity = flow_state[2:5] / density
    stiffness, offset_term = mixture(flow_state[6])
    kinetic = 0.5 * density * lax.optimization_barrier(jnp.sum(velocity * velocity, axis=0))
    pressure = (flow_state[5] - kinetic - offset_term) / stiffness
    return jnp.concatenate([flow_state[0:2], velocity, pressure[None], flow_state[6:7]], axis=0)

def weno_side(cell_first, cell_second, cell_third, cell_fourth, cell_fifth):
    guess_low = (2.0 * cell_first - 7.0 * cell_second + 11.0 * cell_third) / 6.0
    guess_mid = (-cell_second + 5.0 * cell_third + 2.0 * cell_fourth) / 6.0
    guess_high = (2.0 * cell_third + 5.0 * cell_fourth - cell_fifth) / 6.0
    smooth_low = 13.0 / 12.0 * (cell_first - 2.0 * cell_second + cell_third) ** 2 + 0.25 * (cell_first - 4.0 * cell_second + 3.0 * cell_third) ** 2
    smooth_mid = 13.0 / 12.0 * (cell_second - 2.0 * cell_third + cell_fourth) ** 2 + 0.25 * (cell_second - cell_fourth) ** 2
    smooth_high = 13.0 / 12.0 * (cell_third - 2.0 * cell_fourth + cell_fifth) ** 2 + 0.25 * (3.0 * cell_third - 4.0 * cell_fourth + cell_fifth) ** 2
    weight_low = 0.1 / (weno_eps + smooth_low) ** 2
    weight_mid = 0.6 / (weno_eps + smooth_mid) ** 2
    weight_high = 0.3 / (weno_eps + smooth_high) ** 2
    return (weight_low * guess_low + weight_mid * guess_mid + weight_high * guess_high) / (weight_low + weight_mid + weight_high)

def face_states(padded, array_axis):
    cell_count = padded.shape[array_axis] - 6

    def face_slice(first_index):
        return lax.slice_in_dim(padded, first_index, first_index + cell_count + 1, axis=array_axis)
    left_state = weno_side(face_slice(0), face_slice(1), face_slice(2), face_slice(3), face_slice(4))
    right_state = weno_side(face_slice(5), face_slice(4), face_slice(3), face_slice(2), face_slice(1))
    return (left_state, right_state)

def side_terms(primitive, normal):
    density = primitive[0] + primitive[1]
    velocity = primitive[2:5]
    normal_speed = velocity[normal]
    pressure = primitive[5]
    stiffness, offset_term = mixture(primitive[6])
    sound_speed = jnp.sqrt((pressure * (stiffness + 1.0) + offset_term) / (stiffness * density))
    energy = stiffness * pressure + offset_term + 0.5 * density * lax.optimization_barrier(jnp.sum(velocity * velocity, axis=0))
    momentum = density * velocity
    conserved = jnp.concatenate([primitive[0:2], momentum, energy[None]], axis=0)
    unit_vector = (jnp.arange(3) == normal).astype(jnp.float32).reshape((3,) + (1,) * (primitive.ndim - 1))
    face_flux = jnp.concatenate([primitive[0:2] * normal_speed, momentum * normal_speed + pressure * unit_vector, ((energy + pressure) * normal_speed)[None]], axis=0)
    return (density, normal_speed, pressure, sound_speed, conserved, face_flux, unit_vector)

def star_flux(primitive, terms, wave_speed, middle):
    density, normal_speed, pressure, sound_speed, conserved, face_flux, unit_vector = terms
    factor = (wave_speed - normal_speed) / (wave_speed - middle)
    star_velocity = primitive[2:5] * (1.0 - unit_vector) + middle * unit_vector
    star_energy = conserved[5] + (middle - normal_speed) * (density * middle + pressure / (wave_speed - normal_speed))
    star_state = factor * jnp.concatenate([primitive[0:2], density * star_velocity, star_energy[None]], axis=0)
    return face_flux + wave_speed * (star_state - conserved)

def hllc_flux(left_state, right_state, normal):
    terms_left = side_terms(left_state, normal)
    terms_right = side_terms(right_state, normal)
    density_left, speed_left, pressure_left, sound_left = terms_left[0:4]
    density_right, speed_right, pressure_right, sound_right = terms_right[0:4]
    wave_left = jnp.minimum(speed_left - sound_left, speed_right - sound_right)
    wave_right = jnp.maximum(speed_left + sound_left, speed_right + sound_right)
    middle = (pressure_right - pressure_left + density_left * speed_left * (wave_left - speed_left) - density_right * speed_right * (wave_right - speed_right)) / (density_left * (wave_left - speed_left) - density_right * (wave_right - speed_right))
    star_left = star_flux(left_state, terms_left, wave_left, middle)
    star_right = star_flux(right_state, terms_right, wave_right, middle)
    face_flux = jnp.where(wave_left >= 0.0, terms_left[5], jnp.where(middle >= 0.0, star_left, jnp.where(wave_right > 0.0, star_right, terms_right[5])))
    fraction_flux = middle * jnp.where(middle >= 0.0, left_state[6], right_state[6])
    return (jnp.concatenate([face_flux, fraction_flux[None]], axis=0), middle)

def flux_sweep(padded, array_axis, normal):
    left_state, right_state = face_states(padded, array_axis)
    face_flux, middle = hllc_flux(left_state, right_state, normal)
    cell_count = padded.shape[array_axis] - 6
    upper_flux = lax.slice_in_dim(face_flux, 1, cell_count + 1, axis=array_axis)
    lower_flux = lax.slice_in_dim(face_flux, 0, cell_count, axis=array_axis)
    cell_values = lax.slice_in_dim(padded, 3, cell_count + 3, axis=array_axis)
    divergence = lax.slice_in_dim(middle, 1, cell_count + 1, axis=array_axis - 1) - lax.slice_in_dim(middle, 0, cell_count, axis=array_axis - 1)
    change = lower_flux - upper_flux
    return jnp.concatenate([change[:6], (change[6] + cell_values[6] * divergence)[None]], axis=0)

def bubble_block(row_tiles, places, radius, wall_speed, rest_ratio):
    cell_count = row_tiles.shape[-1]
    lateral = jnp.arange(4)
    shift_level = (lateral // 2).astype(jnp.float32)
    shift_column = (lateral % 2).astype(jnp.float32)
    offset_level = places[:, 0]
    offset_column = places[:, 1]
    offset_along = places[:, 2] * (cell_count - 1)
    across = jnp.exp(-((shift_level[None, None, :] - offset_level[..., None]) ** 2 + (shift_column[None, None, :] - offset_column[..., None]) ** 2) / 2.0)
    positions = jnp.arange(cell_count).astype(jnp.float32)
    along = jnp.exp(-(positions[None, None, :] - offset_along[..., None]) ** 2 / 2.0)
    weight_total = lax.optimization_barrier(jnp.sum(across, axis=-1)) * lax.optimization_barrier(jnp.sum(along, axis=-1))
    rowwise = jnp.einsum('gbx,gkx->gbk', along, row_tiles, precision=highest)
    sampled = lax.optimization_barrier(jnp.sum(across * rowwise, axis=-1)) / weight_total
    rest_radius = rest_ratio * radius
    gas_pressure = (1.0 + 2.0 * surface_tension / rest_radius) * (rest_radius / radius) ** (3.0 * polytropic)
    wall_pressure = gas_pressure - 2.0 * surface_tension / radius - 4.0 * liquid_viscosity * wall_speed / radius
    gas_rate = -3.0 * polytropic * gas_pressure * wall_speed / radius
    mach_number = wall_speed / liquid_sound
    acceleration = ((1.0 + mach_number) * (wall_pressure - sampled) + radius * gas_rate / liquid_sound - 1.5 * (1.0 - mach_number / 3.0) * wall_speed ** 2) / ((1.0 - mach_number) * radius)
    motion = jnp.stack([radius + time_step * wall_speed, wall_speed + time_step * acceleration], axis=1)
    share_rate = 4.0 * math.pi * radius * radius * wall_speed / weight_total
    deposit = jnp.einsum('gbk,gbx->gkx', across * share_rate[..., None], along, precision=highest)
    return (motion, deposit)

def reference(flow_state, block_tiles, bubble_place, bubble_radius, bubble_speed, rest_ratio):
    primitive = primitives(flow_state)
    change = jnp.zeros(flow_state.shape, jnp.float32)
    for array_axis, normal in ((3, 0), (2, 1), (1, 2)):
        widths = [(0, 0), (0, 0), (0, 0), (0, 0)]
        widths[array_axis] = (3, 3)
        padded = jnp.pad(primitive, widths, mode='wrap')
        change = change + flux_sweep(padded, array_axis, normal)
    pressure_rows = primitive[5].reshape(NZ * NY, CX)
    row_tiles = pressure_rows[block_tiles]
    places = jnp.transpose(bubble_place, (1, 0, 2))
    group_size = math.gcd(NBLK, 64)

    def regroup(values):
        return values.reshape((NBLK // group_size, group_size) + values.shape[1:])

    def one_group(inputs):
        return bubble_block(inputs[0], inputs[1], inputs[2], inputs[3], inputs[4])
    motion, deposit = lax.map(one_group, (regroup(row_tiles), regroup(places), regroup(bubble_radius), regroup(bubble_speed), regroup(rest_ratio)))
    motion = motion.reshape(NBLK, 2, BB)
    deposit = deposit.reshape(NBLK, 4, CX)
    source_rows = jnp.zeros((NZ * NY, CX), jnp.float32).at[block_tiles].add(deposit)
    bubble_source = source_rows.reshape(NZ, NY, CX)
    state_next = flow_state + time_step * change
    state_next = jnp.concatenate([state_next[:6], (state_next[6] - time_step * bubble_source)[None]], axis=0)
    return (state_next, bubble_source, jnp.transpose(motion, (1, 0, 2)))
```

```python
import functools
import math

import jax
import jax.numpy as jnp
from jax import lax
from jax.experimental import pallas as pl
from jax.experimental.pallas import tpu as pltpu
from jax.sharding import PartitionSpec as P

HB = 8
gamma_liquid = 4.4
stiff_liquid = 3.0
gamma_gas = 1.4
time_step = 0.08
liquid_sound = 20.0
surface_tension = 0.01
liquid_viscosity = 0.001
polytropic = 1.4
weno_eps = 1e-06
stiff_base = 1.0 / (gamma_gas - 1.0)
stiff_slope = 1.0 / (gamma_liquid - 1.0) - 1.0 / (gamma_gas - 1.0)
offset_slope = gamma_liquid * stiff_liquid / (gamma_liquid - 1.0)
pressure_mid = 0.9

VMEM = pl.BlockSpec(memory_space=pltpu.VMEM)
SMEM = pl.BlockSpec(memory_space=pltpu.SMEM)
F32 = jnp.float32
BF16 = jnp.bfloat16


def params(mib=56):
    return pltpu.CompilerParams(vmem_limit_bytes=mib * 2**20)


def shape(dims, dtype=F32):
    return jax.ShapeDtypeStruct(dims, dtype)


def cost(flops, nbytes):
    return pl.CostEstimate(flops=int(flops), bytes_accessed=int(nbytes), transcendentals=0)


def inverse(value):
    guess = pl.reciprocal(value, approx=True)
    return guess * (2.0 - value * guess)


def rough_inverse(value):
    return pl.reciprocal(value, approx=True)


def dot_nt(left, right):
    return lax.dot_general(left, right, (((1,), (1,)), ((), ())), preferred_element_type=F32)


def dot_nn(left, right):
    return lax.dot_general(left, right, (((1,), (0,)), ((), ())), preferred_element_type=F32)


def slot_kernel(home_ref, level_ref, column_ref, slot_ref, wanted_ref, *, height):
    devices = wanted_ref.shape[0]
    blocks = home_ref.shape[1]
    home = home_ref[...]
    onehot = lax.broadcasted_iota(jnp.int32, (devices, blocks), 0) == home
    onehot = jnp.where(onehot, 1.0, 0.0).astype(F32)
    onehot_bf = onehot.astype(BF16)
    earlier = lax.broadcasted_iota(jnp.int32, (blocks, blocks), 0) < lax.broadcasted_iota(
        jnp.int32, (blocks, blocks), 1
    )
    earlier = jnp.where(earlier, 1.0, 0.0).astype(BF16)
    before = dot_nn(onehot_bf, earlier)
    rank = jnp.sum(onehot * before, axis=0, keepdims=True)
    rank = jnp.minimum(rank, HB - 1.0)
    slot_ref[...] = home * HB + rank.astype(jnp.int32)
    chosen = lax.broadcasted_iota(jnp.int32, (HB, blocks), 0).astype(F32) == rank
    level = jnp.where(chosen, level_ref[...].astype(F32) + 1.0, 0.0).astype(BF16)
    column = jnp.where(chosen, column_ref[...].astype(F32), 0.0).astype(BF16)
    level = dot_nt(onehot_bf, level)
    column = dot_nt(onehot_bf, column)
    row = (level - 1.0) * float(height) + column
    wanted_ref[...] = jnp.where(level > 0.0, row, -1.0).astype(jnp.int32)


def primitive_kernel(flow_ref, prim_ref, z_low_ref, z_high_ref, y_low_ref, y_high_ref):
    depth, height = flow_ref.shape[1], flow_ref.shape[2]

    def slab(z, carry):
        first, second = flow_ref[0, z], flow_ref[1, z]
        density = first + second
        inv_density = inverse(density)
        mom = [flow_ref[2 + i, z] for i in range(3)]
        vel = [m * inv_density for m in mom]
        kinetic = 0.5 * (mom[0] * vel[0] + mom[1] * vel[1] + mom[2] * vel[2])
        fraction = flow_ref[6, z]
        stiffness = stiff_base + stiff_slope * fraction
        pressure = (flow_ref[5, z] - kinetic - offset_slope * fraction) * inverse(stiffness)
        for i, value in enumerate([first, second] + vel + [pressure, fraction]):
            prim_ref[i, z] = value
            for j in range(3):
                y_low_ref[i, j, pl.ds(z, 1), :] = value[j : j + 1]
                y_high_ref[i, j, pl.ds(z, 1), :] = value[height - 3 + j : height - 2 + j]
        return carry

    lax.fori_loop(0, depth, slab, 0)
    for i in range(7):
        for j in range(3):
            z_low_ref[i, j] = prim_ref[i, j]
            z_high_ref[i, j] = prim_ref[i, depth - 3 + j]


def weno_pair(cell, dm2, dm1, d0, dp1, zm, z0, zp):
    qm = dm1 + d0
    ql = 3.0 * dm1 - dm2
    qh = dp1 - 3.0 * d0
    tl = zm + ql * ql
    tm = z0 + qm * qm
    th = zp + qh * qh
    tl = tl * tl
    tm = tm * tm
    th = th * th
    low = tm * th
    mid = 6.0 * (tl * th)
    high = tl * tm
    low3 = 3.0 * low
    high3 = 3.0 * high
    den_up = 6.0 * (low + mid + high3)
    den_down = 6.0 * (low3 + mid + high)
    num_up = low * (2.0 * ql - dm1) + mid * (qm + d0) + high3 * (d0 - qh)
    num_down = low3 * (ql + dm1) + mid * (qm + dm1) - high * (2.0 * qh + d0)
    return cell + num_up * rough_inverse(den_up), cell - num_down * rough_inverse(den_down)


def curvature(step):
    return (13.0 / 3.0) * (step * step) + 4.0 * weno_eps


def sound_terms(state):
    density = state[0] + state[1]
    stiff_one = (stiff_base + 1.0) + stiff_slope * state[6]
    enthalpy = state[5] * stiff_one + offset_slope * state[6]
    sound = enthalpy * lax.rsqrt(enthalpy * ((stiff_one - 1.0) * density))
    return density, enthalpy, sound


def hllc(left, right, normal):
    density_l, enthalpy_l, sound_l = sound_terms(left)
    density_r, enthalpy_r, sound_r = sound_terms(right)
    speed_l, speed_r = left[2 + normal], right[2 + normal]
    wave_l = jnp.minimum(speed_l - sound_l, speed_r - sound_r)
    wave_r = jnp.maximum(speed_l + sound_l, speed_r + sound_r)
    mass_l = density_l * (wave_l - speed_l)
    mass_r = density_r * (wave_r - speed_r)
    middle = (right[5] - left[5] + mass_l * speed_l - mass_r * speed_r) * inverse(mass_l - mass_r)
    forward = middle >= 0.0
    use_left = (wave_l >= 0.0) | forward
    one = [jnp.where(use_left, a, b) for a, b in zip(left[:6], right[:6])]
    density = jnp.where(use_left, density_l, density_r)
    enthalpy = jnp.where(use_left, enthalpy_l, enthalpy_r)
    wave = jnp.where(use_left, jnp.minimum(wave_l, 0.0), jnp.maximum(wave_r, 0.0))
    speed, pressure = one[2 + normal], one[5]
    ratio = jnp.where(wave != 0.0, wave * inverse(wave - middle), 0.0)
    extra = ratio * (middle - speed)
    carried = speed + extra
    push = density * (extra * (wave - speed))
    mass = density * carried
    kinetic = 0.5 * density * (one[2] * one[2] + one[3] * one[3] + one[4] * one[4])
    flux = [one[0] * carried, one[1] * carried]
    for i in range(3):
        flow = mass * one[2 + i]
        flux.append(flow + (push + pressure) if i == normal else flow)
    flux.append((enthalpy + kinetic) * carried + push * middle)
    flux.append(middle * jnp.where(forward, left[6], right[6]))
    return flux, middle


def x_kernel(prim_ref, change_ref, left_ref, right_ref):
    depth, height, length = prim_ref.shape[1:]

    def slab(z, carry):
        for i in range(7):
            cell = prim_ref[i, z]
            d0 = pltpu.roll(cell, length - 1, 1) - cell
            dm1 = pltpu.roll(d0, 1, 1)
            dm2 = pltpu.roll(d0, 2, 1)
            dp1 = pltpu.roll(d0, length - 1, 1)
            z0 = curvature(d0 - dm1)
            zm = pltpu.roll(z0, 1, 1)
            zp = pltpu.roll(z0, length - 1, 1)
            up, down = weno_pair(cell, dm2, dm1, d0, dp1, zm, z0, zp)
            left_ref[i] = up
            right_ref[i] = pltpu.roll(down, length - 1, 1)
        for part in range(height // 16):
            rows = pl.ds(16 * part, 16)
            left = [left_ref[i, rows] for i in range(7)]
            right = [right_ref[i, rows] for i in range(7)]
            flux, middle = hllc(left, right, 0)
            for i in range(6):
                change_ref[i, z, rows] = pltpu.roll(flux[i], 1, 1) - flux[i]
            fraction = prim_ref[6, z, rows]
            change_ref[6, z, rows] = (pltpu.roll(flux[6], 1, 1) - flux[6]) + fraction * (
                middle - pltpu.roll(middle, 1, 1)
            )
        return carry

    lax.fori_loop(0, depth, slab, 0)


def row_sweep(cells_ref, step_ref, curve_ref, left_ref, right_ref, flux_ref, stride, first, last, normal):
    def chunk_of(begin, end, size):
        count = -(-(end - begin) // size)
        return count, lambda k: pl.multiple_of(begin + k * size, 8)

    size = 32
    begin = first - 2 * stride if stride % 8 == 0 else first - 8
    count, at = chunk_of(begin, last + 2 * stride, size)

    for i in range(7):

        def prepare(k, carry, i=i):
            row = at(k)
            mid = cells_ref[i, pl.ds(row, size)]
            d0 = cells_ref[i, pl.ds(row + stride, size)] - mid
            dm1 = mid - cells_ref[i, pl.ds(row - stride, size)]
            step_ref[pl.ds(row, size)] = d0
            curve_ref[pl.ds(row, size)] = curvature(d0 - dm1)
            return carry

        if stride % 8 == 0:
            edge = pl.ds(first - 3 * stride, size)
            step_ref[edge] = cells_ref[i, pl.ds(first - 2 * stride, size)] - cells_ref[i, edge]
        lax.fori_loop(0, count, prepare, 0)

        begin_b = first - stride if stride % 8 == 0 else first - 8
        count_b, at_b = chunk_of(begin_b, last + stride, size)

        def states(k, carry, i=i, at_b=at_b):
            row = at_b(k)

            def take(ref, shift):
                return ref[pl.ds(row + shift * stride, size)]

            up, down = weno_pair(
                cells_ref[i, pl.ds(row, size)],
                take(step_ref, -2), take(step_ref, -1), take(step_ref, 0), take(step_ref, 1),
                take(curve_ref, -1), take(curve_ref, 0), take(curve_ref, 1),
            )
            left_ref[i, pl.ds(row, size)] = up
            right_ref[i, pl.ds(row, size)] = down
            return carry

        lax.fori_loop(0, count_b, states, 0)

    begin_c = first - stride if stride % 8 == 0 else first - 8
    count_c, at_c = chunk_of(begin_c, last, 16)

    def faces(k, carry):
        row = at_c(k)
        left = [left_ref[i, pl.ds(row, 16)] for i in range(7)]
        right = [right_ref[i, pl.ds(row + stride, 16)] for i in range(7)]
        flux, middle = hllc(left, right, normal)
        for i in range(7):
            flux_ref[i, pl.ds(row, 16)] = flux[i]
        flux_ref[7, pl.ds(row, 16)] = middle
        return carry

    lax.fori_loop(0, count_c, faces, 0)


def y_kernel(prim_ref, low_ref, high_ref, before_ref, change_ref, cells_ref, step_ref, curve_ref, left_ref, right_ref, flux_ref):
    depth, height = prim_ref.shape[1:3]
    pitch = height + 8
    first = 16

    def fill(z, carry):
        base = pl.multiple_of(first + z * pitch, 8)
        for i in range(7):
            cells_ref[i, pl.ds(base, height)] = prim_ref[i, z]
            for j in range(3):
                cells_ref[i, pl.ds(base - 3 + j, 1)] = low_ref[i, j, pl.ds(z, 1), :]
                cells_ref[i, pl.ds(base + height + j, 1)] = high_ref[i, j, pl.ds(z, 1), :]
        return carry

    lax.fori_loop(0, depth, fill, 0)
    row_sweep(cells_ref, step_ref, curve_ref, left_ref, right_ref, flux_ref, 1, first, first + depth * pitch, 1)

    def gather(z, carry):
        base = pl.multiple_of(first + z * pitch, 8)
        here, below = pl.ds(base, height), pl.ds(base - 1, height)
        for i in range(6):
            change_ref[i, z] = before_ref[i, z] + (flux_ref[i, below] - flux_ref[i, here])
        change_ref[6, z] = before_ref[6, z] + (
            (flux_ref[6, below] - flux_ref[6, here])
            + prim_ref[6, z] * (flux_ref[7, here] - flux_ref[7, below])
        )
        return carry

    lax.fori_loop(0, depth, gather, 0)


def z_kernel(prim_ref, low_ref, high_ref, before_ref, flow_ref, source_ref, next_ref, cells_ref, step_ref, curve_ref, left_ref, right_ref, flux_ref):
    depth, height = prim_ref.shape[1:3]
    first = 3 * height
    for i in range(7):
        for j in range(3):
            cells_ref[i, pl.ds(j * height, height)] = low_ref[i, j]
            cells_ref[i, pl.ds((depth + 3 + j) * height, height)] = high_ref[i, j]

    def fill(z, carry):
        base = pl.multiple_of(first + z * height, 8)
        for i in range(7):
            cells_ref[i, pl.ds(base, height)] = prim_ref[i, z]
        return carry

    lax.fori_loop(0, depth, fill, 0)
    row_sweep(cells_ref, step_ref, curve_ref, left_ref, right_ref, flux_ref, height, first, first + depth * height, 2)

    def update(z, carry):
        base = pl.multiple_of(first + z * height, 8)
        here, below = pl.ds(base, height), pl.ds(base - height, height)
        for i in range(7):
            change = before_ref[i, z] + (flux_ref[i, below] - flux_ref[i, here])
            if i == 6:
                change = change + prim_ref[6, z] * (flux_ref[7, here] - flux_ref[7, below])
                change = change - source_ref[z]
            next_ref[i, z] = flow_ref[i, z] + time_step * change
        return carry

    lax.fori_loop(0, depth, update, 0)


def serve_kernel(asked_ref, pressure_ref, served_ref):
    sources = asked_ref.shape[0]
    height = pressure_ref.shape[1]

    def one(src, carry):
        for r in range(HB):
            row = jnp.maximum(asked_ref[src, r], 0)
            level = row // height
            column = row % height
            slot = src * HB + r
            served_ref[slot, pl.ds(0, 2), :] = pressure_ref[level, pl.ds(column, 2), :]
            served_ref[slot, pl.ds(2, 2), :] = pressure_ref[level + 1, pl.ds(column, 2), :]
        return carry

    lax.fori_loop(0, sources, one, 0)


def scatter_kernel(asked_ref, returned_ref, source_ref, *sums):
    sources = asked_ref.shape[0]
    depth, height, length = source_ref.shape

    def clear(z, carry):
        for total in sums:
            total[pl.ds(pl.multiple_of(z * height, 8), height)] = jnp.zeros((height, length), F32)
        return carry

    lax.fori_loop(0, depth, clear, 0)

    def one(src, carry):
        for r in range(HB):
            total = sums[r % len(sums)]
            row = asked_ref[src, r]
            row = jnp.where(row < 0, depth * height, row)
            slot = src * HB + r
            near, far = pl.ds(row, 2), pl.ds(row + height, 2)
            total[near] = total[near] + returned_ref[slot, pl.ds(0, 2), :]
            total[far] = total[far] + returned_ref[slot, pl.ds(2, 2), :]
        return carry

    lax.fori_loop(0, sources, one, 0)

    def collect(z, carry):
        rows = pl.ds(pl.multiple_of(z * height, 8), height)
        value = sums[0][rows]
        for total in sums[1:]:
            value = value + total[rows]
        source_ref[z] = value
        return carry

    lax.fori_loop(0, depth, collect, 0)


def block_weights(place_ref, block, length):
    lateral = lax.broadcasted_iota(jnp.int32, (8, 128), 0) % 4
    shift_z = (lateral // 2).astype(F32) - place_ref[0, pl.ds(block, 1), :]
    shift_y = (lateral % 2).astype(F32) - place_ref[1, pl.ds(block, 1), :]
    across = jnp.exp(-0.5 * (shift_z * shift_z + shift_y * shift_y))
    across_sum = 0.5 * jnp.sum(across, axis=0, keepdims=True)
    offset = place_ref[2, pl.ds(block, 1), :] * float(length - 1)
    shift_x = lax.broadcasted_iota(jnp.int32, (length, 128), 0).astype(F32) - offset
    along = jnp.exp(-0.5 * (shift_x * shift_x))
    return across, across_sum, along


def deposit_kernel(slot_ref, place_ref, radius_ref, speed_ref, out_ref):
    length = out_ref.shape[2]
    upper = lax.broadcasted_iota(jnp.int32, (8, 128), 0) < 4

    def one(block):
        across, across_sum, along = block_weights(place_ref, block, length)
        along_sum = jnp.sum(along, axis=0, keepdims=True)
        radius = radius_ref[pl.ds(block, 1), :]
        rate = 4.0 * math.pi * radius * radius * speed_ref[pl.ds(block, 1), :]
        share = across * (rate * inverse(across_sum * along_sum))
        along_hi = along.astype(BF16)
        along_lo = (along - along_hi.astype(F32)).astype(BF16)
        share_hi = share.astype(BF16).astype(F32)
        both = jnp.where(upper, share_hi, share - share_hi).astype(BF16)
        only = jnp.where(upper, share_hi, 0.0).astype(BF16)
        result = dot_nt(both, along_hi) + dot_nt(only, along_lo)
        out_ref[slot_ref[0, block]] = result[0:4] + result[4:8]

    def several(k, carry):
        for j in range(4):
            one(k * 4 + j)
        return carry

    lax.fori_loop(0, radius_ref.shape[0] // 4, several, 0)


def sample_kernel(slot_ref, place_ref, radius_ref, speed_ref, rest_ref, rows_ref, motion_ref, sampled_ref):
    length = rows_ref.shape[2]
    upper = lax.broadcasted_iota(jnp.int32, (8, 128), 0) < 4

    def one(block):
        across, across_sum, along = block_weights(place_ref, block, length)
        value = rows_ref[slot_ref[0, block]] - pressure_mid
        value = jnp.concatenate([value, value], axis=0)
        high = value.astype(BF16).astype(F32)
        both = jnp.where(upper, high, value - high)
        both = jnp.concatenate([both, jnp.ones_like(both)], axis=0).astype(BF16)
        result = dot_nn(both, along.astype(BF16))
        total = jnp.sum(across * result[0:8], axis=0, keepdims=True)
        sampled_ref[pl.ds(block, 1), :] = pressure_mid + total * inverse(across_sum * result[8:9])

    def several(k, carry):
        for j in range(4):
            one(k * 4 + j)
        return carry

    lax.fori_loop(0, radius_ref.shape[0] // 4, several, 0)

    radius, speed, ratio = radius_ref[...], speed_ref[...], rest_ref[...]
    inv_radius = 1.0 / radius
    gas = (1.0 + 2.0 * surface_tension / (ratio * radius)) * jnp.exp(3.0 * polytropic * jnp.log(ratio))
    wall = gas - (2.0 * surface_tension + 4.0 * liquid_viscosity * speed) * inv_radius
    gas_rate = -3.0 * polytropic * gas * speed * inv_radius
    mach = speed / liquid_sound
    acceleration = (
        (1.0 + mach) * (wall - sampled_ref[...])
        + radius * gas_rate / liquid_sound
        - 1.5 * (1.0 - mach / 3.0) * speed * speed
    ) / ((1.0 - mach) * radius)
    motion_ref[0] = radius + time_step * speed
    motion_ref[1] = speed + time_step * acceleration


def shift_both(low_layers, high_layers, axis):
    count = lax.axis_size(axis)
    below = lax.ppermute(high_layers, axis, [(i, (i + 1) % count) for i in range(count)])
    above = lax.ppermute(low_layers, axis, [((i + 1) % count, i) for i in range(count)])
    return below, above


def exchange(values):
    return lax.all_to_all(values, ("gz", "gy"), split_axis=0, concat_axis=0, tiled=True)


def body(flow_state, block_tiles, bubble_place, bubble_radius, bubble_speed, rest_ratio):
    _, depth, height, length = flow_state.shape
    across_gy = lax.axis_size("gy")
    devices = lax.axis_size("gz") * across_gy
    blocks = block_tiles.shape[0]
    slots = devices * HB
    full_height = height * across_gy
    field = (7, depth, height, length)
    field_bytes = 4 * 7 * depth * height * length
    cells = depth * height * length

    anchor = block_tiles[:, 0].reshape(1, blocks)
    level, column = anchor // full_height, anchor % full_height
    home = level // depth * across_gy + column // height
    slot, wanted = pl.pallas_call(
        functools.partial(slot_kernel, height=height),
        out_shape=(shape((1, blocks), jnp.int32), shape((devices, HB), jnp.int32)),
        in_specs=[VMEM] * 3,
        out_specs=(VMEM, VMEM),
        cost_estimate=cost(1e6, 1e5),
        name="slots",
    )(home, level % depth, column % height)
    asked = exchange(wanted)

    prim, z_low, z_high, y_low, y_high = pl.pallas_call(
        primitive_kernel,
        out_shape=(
            shape(field),
            shape((7, 3, height, length)),
            shape((7, 3, height, length)),
            shape((7, 3, depth, length)),
            shape((7, 3, depth, length)),
        ),
        in_specs=[VMEM],
        out_specs=(VMEM,) * 5,
        compiler_params=params(),
        cost_estimate=cost(cells * 40, 2.5 * field_bytes),
        name="primitives",
    )(flow_state)
    z_below, z_above = shift_both(z_low, z_high, "gz")
    y_below, y_above = shift_both(y_low, y_high, "gy")

    outgoing = pl.pallas_call(
        deposit_kernel,
        out_shape=shape((slots, 4, length)),
        in_specs=[SMEM, VMEM, VMEM, VMEM],
        out_specs=VMEM,
        compiler_params=params(),
        cost_estimate=cost(2e9, 3e6),
        name="deposit",
    )(slot, bubble_place, bubble_radius, bubble_speed)
    returned = exchange(outgoing)

    served = pl.pallas_call(
        serve_kernel,
        out_shape=shape((slots, 4, length)),
        in_specs=[SMEM, VMEM],
        out_specs=VMEM,
        compiler_params=params(),
        cost_estimate=cost(1e6, 3e6),
        name="serve",
    )(asked, prim[5])
    fetched = exchange(served)

    change_x = pl.pallas_call(
        x_kernel,
        out_shape=shape(field),
        in_specs=[VMEM],
        out_specs=VMEM,
        scratch_shapes=[pltpu.VMEM((7, height, length), F32)] * 2,
        compiler_params=params(),
        cost_estimate=cost(cells * 600, 2 * field_bytes),
        name="sweep_x",
    )(prim)

    def scratch(rows):
        return [
            pltpu.VMEM((7, rows, length), F32),
            pltpu.VMEM((rows, length), F32),
            pltpu.VMEM((rows, length), F32),
            pltpu.VMEM((7, rows, length), F32),
            pltpu.VMEM((7, rows, length), F32),
            pltpu.VMEM((8, rows, length), F32),
        ]

    change_xy = pl.pallas_call(
        y_kernel,
        out_shape=shape(field),
        in_specs=[VMEM] * 4,
        out_specs=VMEM,
        scratch_shapes=scratch(16 + depth * (height + 8) + 56),
        compiler_params=params(),
        cost_estimate=cost(cells * 600, 3 * field_bytes),
        name="sweep_y",
    )(prim, y_below, y_above, change_x)

    source = pl.pallas_call(
        scatter_kernel,
        out_shape=shape((depth, height, length)),
        in_specs=[SMEM, VMEM],
        out_specs=VMEM,
        scratch_shapes=[pltpu.VMEM(((depth + 2) * height, length), F32)] * 4,
        compiler_params=params(),
        cost_estimate=cost(1e6, 3e6),
        name="scatter",
    )(asked, returned)

    state_next = pl.pallas_call(
        z_kernel,
        out_shape=shape(field),
        in_specs=[VMEM] * 6,
        out_specs=VMEM,
        scratch_shapes=scratch((depth + 6) * height),
        compiler_params=params(),
        cost_estimate=cost(cells * 600, 4 * field_bytes),
        name="sweep_z",
    )(prim, z_below, z_above, change_xy, flow_state, source)

    motion = pl.pallas_call(
        sample_kernel,
        out_shape=shape((2, blocks, 128)),
        in_specs=[SMEM] + [VMEM] * 5,
        out_specs=VMEM,
        scratch_shapes=[pltpu.VMEM((blocks, 128), F32)],
        compiler_params=params(),
        cost_estimate=cost(2e9, 4e6),
        name="sample",
    )(slot, bubble_place, bubble_radius, bubble_speed, rest_ratio, fetched)
    return state_next, source, motion


def solution(mesh):
    in_specs = (
        P(None, "gz", "gy", None),
        P(("gz", "gy"), None),
        P(None, ("gz", "gy"), None),
        P(("gz", "gy"), None),
        P(("gz", "gy"), None),
        P(("gz", "gy"), None),
    )
    out_specs = (P(None, "gz", "gy", None), P("gz", "gy", None), P(None, ("gz", "gy"), None))
    return jax.shard_map(body, mesh=mesh, in_specs=in_specs, out_specs=out_specs, check_vma=False)
```

```python
import functools
import math

import jax
import jax.numpy as jnp
from jax import lax
from jax.experimental import pallas as pl
from jax.experimental.pallas import tpu as pltpu
from jax.sharding import PartitionSpec as P

HB = 8
gamma_liquid = 4.4
stiff_liquid = 3.0
gamma_gas = 1.4
time_step = 0.08
liquid_sound = 20.0
surface_tension = 0.01
liquid_viscosity = 0.001
polytropic = 1.4
weno_eps = 1e-06
stiff_base = 1.0 / (gamma_gas - 1.0)
stiff_slope = 1.0 / (gamma_liquid - 1.0) - 1.0 / (gamma_gas - 1.0)
offset_slope = gamma_liquid * stiff_liquid / (gamma_liquid - 1.0)
pressure_mid = 0.9

VMEM = pl.BlockSpec(memory_space=pltpu.VMEM)
SMEM = pl.BlockSpec(memory_space=pltpu.SMEM)
F32 = jnp.float32
BF16 = jnp.bfloat16


def params(mib=56):
    return pltpu.CompilerParams(vmem_limit_bytes=mib * 2**20)


def shape(dims, dtype=F32):
    return jax.ShapeDtypeStruct(dims, dtype)


def cost(microseconds):
    return pl.CostEstimate(flops=int(microseconds * 1.15e9), bytes_accessed=1000, transcendentals=0)


def inverse(value):
    guess = pl.reciprocal(value, approx=True)
    return guess * (2.0 - value * guess)


def rough_inverse(value):
    return pl.reciprocal(value, approx=True)


def dot_nt(left, right):
    return lax.dot_general(left, right, (((1,), (1,)), ((), ())), preferred_element_type=F32)


def dot_nn(left, right):
    return lax.dot_general(left, right, (((1,), (0,)), ((), ())), preferred_element_type=F32)


def slot_kernel(tiles_ref, slot_ref, wanted_ref, *, depth, height, across_gy):
    devices = wanted_ref.shape[0]
    blocks = tiles_ref.shape[1]
    anchor = tiles_ref[0:1, :].astype(F32)

    def split(value, size):
        whole = jnp.floor((value + 0.5) * (1.0 / size))
        return whole, value - whole * float(size)

    level, column = split(anchor, height * across_gy)
    home_z, level = split(level, depth)
    home_y, column = split(column, height)
    home = (home_z * float(across_gy) + home_y).astype(jnp.int32)
    onehot = lax.broadcasted_iota(jnp.int32, (devices, blocks), 0) == home
    onehot = jnp.where(onehot, 1.0, 0.0).astype(F32)
    onehot_bf = onehot.astype(BF16)
    earlier = lax.broadcasted_iota(jnp.int32, (blocks, blocks), 0) < lax.broadcasted_iota(
        jnp.int32, (blocks, blocks), 1
    )
    earlier = jnp.where(earlier, 1.0, 0.0).astype(BF16)
    before = dot_nn(onehot_bf, earlier)
    rank = jnp.sum(onehot * before, axis=0, keepdims=True)
    rank = jnp.minimum(rank, HB - 1.0)
    slot_ref[...] = home * HB + rank.astype(jnp.int32)
    chosen = lax.broadcasted_iota(jnp.int32, (HB, blocks), 0).astype(F32) == rank
    level = jnp.where(chosen, level + 1.0, 0.0).astype(BF16)
    column = jnp.where(chosen, column, 0.0).astype(BF16)
    level = dot_nt(onehot_bf, level)
    column = dot_nt(onehot_bf, column)
    row = (level - 1.0) * float(height) + column
    wanted_ref[...] = jnp.where(level > 0.0, row, -1.0).astype(jnp.int32)


def primitive_kernel(flow_ref, prim_ref, z_low_ref, z_high_ref, y_low_ref, y_high_ref):
    depth, height = flow_ref.shape[1], flow_ref.shape[2]

    def slab(z, carry):
        first, second = flow_ref[0, z], flow_ref[1, z]
        density = first + second
        inv_density = inverse(density)
        mom = [flow_ref[2 + i, z] for i in range(3)]
        vel = [m * inv_density for m in mom]
        kinetic = 0.5 * (mom[0] * vel[0] + mom[1] * vel[1] + mom[2] * vel[2])
        fraction = flow_ref[6, z]
        stiffness = stiff_base + stiff_slope * fraction
        pressure = (flow_ref[5, z] - kinetic - offset_slope * fraction) * inverse(stiffness)
        for i, value in enumerate([first, second] + vel + [pressure, fraction]):
            prim_ref[i, z] = value
            for j in range(3):
                y_low_ref[i, j, pl.ds(z, 1), :] = value[j : j + 1]
                y_high_ref[i, j, pl.ds(z, 1), :] = value[height - 3 + j : height - 2 + j]
        return carry

    lax.fori_loop(0, depth, slab, 0)
    for i in range(7):
        for j in range(3):
            z_low_ref[i, j] = prim_ref[i, j]
            z_high_ref[i, j] = prim_ref[i, depth - 3 + j]


def weno_pair(cell, dm2, dm1, d0, dp1, zm, z0, zp):
    qm = dm1 + d0
    ql = 3.0 * dm1 - dm2
    qh = dp1 - 3.0 * d0
    tl = zm + ql * ql
    tm = z0 + qm * qm
    th = zp + qh * qh
    tl = tl * tl
    tm = tm * tm
    th = th * th
    low = tm * th
    mid = 6.0 * (tl * th)
    high = tl * tm
    low3 = 3.0 * low
    high3 = 3.0 * high
    den_up = 6.0 * (low + mid + high3)
    den_down = 6.0 * (low3 + mid + high)
    num_up = low * (2.0 * ql - dm1) + mid * (qm + d0) + high3 * (d0 - qh)
    num_down = low3 * (ql + dm1) + mid * (qm + dm1) - high * (2.0 * qh + d0)
    return cell + num_up * rough_inverse(den_up), cell - num_down * rough_inverse(den_down)


def curvature(step):
    return (13.0 / 3.0) * (step * step) + 4.0 * weno_eps


def sound_terms(state):
    density = state[0] + state[1]
    stiff_one = (stiff_base + 1.0) + stiff_slope * state[6]
    enthalpy = state[5] * stiff_one + offset_slope * state[6]
    sound = enthalpy * lax.rsqrt(enthalpy * ((stiff_one - 1.0) * density))
    return density, enthalpy, sound


def hllc(left, right, normal):
    density_l, enthalpy_l, sound_l = sound_terms(left)
    density_r, enthalpy_r, sound_r = sound_terms(right)
    speed_l, speed_r = left[2 + normal], right[2 + normal]
    wave_l = jnp.minimum(speed_l - sound_l, speed_r - sound_r)
    wave_r = jnp.maximum(speed_l + sound_l, speed_r + sound_r)
    mass_l = density_l * (wave_l - speed_l)
    mass_r = density_r * (wave_r - speed_r)
    middle = (right[5] - left[5] + mass_l * speed_l - mass_r * speed_r) * inverse(mass_l - mass_r)
    forward = middle >= 0.0
    use_left = (wave_l >= 0.0) | forward
    one = [jnp.where(use_left, a, b) for a, b in zip(left[:6], right[:6])]
    density = jnp.where(use_left, density_l, density_r)
    enthalpy = jnp.where(use_left, enthalpy_l, enthalpy_r)
    wave = jnp.where(use_left, jnp.minimum(wave_l, 0.0), jnp.maximum(wave_r, 0.0))
    speed, pressure = one[2 + normal], one[5]
    ratio = jnp.where(wave != 0.0, wave * inverse(wave - middle), 0.0)
    extra = ratio * (middle - speed)
    carried = speed + extra
    push = density * (extra * (wave - speed))
    mass = density * carried
    kinetic = 0.5 * density * (one[2] * one[2] + one[3] * one[3] + one[4] * one[4])
    flux = [one[0] * carried, one[1] * carried]
    for i in range(3):
        flow = mass * one[2 + i]
        flux.append(flow + (push + pressure) if i == normal else flow)
    flux.append((enthalpy + kinetic) * carried + push * middle)
    flux.append(middle * jnp.where(forward, left[6], right[6]))
    return flux, middle


def x_kernel(prim_ref, change_ref, left_ref, right_ref):
    depth, height, length = prim_ref.shape[1:]

    def slab(z, carry):
        for i in range(7):
            cell = prim_ref[i, z]
            d0 = pltpu.roll(cell, length - 1, 1) - cell
            dm1 = pltpu.roll(d0, 1, 1)
            dm2 = pltpu.roll(d0, 2, 1)
            dp1 = pltpu.roll(d0, length - 1, 1)
            z0 = curvature(d0 - dm1)
            zm = pltpu.roll(z0, 1, 1)
            zp = pltpu.roll(z0, length - 1, 1)
            up, down = weno_pair(cell, dm2, dm1, d0, dp1, zm, z0, zp)
            left_ref[i] = up
            right_ref[i] = pltpu.roll(down, length - 1, 1)
        for part in range(height // 16):
            rows = pl.ds(16 * part, 16)
            left = [left_ref[i, rows] for i in range(7)]
            right = [right_ref[i, rows] for i in range(7)]
            flux, middle = hllc(left, right, 0)
            for i in range(6):
                change_ref[i, z, rows] = pltpu.roll(flux[i], 1, 1) - flux[i]
            fraction = prim_ref[6, z, rows]
            change_ref[6, z, rows] = (pltpu.roll(flux[6], 1, 1) - flux[6]) + fraction * (
                middle - pltpu.roll(middle, 1, 1)
            )
        return carry

    lax.fori_loop(0, depth, slab, 0)


def row_sweep(cells_ref, step_ref, curve_ref, left_ref, right_ref, flux_ref, stride, first, last, normal):
    def chunk_of(begin, end, size):
        count = -(-(end - begin) // size)
        return count, lambda k: pl.multiple_of(begin + k * size, 8)

    size = 32
    begin = first - 2 * stride if stride % 8 == 0 else first - 8
    count, at = chunk_of(begin, last + 2 * stride, size)

    for i in range(7):

        def prepare(k, carry, i=i):
            row = at(k)
            mid = cells_ref[i, pl.ds(row, size)]
            d0 = cells_ref[i, pl.ds(row + stride, size)] - mid
            dm1 = mid - cells_ref[i, pl.ds(row - stride, size)]
            step_ref[pl.ds(row, size)] = d0
            curve_ref[pl.ds(row, size)] = curvature(d0 - dm1)
            return carry

        if stride % 8 == 0:
            edge = pl.ds(first - 3 * stride, size)
            step_ref[edge] = cells_ref[i, pl.ds(first - 2 * stride, size)] - cells_ref[i, edge]
        lax.fori_loop(0, count, prepare, 0)

        begin_b = first - stride if stride % 8 == 0 else first - 8
        count_b, at_b = chunk_of(begin_b, last + stride, size)

        def states(k, carry, i=i, at_b=at_b):
            row = at_b(k)

            def take(ref, shift):
                return ref[pl.ds(row + shift * stride, size)]

            up, down = weno_pair(
                cells_ref[i, pl.ds(row, size)],
                take(step_ref, -2), take(step_ref, -1), take(step_ref, 0), take(step_ref, 1),
                take(curve_ref, -1), take(curve_ref, 0), take(curve_ref, 1),
            )
            left_ref[i, pl.ds(row, size)] = up
            right_ref[i, pl.ds(row, size)] = down
            return carry

        lax.fori_loop(0, count_b, states, 0)

    begin_c = first - stride if stride % 8 == 0 else first - 8
    count_c, at_c = chunk_of(begin_c, last, 16)

    def faces(k, carry):
        row = at_c(k)
        left = [left_ref[i, pl.ds(row, 16)] for i in range(7)]
        right = [right_ref[i, pl.ds(row + stride, 16)] for i in range(7)]
        flux, middle = hllc(left, right, normal)
        for i in range(7):
            flux_ref[i, pl.ds(row, 16)] = flux[i]
        flux_ref[7, pl.ds(row, 16)] = middle
        return carry

    lax.fori_loop(0, count_c, faces, 0)


def y_kernel(prim_ref, low_ref, high_ref, before_ref, change_ref, cells_ref, step_ref, curve_ref, left_ref, right_ref, flux_ref):
    depth, height = prim_ref.shape[1:3]
    pitch = height + 8
    first = 16

    def fill(z, carry):
        base = pl.multiple_of(first + z * pitch, 8)
        for i in range(7):
            cells_ref[i, pl.ds(base, height)] = prim_ref[i, z]
            for j in range(3):
                cells_ref[i, pl.ds(base - 3 + j, 1)] = low_ref[i, j, pl.ds(z, 1), :]
                cells_ref[i, pl.ds(base + height + j, 1)] = high_ref[i, j, pl.ds(z, 1), :]
        return carry

    lax.fori_loop(0, depth, fill, 0)
    row_sweep(cells_ref, step_ref, curve_ref, left_ref, right_ref, flux_ref, 1, first, first + depth * pitch, 1)

    def gather(z, carry):
        base = pl.multiple_of(first + z * pitch, 8)
        here, below = pl.ds(base, height), pl.ds(base - 1, height)
        for i in range(6):
            change_ref[i, z] = before_ref[i, z] + (flux_ref[i, below] - flux_ref[i, here])
        change_ref[6, z] = before_ref[6, z] + (
            (flux_ref[6, below] - flux_ref[6, here])
            + prim_ref[6, z] * (flux_ref[7, here] - flux_ref[7, below])
        )
        return carry

    lax.fori_loop(0, depth, gather, 0)


def z_kernel(prim_ref, low_ref, high_ref, before_ref, flow_ref, next_ref, cells_ref, step_ref, curve_ref, left_ref, right_ref, flux_ref):
    depth, height = prim_ref.shape[1:3]
    first = 3 * height
    for i in range(7):
        for j in range(3):
            cells_ref[i, pl.ds(j * height, height)] = low_ref[i, j]
            cells_ref[i, pl.ds((depth + 3 + j) * height, height)] = high_ref[i, j]

    def fill(z, carry):
        base = pl.multiple_of(first + z * height, 8)
        for i in range(7):
            cells_ref[i, pl.ds(base, height)] = prim_ref[i, z]
        return carry

    lax.fori_loop(0, depth, fill, 0)
    row_sweep(cells_ref, step_ref, curve_ref, left_ref, right_ref, flux_ref, height, first, first + depth * height, 2)

    def update(z, carry):
        base = pl.multiple_of(first + z * height, 8)
        here, below = pl.ds(base, height), pl.ds(base - height, height)
        for i in range(7):
            change = before_ref[i, z] + (flux_ref[i, below] - flux_ref[i, here])
            if i == 6:
                change = change + prim_ref[6, z] * (flux_ref[7, here] - flux_ref[7, below])
            next_ref[i, z] = flow_ref[i, z] + time_step * change
        return carry

    lax.fori_loop(0, depth, update, 0)


def serve_kernel(asked_ref, pressure_ref, served_ref, *, height):
    def one(src, carry):
        for r in range(HB):
            row = jnp.maximum(asked_ref[src, r], 0)
            slot = src * HB + r
            served_ref[slot, pl.ds(0, 2), :] = pressure_ref[0, pl.ds(row, 2), :]
            served_ref[slot, pl.ds(2, 2), :] = pressure_ref[0, pl.ds(row + height, 2), :]
        return carry

    lax.fori_loop(0, asked_ref.shape[0], one, 0)


def scatter_kernel(asked_ref, returned_ref, state_ref, source_ref, next_ref, fraction_ref, sem, *sums):
    sources = asked_ref.shape[0]
    depth, height, length = source_ref.shape
    load = pltpu.make_async_copy(state_ref.at[6], fraction_ref, sem)
    load.start()

    def clear(z, carry):
        for total in sums:
            total[pl.ds(pl.multiple_of(z * height, 8), height)] = jnp.zeros((height, length), F32)
        return carry

    lax.fori_loop(0, depth, clear, 0)

    def one(src, carry):
        for r in range(HB):
            total = sums[r % len(sums)]
            row = asked_ref[src, r]
            row = jnp.where(row < 0, depth * height, row)
            slot = src * HB + r
            near, far = pl.ds(row, 2), pl.ds(row + height, 2)
            total[near] = total[near] + returned_ref[slot, pl.ds(0, 2), :]
            total[far] = total[far] + returned_ref[slot, pl.ds(2, 2), :]
        return carry

    lax.fori_loop(0, sources, one, 0)

    def collect(z, carry):
        rows = pl.ds(pl.multiple_of(z * height, 8), height)
        value = sums[0][rows]
        for total in sums[1:]:
            value = value + total[rows]
        source_ref[z] = value
        fraction_ref[z] = fraction_ref[z] - time_step * value
        return carry

    load.wait()
    lax.fori_loop(0, depth, collect, 0)
    save = pltpu.make_async_copy(fraction_ref, next_ref.at[6], sem)
    save.start()
    save.wait()


def block_weights(place_ref, block, length):
    lateral = lax.broadcasted_iota(jnp.int32, (8, 128), 0) % 4
    shift_z = (lateral // 2).astype(F32) - place_ref[0, pl.ds(block, 1), :]
    shift_y = (lateral % 2).astype(F32) - place_ref[1, pl.ds(block, 1), :]
    across = jnp.exp(-0.5 * (shift_z * shift_z + shift_y * shift_y))
    across_sum = 0.5 * jnp.sum(across, axis=0, keepdims=True)
    offset = place_ref[2, pl.ds(block, 1), :] * float(length - 1)
    shift_x = lax.broadcasted_iota(jnp.int32, (length, 128), 0).astype(F32) - offset
    along = jnp.exp(-0.5 * (shift_x * shift_x))
    return across, across_sum, along


def deposit_kernel(slot_ref, place_ref, radius_ref, speed_ref, out_ref):
    length = out_ref.shape[2]
    upper = lax.broadcasted_iota(jnp.int32, (8, 128), 0) < 4

    def one(block):
        across, across_sum, along = block_weights(place_ref, block, length)
        along_sum = jnp.sum(along, axis=0, keepdims=True)
        radius = radius_ref[pl.ds(block, 1), :]
        rate = 4.0 * math.pi * radius * radius * speed_ref[pl.ds(block, 1), :]
        share = across * (rate * inverse(across_sum * along_sum))
        along_hi = along.astype(BF16)
        along_lo = (along - along_hi.astype(F32)).astype(BF16)
        share_hi = share.astype(BF16).astype(F32)
        both = jnp.where(upper, share_hi, share - share_hi).astype(BF16)
        only = jnp.where(upper, share_hi, 0.0).astype(BF16)
        result = dot_nt(both, along_hi) + dot_nt(only, along_lo)
        out_ref[slot_ref[0, block]] = result[0:4] + result[4:8]

    def several(k, carry):
        for j in range(4):
            one(k * 4 + j)
        return carry

    lax.fori_loop(0, radius_ref.shape[0] // 4, several, 0)


def sample_kernel(slot_ref, place_ref, radius_ref, speed_ref, rest_ref, rows_ref, motion_ref, sampled_ref):
    length = rows_ref.shape[2]
    upper = lax.broadcasted_iota(jnp.int32, (8, 128), 0) < 4

    def one(block):
        across, across_sum, along = block_weights(place_ref, block, length)
        value = rows_ref[slot_ref[0, block]] - pressure_mid
        value = jnp.concatenate([value, value], axis=0)
        high = value.astype(BF16).astype(F32)
        both = jnp.where(upper, high, value - high)
        both = jnp.concatenate([both, jnp.ones_like(both)], axis=0).astype(BF16)
        result = dot_nn(both, along.astype(BF16))
        total = jnp.sum(across * result[0:8], axis=0, keepdims=True)
        sampled_ref[pl.ds(block, 1), :] = pressure_mid + total * inverse(across_sum * result[8:9])

    def several(k, carry):
        for j in range(4):
            one(k * 4 + j)
        return carry

    lax.fori_loop(0, radius_ref.shape[0] // 4, several, 0)

    radius, speed, ratio = radius_ref[...], speed_ref[...], rest_ref[...]
    inv_radius = 1.0 / radius
    gas = (1.0 + 2.0 * surface_tension / (ratio * radius)) * jnp.exp(3.0 * polytropic * jnp.log(ratio))
    wall = gas - (2.0 * surface_tension + 4.0 * liquid_viscosity * speed) * inv_radius
    gas_rate = -3.0 * polytropic * gas * speed * inv_radius
    mach = speed / liquid_sound
    acceleration = (
        (1.0 + mach) * (wall - sampled_ref[...])
        + radius * gas_rate / liquid_sound
        - 1.5 * (1.0 - mach / 3.0) * speed * speed
    ) / ((1.0 - mach) * radius)
    motion_ref[0] = radius + time_step * speed
    motion_ref[1] = speed + time_step * acceleration


def shift_both(low_layers, high_layers, axis):
    count = lax.axis_size(axis)
    below = lax.ppermute(high_layers, axis, [(i, (i + 1) % count) for i in range(count)])
    above = lax.ppermute(low_layers, axis, [((i + 1) % count, i) for i in range(count)])
    return below, above


def exchange(values):
    return lax.all_to_all(values, ("gz", "gy"), split_axis=0, concat_axis=0, tiled=True)


def body(flow_state, block_tiles, bubble_place, bubble_radius, bubble_speed, rest_ratio):
    _, depth, height, length = flow_state.shape
    across_gy = lax.axis_size("gy")
    devices = lax.axis_size("gz") * across_gy
    blocks = block_tiles.shape[0]
    slots = devices * HB
    field = (7, depth, height, length)

    slot, wanted = pl.pallas_call(
        functools.partial(slot_kernel, depth=depth, height=height, across_gy=across_gy),
        out_shape=(shape((1, blocks), jnp.int32), shape((devices, HB), jnp.int32)),
        in_specs=[VMEM],
        out_specs=(VMEM, VMEM),
        cost_estimate=cost(2),
        name="slots",
    )(block_tiles.T)
    asked = exchange(wanted)

    prim, z_low, z_high, y_low, y_high = pl.pallas_call(
        primitive_kernel,
        out_shape=(
            shape(field),
            shape((7, 3, height, length)),
            shape((7, 3, height, length)),
            shape((7, 3, depth, length)),
            shape((7, 3, depth, length)),
        ),
        in_specs=[VMEM],
        out_specs=(VMEM,) * 5,
        compiler_params=params(),
        cost_estimate=cost(4),
        name="primitives",
    )(flow_state)
    y_below, y_above = shift_both(y_low, y_high, "gy")
    z_below, z_above = shift_both(z_low, z_high, "gz")
    slot, prim = lax.optimization_barrier((slot, prim))

    outgoing = pl.pallas_call(
        deposit_kernel,
        out_shape=shape((slots, 4, length)),
        in_specs=[SMEM, VMEM, VMEM, VMEM],
        out_specs=VMEM,
        compiler_params=params(),
        cost_estimate=cost(21),
        name="deposit",
    )(slot, bubble_place, bubble_radius, bubble_speed)

    rows = depth * height
    asked, outgoing, y_below, y_above, z_below, z_above = lax.optimization_barrier(
        (asked, outgoing, y_below, y_above, z_below, z_above)
    )
    served = pl.pallas_call(
        functools.partial(serve_kernel, height=height),
        grid=(1,),
        out_shape=shape((slots, 4, length)),
        in_specs=[SMEM, pl.BlockSpec((1, rows, length), lambda i: (5, 0, 0))],
        out_specs=VMEM,
        compiler_params=params(),
        cost_estimate=cost(5),
        name="serve",
    )(asked, prim.reshape(7, rows, length))
    fetched = exchange(served)

    change_x = pl.pallas_call(
        x_kernel,
        out_shape=shape(field),
        in_specs=[VMEM],
        out_specs=VMEM,
        scratch_shapes=[pltpu.VMEM((7, height, length), F32)] * 2,
        compiler_params=params(),
        cost_estimate=cost(16),
        name="sweep_x",
    )(prim)

    def scratch(rows):
        return [
            pltpu.VMEM((7, rows, length), F32),
            pltpu.VMEM((rows, length), F32),
            pltpu.VMEM((rows, length), F32),
            pltpu.VMEM((7, rows, length), F32),
            pltpu.VMEM((7, rows, length), F32),
            pltpu.VMEM((8, rows, length), F32),
        ]

    change_xy = pl.pallas_call(
        y_kernel,
        out_shape=shape(field),
        in_specs=[VMEM] * 4,
        out_specs=VMEM,
        scratch_shapes=scratch(16 + depth * (height + 8) + 56),
        compiler_params=params(),
        cost_estimate=cost(19),
        name="sweep_y",
    )(prim, y_below, y_above, change_x)

    outgoing, fetched, change_xy = lax.optimization_barrier((outgoing, fetched, change_xy))
    returned = exchange(outgoing)

    state_next = pl.pallas_call(
        z_kernel,
        out_shape=shape(field),
        in_specs=[VMEM] * 5,
        out_specs=VMEM,
        scratch_shapes=scratch((depth + 6) * height),
        compiler_params=params(),
        cost_estimate=cost(17),
        name="sweep_z",
    )(prim, z_below, z_above, change_xy, flow_state)

    motion = pl.pallas_call(
        sample_kernel,
        out_shape=shape((2, blocks, 128)),
        in_specs=[SMEM] + [VMEM] * 5,
        out_specs=VMEM,
        scratch_shapes=[pltpu.VMEM((blocks, 128), F32)],
        compiler_params=params(),
        cost_estimate=cost(15),
        name="sample",
    )(slot, bubble_place, bubble_radius, bubble_speed, rest_ratio, fetched)

    returned, state_next, motion = lax.optimization_barrier((returned, state_next, motion))
    source, state_next = pl.pallas_call(
        scatter_kernel,
        out_shape=(shape((depth, height, length)), shape(field)),
        in_specs=[SMEM, VMEM, pl.BlockSpec(memory_space=pl.ANY)],
        out_specs=(VMEM, pl.BlockSpec(memory_space=pl.ANY)),
        scratch_shapes=[pltpu.VMEM((depth, height, length), F32), pltpu.SemaphoreType.DMA]
        + [pltpu.VMEM(((depth + 2) * height, length), F32)] * 4,
        input_output_aliases={2: 1},
        compiler_params=params(),
        cost_estimate=cost(6),
        name="scatter",
    )(asked, returned, state_next)
    return state_next, source, motion


def solution(mesh):
    in_specs = (
        P(None, "gz", "gy", None),
        P(("gz", "gy"), None),
        P(None, ("gz", "gy"), None),
        P(("gz", "gy"), None),
        P(("gz", "gy"), None),
        P(("gz", "gy"), None),
    )
    out_specs = (P(None, "gz", "gy", None), P("gz", "gy", None), P(None, ("gz", "gy"), None))
    return jax.shard_map(body, mesh=mesh, in_specs=in_specs, out_specs=out_specs, check_vma=False)
```

```python
import functools
import math

import jax
import jax.numpy as jnp
from jax import lax
from jax.experimental import pallas as pl
from jax.experimental.pallas import tpu as pltpu
from jax.sharding import PartitionSpec as P

HB = 8
PAIRS = 2 * HB + 1
gamma_liquid = 4.4
stiff_liquid = 3.0
gamma_gas = 1.4
time_step = 0.08
liquid_sound = 20.0
surface_tension = 0.01
liquid_viscosity = 0.001
polytropic = 1.4
weno_eps = 1e-06
stiff_base = 1.0 / (gamma_gas - 1.0)
stiff_slope = 1.0 / (gamma_liquid - 1.0) - 1.0 / (gamma_gas - 1.0)
offset_slope = gamma_liquid * stiff_liquid / (gamma_liquid - 1.0)
pressure_mid = 0.9

VMEM = pl.BlockSpec(memory_space=pltpu.VMEM)
SMEM = pl.BlockSpec(memory_space=pltpu.SMEM)
F32 = jnp.float32
BF16 = jnp.bfloat16


def params(mib=56):
    return pltpu.CompilerParams(vmem_limit_bytes=mib * 2**20)


def shape(dims, dtype=F32):
    return jax.ShapeDtypeStruct(dims, dtype)


def cost(microseconds):
    return pl.CostEstimate(flops=int(microseconds * 1.15e9), bytes_accessed=1000, transcendentals=0)


def inverse(value):
    return pl.reciprocal(value, approx=True)


def dot_nt(left, right):
    return lax.dot_general(left, right, (((1,), (1,)), ((), ())), preferred_element_type=F32)


def dot_nn(left, right):
    return lax.dot_general(left, right, (((1,), (0,)), ((), ())), preferred_element_type=F32)


def slot_kernel(tiles_ref, slot_ref, wanted_ref, *, depth, height, across_gy):
    devices = wanted_ref.shape[0]
    blocks = tiles_ref.shape[1]
    anchor = tiles_ref[0:1, :].astype(F32)

    def split(value, size):
        whole = jnp.floor((value + 0.5) * (1.0 / size))
        return whole, value - whole * float(size)

    level, column = split(anchor, height * across_gy)
    home_z, level = split(level, depth)
    home_y, column = split(column, height)
    home = (home_z * float(across_gy) + home_y).astype(jnp.int32)
    onehot = lax.broadcasted_iota(jnp.int32, (devices, blocks), 0) == home
    onehot = jnp.where(onehot, 1.0, 0.0).astype(F32)
    onehot_bf = onehot.astype(BF16)
    earlier = lax.broadcasted_iota(jnp.int32, (blocks, blocks), 0) < lax.broadcasted_iota(
        jnp.int32, (blocks, blocks), 1
    )
    earlier = jnp.where(earlier, 1.0, 0.0).astype(BF16)
    before = dot_nn(onehot_bf, earlier)
    rank = jnp.sum(onehot * before, axis=0, keepdims=True)
    rank = jnp.minimum(rank, HB - 1.0)
    rank_int = rank.astype(jnp.int32)
    slot_ref[...] = jnp.concatenate([home * HB + rank_int, home * PAIRS + 2 * rank_int], axis=0)
    chosen = lax.broadcasted_iota(jnp.int32, (wanted_ref.shape[1], blocks), 0).astype(F32) == rank
    level = jnp.where(chosen, level + 1.0, 0.0).astype(BF16)
    column = jnp.where(chosen, column, 0.0).astype(BF16)
    level = dot_nt(onehot_bf, level)
    column = dot_nt(onehot_bf, column)
    row = (level - 1.0) * float(height) + column
    wanted_ref[...] = jnp.where(level > 0.0, row, -1.0)


def primitive_kernel(flow_ref, prim_ref, z_low_ref, z_high_ref, y_low_ref, y_high_ref):
    depth, height = flow_ref.shape[1], flow_ref.shape[2]

    def slab(z, carry):
        first, second = flow_ref[0, z], flow_ref[1, z]
        density = first + second
        inv_density = inverse(density)
        mom = [flow_ref[2 + i, z] for i in range(3)]
        vel = [m * inv_density for m in mom]
        kinetic = 0.5 * (mom[0] * vel[0] + mom[1] * vel[1] + mom[2] * vel[2])
        fraction = flow_ref[6, z]
        stiffness = stiff_base + stiff_slope * fraction
        pressure = (flow_ref[5, z] - kinetic - offset_slope * fraction) * inverse(stiffness)
        for i, value in enumerate([first, second] + vel + [pressure, fraction]):
            prim_ref[i, z] = value
            for j in range(3):
                y_low_ref[i, j, pl.ds(z, 1), :] = value[j : j + 1]
                y_high_ref[i, j, pl.ds(z, 1), :] = value[height - 3 + j : height - 2 + j]
        return carry

    lax.fori_loop(0, depth, slab, 0)
    for i in range(7):
        for j in range(3):
            z_low_ref[i, j] = prim_ref[i, j]
            z_high_ref[i, j] = prim_ref[i, depth - 3 + j]


def weno_pair(cell, dm2, dm1, d0, dp1, zm, z0, zp):
    qm = dm1 + d0
    ql = 3.0 * dm1 - dm2
    qh = dp1 - 3.0 * d0
    tl = zm + ql * ql
    tm = z0 + qm * qm
    th = zp + qh * qh
    tl = tl * tl
    tm = tm * tm
    th = th * th
    low = tm * th
    mid = 6.0 * (tl * th)
    high = tl * tm
    low3 = 3.0 * low
    high3 = 3.0 * high
    den_up = 6.0 * (low + mid + high3)
    den_down = 6.0 * (low3 + mid + high)
    num_up = low * (2.0 * ql - dm1) + mid * (qm + d0) + high3 * (d0 - qh)
    num_down = low3 * (ql + dm1) + mid * (qm + dm1) - high * (2.0 * qh + d0)
    return cell + num_up * inverse(den_up), cell - num_down * inverse(den_down)


def curvature(step):
    return (13.0 / 3.0) * (step * step) + 4.0 * weno_eps


def sound_terms(state):
    density = state[0] + state[1]
    stiff_one = (stiff_base + 1.0) + stiff_slope * state[6]
    enthalpy = state[5] * stiff_one + offset_slope * state[6]
    sound = enthalpy * lax.rsqrt(enthalpy * ((stiff_one - 1.0) * density))
    return density, enthalpy, sound


def hllc(left, right, normal):
    density_l, enthalpy_l, sound_l = sound_terms(left)
    density_r, enthalpy_r, sound_r = sound_terms(right)
    speed_l, speed_r = left[2 + normal], right[2 + normal]
    wave_l = jnp.minimum(speed_l - sound_l, speed_r - sound_r)
    wave_r = jnp.maximum(speed_l + sound_l, speed_r + sound_r)
    mass_l = density_l * (wave_l - speed_l)
    mass_r = density_r * (wave_r - speed_r)
    middle = (right[5] - left[5] + mass_l * speed_l - mass_r * speed_r) * inverse(mass_l - mass_r)
    forward = middle >= 0.0
    use_left = (wave_l >= 0.0) | forward
    one = [jnp.where(use_left, a, b) for a, b in zip(left[:6], right[:6])]
    density = jnp.where(use_left, density_l, density_r)
    enthalpy = jnp.where(use_left, enthalpy_l, enthalpy_r)
    wave = jnp.where(use_left, jnp.minimum(wave_l, 0.0), jnp.maximum(wave_r, 0.0))
    speed, pressure = one[2 + normal], one[5]
    ratio = jnp.where(wave != 0.0, wave * inverse(wave - middle), 0.0)
    extra = ratio * (middle - speed)
    carried = speed + extra
    push = density * (extra * (wave - speed))
    mass = density * carried
    kinetic = 0.5 * density * (one[2] * one[2] + one[3] * one[3] + one[4] * one[4])
    flux = [one[0] * carried, one[1] * carried]
    for i in range(3):
        flow = mass * one[2 + i]
        flux.append(flow + (push + pressure) if i == normal else flow)
    flux.append((enthalpy + kinetic) * carried + push * middle)
    flux.append(middle * jnp.where(forward, left[6], right[6]))
    return flux, middle


def x_kernel(prim_ref, change_ref, left_ref, right_ref):
    depth, height, length = prim_ref.shape[1:]

    def slab(z, carry):
        for i in range(7):
            cell = prim_ref[i, z]
            d0 = pltpu.roll(cell, length - 1, 1) - cell
            dm1 = pltpu.roll(d0, 1, 1)
            dm2 = pltpu.roll(d0, 2, 1)
            dp1 = pltpu.roll(d0, length - 1, 1)
            z0 = curvature(d0 - dm1)
            zm = pltpu.roll(z0, 1, 1)
            zp = pltpu.roll(z0, length - 1, 1)
            up, down = weno_pair(cell, dm2, dm1, d0, dp1, zm, z0, zp)
            left_ref[i] = up
            right_ref[i] = pltpu.roll(down, length - 1, 1)
        for part in range(height // 16):
            rows = pl.ds(16 * part, 16)
            left = [left_ref[i, rows] for i in range(7)]
            right = [right_ref[i, rows] for i in range(7)]
            flux, middle = hllc(left, right, 0)
            for i in range(6):
                change_ref[i, z, rows] = pltpu.roll(flux[i], 1, 1) - flux[i]
            fraction = prim_ref[6, z, rows]
            change_ref[6, z, rows] = (pltpu.roll(flux[6], 1, 1) - flux[6]) + fraction * (
                middle - pltpu.roll(middle, 1, 1)
            )
        return carry

    lax.fori_loop(0, depth, slab, 0)


def row_sweep(cells_ref, step_ref, curve_ref, left_ref, right_ref, flux_ref, stride, first, last, normal):
    def chunk_of(begin, end, size):
        count = -(-(end - begin) // size)
        return count, lambda k: pl.multiple_of(begin + k * size, 8)

    size = 64
    begin = first - 2 * stride if stride % 8 == 0 else first - 8
    count, at = chunk_of(begin, last + 2 * stride, size)

    for i in range(7):

        def prepare(k, carry, i=i):
            row = at(k)
            mid = cells_ref[i, pl.ds(row, size)]
            d0 = cells_ref[i, pl.ds(row + stride, size)] - mid
            dm1 = mid - cells_ref[i, pl.ds(row - stride, size)]
            step_ref[pl.ds(row, size)] = d0
            curve_ref[pl.ds(row, size)] = curvature(d0 - dm1)
            return carry

        if stride % 8 == 0:
            edge = pl.ds(first - 3 * stride, size)
            step_ref[edge] = cells_ref[i, pl.ds(first - 2 * stride, size)] - cells_ref[i, edge]
        lax.fori_loop(0, count, prepare, 0)

        begin_b = first - stride if stride % 8 == 0 else first - 8
        count_b, at_b = chunk_of(begin_b, last + stride, size)

        def states(k, carry, i=i, at_b=at_b):
            row = at_b(k)

            def take(ref, shift):
                return ref[pl.ds(row + shift * stride, size)]

            up, down = weno_pair(
                cells_ref[i, pl.ds(row, size)],
                take(step_ref, -2), take(step_ref, -1), take(step_ref, 0), take(step_ref, 1),
                take(curve_ref, -1), take(curve_ref, 0), take(curve_ref, 1),
            )
            left_ref[i, pl.ds(row, size)] = up
            right_ref[i, pl.ds(row, size)] = down
            return carry

        lax.fori_loop(0, count_b, states, 0)

    begin_c = first - stride if stride % 8 == 0 else first - 8
    count_c, at_c = chunk_of(begin_c, last, 32)

    def faces(k, carry):
        row = at_c(k)
        left = [left_ref[i, pl.ds(row, 32)] for i in range(7)]
        right = [right_ref[i, pl.ds(row + stride, 32)] for i in range(7)]
        flux, middle = hllc(left, right, normal)
        for i in range(7):
            flux_ref[i, pl.ds(row, 32)] = flux[i]
        flux_ref[7, pl.ds(row, 32)] = middle
        return carry

    lax.fori_loop(0, count_c, faces, 0)


def y_kernel(prim_ref, low_ref, high_ref, before_ref, change_ref, cells_ref, step_ref, curve_ref, left_ref, right_ref, flux_ref):
    depth, height = prim_ref.shape[1:3]
    pitch = height + 8
    first = 16

    def fill(z, carry):
        base = pl.multiple_of(first + z * pitch, 8)
        for i in range(7):
            cells_ref[i, pl.ds(base, height)] = prim_ref[i, z]
            for j in range(3):
                cells_ref[i, pl.ds(base - 3 + j, 1)] = low_ref[i, j, pl.ds(z, 1), :]
                cells_ref[i, pl.ds(base + height + j, 1)] = high_ref[i, j, pl.ds(z, 1), :]
        return carry

    lax.fori_loop(0, depth, fill, 0)
    row_sweep(cells_ref, step_ref, curve_ref, left_ref, right_ref, flux_ref, 1, first, first + depth * pitch, 1)

    def gather(z, carry):
        base = pl.multiple_of(first + z * pitch, 8)
        here, below = pl.ds(base, height), pl.ds(base - 1, height)
        for i in range(6):
            change_ref[i, z] = before_ref[i, z] + (flux_ref[i, below] - flux_ref[i, here])
        change_ref[6, z] = before_ref[6, z] + (
            (flux_ref[6, below] - flux_ref[6, here])
            + prim_ref[6, z] * (flux_ref[7, here] - flux_ref[7, below])
        )
        return carry

    lax.fori_loop(0, depth, gather, 0)


def z_kernel(prim_ref, low_ref, high_ref, before_ref, flow_ref, source_ref, next_ref, cells_ref, step_ref, curve_ref, left_ref, right_ref, flux_ref):
    depth, height = prim_ref.shape[1:3]
    first = 3 * height
    for i in range(7):
        for j in range(3):
            cells_ref[i, pl.ds(j * height, height)] = low_ref[i, j]
            cells_ref[i, pl.ds((depth + 3 + j) * height, height)] = high_ref[i, j]

    def fill(z, carry):
        base = pl.multiple_of(first + z * height, 8)
        for i in range(7):
            cells_ref[i, pl.ds(base, height)] = prim_ref[i, z]
        return carry

    lax.fori_loop(0, depth, fill, 0)
    row_sweep(cells_ref, step_ref, curve_ref, left_ref, right_ref, flux_ref, height, first, first + depth * height, 2)

    def update(z, carry):
        base = pl.multiple_of(first + z * height, 8)
        here, below = pl.ds(base, height), pl.ds(base - height, height)
        for i in range(7):
            change = before_ref[i, z] + (flux_ref[i, below] - flux_ref[i, here])
            if i == 6:
                change = change + prim_ref[6, z] * (flux_ref[7, here] - flux_ref[7, below])
                change = change - source_ref[z]
            next_ref[i, z] = flow_ref[i, z] + time_step * change
        return carry

    lax.fori_loop(0, depth, update, 0)


def serve_kernel(asked_ref, pressure_ref, served_ref, *, height):
    def one(src, carry):
        for r in range(HB):
            row = jnp.maximum(asked_ref[src, r], 0)
            slot = src * HB + r
            served_ref[slot, pl.ds(0, 2), :] = pressure_ref[0, pl.ds(row, 2), :]
            served_ref[slot, pl.ds(2, 2), :] = pressure_ref[0, pl.ds(row + height, 2), :]
        return carry

    lax.fori_loop(0, asked_ref.shape[0], one, 0)


def scatter_kernel(asked_ref, returned_ref, source_ref, *sums):
    depth, height, length = source_ref.shape

    def clear(z, carry):
        for total in sums:
            total[pl.ds(pl.multiple_of(z * height, 8), height)] = jnp.zeros((height, length), F32)
        return carry

    lax.fori_loop(0, depth, clear, 0)

    def one(src, carry):
        for r in range(HB):
            total = sums[r % len(sums)]
            row = asked_ref[src, r]
            row = jnp.where(row < 0, depth * height, row)
            pair = src * PAIRS + 2 * r
            near, far = pl.ds(row, 2), pl.ds(row + height, 2)
            total[near] = total[near] + returned_ref[pair]
            total[far] = total[far] + returned_ref[pair + 1]
        return carry

    lax.fori_loop(0, asked_ref.shape[0], one, 0)

    def collect(z, carry):
        rows = pl.ds(pl.multiple_of(z * height, 8), height)
        value = sums[0][rows]
        for total in sums[1:]:
            value = value + total[rows]
        source_ref[z] = value
        return carry

    lax.fori_loop(0, depth, collect, 0)


def block_weights(place_ref, block, length):
    lateral = lax.broadcasted_iota(jnp.int32, (8, 128), 0) % 4
    shift_z = (lateral // 2).astype(F32) - place_ref[0, pl.ds(block, 1), :]
    shift_y = (lateral % 2).astype(F32) - place_ref[1, pl.ds(block, 1), :]
    across = jnp.exp(-0.5 * (shift_z * shift_z + shift_y * shift_y))
    across_sum = 0.5 * jnp.sum(across, axis=0, keepdims=True)
    offset = place_ref[2, pl.ds(block, 1), :] * float(length - 1)
    shift_x = lax.broadcasted_iota(jnp.int32, (length, 128), 0).astype(F32) - offset
    along = jnp.exp2((-0.5 * math.log2(math.e)) * (shift_x * shift_x))
    return across, across_sum, along


def deposit_kernel(slot_ref, wanted_ref, place_ref, radius_ref, speed_ref, out_ref):
    length = out_ref.shape[2]
    upper = lax.broadcasted_iota(jnp.int32, (8, 128), 0) < 4

    def ask(k, carry):
        for j in range(8):
            home = k * 8 + j
            out_ref[home * PAIRS + 2 * HB, pl.ds(0, 1), :] = wanted_ref[pl.ds(home, 1), :]
        return carry

    lax.fori_loop(0, wanted_ref.shape[0] // 8, ask, 0)

    def one(block):
        across, across_sum, along = block_weights(place_ref, block, length)
        along_sum = jnp.sum(along, axis=0, keepdims=True)
        radius = radius_ref[pl.ds(block, 1), :]
        rate = 4.0 * math.pi * radius * radius * speed_ref[pl.ds(block, 1), :]
        share = across * (rate * inverse(across_sum * along_sum))
        along_hi = along.astype(BF16)
        along_lo = (along - along_hi.astype(F32)).astype(BF16)
        share_hi = share.astype(BF16).astype(F32)
        both = jnp.where(upper, share_hi, share - share_hi).astype(BF16)
        only = jnp.where(upper, share_hi, 0.0).astype(BF16)
        result = dot_nt(both, along_hi) + dot_nt(only, along_lo)
        result = result[0:4] + result[4:8]
        pair = slot_ref[1, block]
        out_ref[pair] = result[0:2]
        out_ref[pair + 1] = result[2:4]

    group = math.gcd(radius_ref.shape[0], 32)

    def several(k, carry):
        for j in range(group):
            one(k * group + j)
        return carry

    lax.fori_loop(0, radius_ref.shape[0] // group, several, 0)


def sample_kernel(slot_ref, place_ref, radius_ref, speed_ref, rest_ref, rows_ref, motion_ref, sampled_ref):
    length = rows_ref.shape[2]
    upper = lax.broadcasted_iota(jnp.int32, (8, 128), 0) < 4

    def one(block):
        across, across_sum, along = block_weights(place_ref, block, length)
        value = rows_ref[slot_ref[0, block]] - pressure_mid
        value = jnp.concatenate([value, value], axis=0)
        high = value.astype(BF16).astype(F32)
        both = jnp.where(upper, high, value - high)
        both = jnp.concatenate([both, jnp.ones_like(both)], axis=0).astype(BF16)
        result = dot_nn(both, along.astype(BF16))
        total = jnp.sum(across * result[0:8], axis=0, keepdims=True)
        sampled_ref[pl.ds(block, 1), :] = pressure_mid + total * inverse(across_sum * result[8:9])

    group = math.gcd(radius_ref.shape[0], 32)

    def several(k, carry):
        for j in range(group):
            one(k * group + j)
        return carry

    lax.fori_loop(0, radius_ref.shape[0] // group, several, 0)

    radius, speed, ratio = radius_ref[...], speed_ref[...], rest_ref[...]
    inv_radius = 1.0 / radius
    gas = (1.0 + 2.0 * surface_tension / (ratio * radius)) * jnp.exp(3.0 * polytropic * jnp.log(ratio))
    wall = gas - (2.0 * surface_tension + 4.0 * liquid_viscosity * speed) * inv_radius
    gas_rate = -3.0 * polytropic * gas * speed * inv_radius
    mach = speed / liquid_sound
    acceleration = (
        (1.0 + mach) * (wall - sampled_ref[...])
        + radius * gas_rate / liquid_sound
        - 1.5 * (1.0 - mach / 3.0) * speed * speed
    ) / ((1.0 - mach) * radius)
    motion_ref[0] = radius + time_step * speed
    motion_ref[1] = speed + time_step * acceleration


def shift_both(low_layers, high_layers, axis):
    count = lax.axis_size(axis)
    below = lax.ppermute(high_layers, axis, [(i, (i + 1) % count) for i in range(count)])
    above = lax.ppermute(low_layers, axis, [((i + 1) % count, i) for i in range(count)])
    return below, above


def exchange(values):
    return lax.all_to_all(values, ("gz", "gy"), split_axis=0, concat_axis=0, tiled=True)


def body(flow_state, block_tiles, bubble_place, bubble_radius, bubble_speed, rest_ratio):
    _, depth, height, length = flow_state.shape
    across_gy = lax.axis_size("gy")
    devices = lax.axis_size("gz") * across_gy
    blocks = block_tiles.shape[0]
    slots = devices * HB
    field = (7, depth, height, length)

    slot, wanted = pl.pallas_call(
        functools.partial(slot_kernel, depth=depth, height=height, across_gy=across_gy),
        out_shape=(shape((2, blocks), jnp.int32), shape((devices, 128))),
        in_specs=[VMEM],
        out_specs=(VMEM, VMEM),
        cost_estimate=cost(2),
        name="slots",
    )(block_tiles.T)
    outgoing = pl.pallas_call(
        deposit_kernel,
        out_shape=shape((devices * PAIRS, 2, length)),
        in_specs=[SMEM] + [VMEM] * 4,
        out_specs=VMEM,
        compiler_params=params(),
        cost_estimate=cost(12),
        name="deposit",
    )(slot, wanted, bubble_place, bubble_radius, bubble_speed)
    returned = exchange(outgoing)

    flow_state, _ = lax.optimization_barrier((flow_state, outgoing))
    prim, z_low, z_high, y_low, y_high = pl.pallas_call(
        primitive_kernel,
        out_shape=(
            shape(field),
            shape((7, 3, height, length)),
            shape((7, 3, height, length)),
            shape((7, 3, depth, length)),
            shape((7, 3, depth, length)),
        ),
        in_specs=[VMEM],
        out_specs=(VMEM,) * 5,
        compiler_params=params(),
        cost_estimate=cost(4),
        name="primitives",
    )(flow_state)
    y_below, y_above = shift_both(y_low, y_high, "gy")
    z_below, z_above = shift_both(z_low, z_high, "gz")

    change_x = pl.pallas_call(
        x_kernel,
        out_shape=shape(field),
        in_specs=[VMEM],
        out_specs=VMEM,
        scratch_shapes=[pltpu.VMEM((7, height, length), F32)] * 2,
        compiler_params=params(),
        cost_estimate=cost(16),
        name="sweep_x",
    )(prim)
    returned, change_x = lax.optimization_barrier((returned, change_x))

    asked = returned.reshape(devices, PAIRS, 2, length)[:, 2 * HB, 0, :HB].astype(jnp.int32)
    rows = depth * height
    served = pl.pallas_call(
        functools.partial(serve_kernel, height=height),
        grid=(1,),
        out_shape=shape((slots, 4, length)),
        in_specs=[SMEM, pl.BlockSpec((1, rows, length), lambda i: (5, 0, 0))],
        out_specs=VMEM,
        compiler_params=params(),
        cost_estimate=cost(5),
        name="serve",
    )(asked, prim.reshape(7, rows, length))
    fetched = exchange(served)

    returned, asked, change_x, served = lax.optimization_barrier((returned, asked, change_x, served))
    source = pl.pallas_call(
        scatter_kernel,
        out_shape=shape((depth, height, length)),
        in_specs=[SMEM, VMEM],
        out_specs=VMEM,
        scratch_shapes=[pltpu.VMEM(((depth + 2) * height, length), F32)] * 4,
        compiler_params=params(),
        cost_estimate=cost(6),
        name="scatter",
    )(asked, returned)

    def scratch(rows):
        return [
            pltpu.VMEM((7, rows, length), F32),
            pltpu.VMEM((rows, length), F32),
            pltpu.VMEM((rows, length), F32),
            pltpu.VMEM((7, rows, length), F32),
            pltpu.VMEM((7, rows, length), F32),
            pltpu.VMEM((8, rows, length), F32),
        ]

    change_xy = pl.pallas_call(
        y_kernel,
        out_shape=shape(field),
        in_specs=[VMEM] * 4,
        out_specs=VMEM,
        scratch_shapes=scratch(16 + depth * (height + 8) + 80),
        compiler_params=params(),
        cost_estimate=cost(16),
        name="sweep_y",
    )(prim, y_below, y_above, change_x)

    state_next = pl.pallas_call(
        z_kernel,
        out_shape=shape(field),
        in_specs=[VMEM] * 6,
        out_specs=VMEM,
        scratch_shapes=scratch((depth + 6) * height),
        compiler_params=params(),
        cost_estimate=cost(15),
        name="sweep_z",
    )(prim, z_below, z_above, change_xy, flow_state, source)

    fetched, state_next = lax.optimization_barrier((fetched, state_next))
    motion = pl.pallas_call(
        sample_kernel,
        out_shape=shape((2, blocks, 128)),
        in_specs=[SMEM] + [VMEM] * 5,
        out_specs=VMEM,
        scratch_shapes=[pltpu.VMEM((blocks, 128), F32)],
        compiler_params=params(),
        cost_estimate=cost(7),
        name="sample",
    )(slot, bubble_place, bubble_radius, bubble_speed, rest_ratio, fetched)
    return state_next, source, motion


def solution(mesh):
    in_specs = (
        P(None, "gz", "gy", None),
        P(("gz", "gy"), None),
        P(None, ("gz", "gy"), None),
        P(("gz", "gy"), None),
        P(("gz", "gy"), None),
        P(("gz", "gy"), None),
    )
    out_specs = (P(None, "gz", "gy", None), P("gz", "gy", None), P(None, ("gz", "gy"), None))
    return jax.shard_map(body, mesh=mesh, in_specs=in_specs, out_specs=out_specs, check_vma=False)
```

```python
import functools
import math

import jax
import jax.numpy as jnp
from jax import lax
from jax.experimental import pallas as pl
from jax.experimental.pallas import tpu as pltpu
from jax.sharding import PartitionSpec as P

HB = 8
PAIRS = 2 * HB + 1
gamma_liquid = 4.4
stiff_liquid = 3.0
gamma_gas = 1.4
time_step = 0.08
liquid_sound = 20.0
surface_tension = 0.01
liquid_viscosity = 0.001
polytropic = 1.4
weno_eps = 1e-06
stiff_base = 1.0 / (gamma_gas - 1.0)
stiff_slope = 1.0 / (gamma_liquid - 1.0) - 1.0 / (gamma_gas - 1.0)
offset_slope = gamma_liquid * stiff_liquid / (gamma_liquid - 1.0)
pressure_mid = 0.9

VMEM = pl.BlockSpec(memory_space=pltpu.VMEM)
SMEM = pl.BlockSpec(memory_space=pltpu.SMEM)
ANY = pl.BlockSpec(memory_space=pl.ANY)
F32 = jnp.float32
BF16 = jnp.bfloat16


def params(mib=56):
    return pltpu.CompilerParams(vmem_limit_bytes=mib * 2**20)


def shape(dims, dtype=F32):
    return jax.ShapeDtypeStruct(dims, dtype)


def cost(microseconds):
    return pl.CostEstimate(flops=int(microseconds * 1.15e9), bytes_accessed=1000, transcendentals=0)


def inverse(value):
    return pl.reciprocal(value, approx=True)


def dot_nt(left, right):
    return lax.dot_general(left, right, (((1,), (1,)), ((), ())), preferred_element_type=F32)


def dot_nn(left, right):
    return lax.dot_general(left, right, (((1,), (0,)), ((), ())), preferred_element_type=F32)


def slot_kernel(tiles_ref, slot_ref, wanted_ref, *, depth, height, across_gy):
    devices = wanted_ref.shape[0]
    blocks = tiles_ref.shape[1]
    anchor = tiles_ref[0:1, :].astype(F32)

    def split(value, size):
        whole = jnp.floor((value + 0.5) * (1.0 / size))
        return whole, value - whole * float(size)

    level, column = split(anchor, height * across_gy)
    home_z, level = split(level, depth)
    home_y, column = split(column, height)
    home = (home_z * float(across_gy) + home_y).astype(jnp.int32)
    onehot = lax.broadcasted_iota(jnp.int32, (devices, blocks), 0) == home
    onehot = jnp.where(onehot, 1.0, 0.0).astype(F32)
    onehot_bf = onehot.astype(BF16)
    earlier = lax.broadcasted_iota(jnp.int32, (blocks, blocks), 0) < lax.broadcasted_iota(
        jnp.int32, (blocks, blocks), 1
    )
    earlier = jnp.where(earlier, 1.0, 0.0).astype(BF16)
    before = dot_nn(onehot_bf, earlier)
    rank = jnp.sum(onehot * before, axis=0, keepdims=True)
    rank = jnp.minimum(rank, HB - 1.0)
    rank_int = rank.astype(jnp.int32)
    slot_ref[...] = jnp.concatenate([home * HB + rank_int, home * PAIRS + 2 * rank_int], axis=0)
    chosen = lax.broadcasted_iota(jnp.int32, (wanted_ref.shape[1], blocks), 0).astype(F32) == rank
    level = jnp.where(chosen, level + 1.0, 0.0).astype(BF16)
    column = jnp.where(chosen, column, 0.0).astype(BF16)
    level = dot_nt(onehot_bf, level)
    column = dot_nt(onehot_bf, column)
    row = (level - 1.0) * float(height) + column
    wanted_ref[...] = jnp.where(level > 0.0, row, -1.0)


def primitives(value):
    first, second = value[0], value[1]
    density = first + second
    inv_density = inverse(density)
    vel = [value[2 + i] * inv_density for i in range(3)]
    kinetic = 0.5 * (value[2] * vel[0] + value[3] * vel[1] + value[4] * vel[2])
    fraction = value[6]
    stiffness = stiff_base + stiff_slope * fraction
    pressure = (value[5] - kinetic - offset_slope * fraction) * inverse(stiffness)
    return [first, second] + vel + [pressure, fraction]


def weno_pair(cell, dm2, dm1, d0, dp1, zm, z0, zp):
    qm = dm1 + d0
    ql = 3.0 * dm1 - dm2
    qh = dp1 - 3.0 * d0
    tl = zm + ql * ql
    tm = z0 + qm * qm
    th = zp + qh * qh
    tl = tl * tl
    tm = tm * tm
    th = th * th
    low = tm * th
    mid = 6.0 * (tl * th)
    high = tl * tm
    low3 = 3.0 * low
    high3 = 3.0 * high
    den_up = 6.0 * (low + mid + high3)
    den_down = 6.0 * (low3 + mid + high)
    num_up = low * (2.0 * ql - dm1) + mid * (qm + d0) + high3 * (d0 - qh)
    num_down = low3 * (ql + dm1) + mid * (qm + dm1) - high * (2.0 * qh + d0)
    return cell + num_up * inverse(den_up), cell - num_down * inverse(den_down)


def curvature(step):
    return (13.0 / 3.0) * (step * step) + 4.0 * weno_eps


def sound_terms(state):
    density = state[0] + state[1]
    stiff_one = (stiff_base + 1.0) + stiff_slope * state[6]
    enthalpy = state[5] * stiff_one + offset_slope * state[6]
    sound = enthalpy * lax.rsqrt(enthalpy * ((stiff_one - 1.0) * density))
    return density, enthalpy, sound


def hllc(left, right, normal):
    density_l, enthalpy_l, sound_l = sound_terms(left)
    density_r, enthalpy_r, sound_r = sound_terms(right)
    speed_l, speed_r = left[2 + normal], right[2 + normal]
    wave_l = jnp.minimum(speed_l - sound_l, speed_r - sound_r)
    wave_r = jnp.maximum(speed_l + sound_l, speed_r + sound_r)
    mass_l = density_l * (wave_l - speed_l)
    mass_r = density_r * (wave_r - speed_r)
    middle = (right[5] - left[5] + mass_l * speed_l - mass_r * speed_r) * inverse(mass_l - mass_r)
    forward = middle >= 0.0
    use_left = (wave_l >= 0.0) | forward
    one = [jnp.where(use_left, a, b) for a, b in zip(left[:6], right[:6])]
    density = jnp.where(use_left, density_l, density_r)
    enthalpy = jnp.where(use_left, enthalpy_l, enthalpy_r)
    wave = jnp.where(use_left, jnp.minimum(wave_l, 0.0), jnp.maximum(wave_r, 0.0))
    speed, pressure = one[2 + normal], one[5]
    ratio = jnp.where(wave != 0.0, wave * inverse(wave - middle), 0.0)
    extra = ratio * (middle - speed)
    carried = speed + extra
    push = density * (extra * (wave - speed))
    mass = density * carried
    kinetic = 0.5 * density * (one[2] * one[2] + one[3] * one[3] + one[4] * one[4])
    flux = [one[0] * carried, one[1] * carried]
    for i in range(3):
        flow = mass * one[2 + i]
        flux.append(flow + (push + pressure) if i == normal else flow)
    flux.append((enthalpy + kinetic) * carried + push * middle)
    flux.append(middle * jnp.where(forward, left[6], right[6]))
    return flux, middle


def x_kernel(
    flow_in, change_out, pressure_ref, z_low_ref, z_high_ref, y_low_ref, y_high_ref,
    flow_ref, prim_ref, cells_ref, step_ref, curve_ref, left_ref, right_ref, flux_ref, load_sems, save_sems,
):
    depth, height, length = flow_ref.shape[1:]
    groups = load_sems.shape[0]
    slabs = depth // groups
    width = slabs * height
    pitch = length + 8
    first = 16
    loads = []
    for g in range(groups):
        here = pl.ds(g * slabs, slabs)
        loads.append(pltpu.make_async_copy(flow_in.at[:, here], flow_ref.at[:, here], load_sems.at[g]))
        loads[-1].start()

    def slab(z, carry):
        rows = pl.ds(pl.multiple_of(z * height, 8), height)
        values = primitives([flow_ref[i, z] for i in range(7)])
        pressure_ref[z] = values[5]
        for i, value in enumerate(values):
            prim_ref[i, rows] = value
            for j in range(3):
                y_low_ref[i, j, pl.ds(z, 1), :] = value[j : j + 1]
                y_high_ref[i, j, pl.ds(z, 1), :] = value[height - 3 + j : height - 2 + j]
        return carry

    for g in range(groups):
        loads[g].wait()
        lax.fori_loop(g * slabs, (g + 1) * slabs, slab, 0)
        base = first + g * pitch
        for i in range(7):
            tile = prim_ref[i, pl.ds(g * width, width)].T
            cells_ref[i, pl.ds(base, length)] = tile
            cells_ref[i, pl.ds(base - 3, 3)] = tile[length - 3 :]
            cells_ref[i, pl.ds(base + length, 3)] = tile[:3]
    for i in range(7):
        z_low_ref[i] = prim_ref[i, pl.ds(0, 3 * height)]
        z_high_ref[i] = prim_ref[i, pl.ds((depth - 3) * height, 3 * height)]

    last = first + groups * pitch
    row_states(cells_ref, step_ref, curve_ref, left_ref, right_ref, 1, first, last)
    row_faces(left_ref, right_ref, flux_ref, 1, first - 8, -(-(last - first + 8) // 32), 0)

    saves = []
    for g in range(groups):
        here, under = pl.ds(first + g * pitch, length), pl.ds(first + g * pitch - 1, length)
        out = pl.ds(g * width, width)
        for i in range(7):
            diff = flux_ref[i, under] - flux_ref[i, here]
            if i == 6:
                diff = diff + cells_ref[6, here] * (flux_ref[7, here] - flux_ref[7, under])
            prim_ref[i, out] = diff.T
        saves.append(pltpu.make_async_copy(prim_ref.at[:, out], change_out.at[:, out], save_sems.at[g]))
        saves[-1].start()
    for save in saves:
        save.wait()


def row_states(cells_ref, step_ref, curve_ref, left_ref, right_ref, stride, first, last):
    size = 64
    reach = -(-stride // 8) * 8

    def loop(begin, end, step):
        lax.fori_loop(0, -(-(end - begin) // size), lambda k, c: step(pl.multiple_of(begin + k * size, 8), c), 0)

    for i in range(7):

        def prepare(row, carry, i=i):
            mid = cells_ref[i, pl.ds(row, size)]
            d0 = cells_ref[i, pl.ds(row + stride, size)] - mid
            dm1 = mid - cells_ref[i, pl.ds(row - stride, size)]
            step_ref[pl.ds(row, size)] = d0
            curve_ref[pl.ds(row, size)] = curvature(d0 - dm1)
            return carry

        if stride == reach:
            edge = pl.ds(first - 3 * stride, size)
            step_ref[edge] = cells_ref[i, pl.ds(first - 2 * stride, size)] - cells_ref[i, edge]
            loop(first - 2 * stride, last + 2 * stride, prepare)
        else:
            loop(first - reach, last + 2 * stride, prepare)

        def states(row, carry, i=i):
            def take(ref, shift):
                return ref[pl.ds(row + shift * stride, size)]

            up, down = weno_pair(
                cells_ref[i, pl.ds(row, size)],
                take(step_ref, -2), take(step_ref, -1), take(step_ref, 0), take(step_ref, 1),
                take(curve_ref, -1), take(curve_ref, 0), take(curve_ref, 1),
            )
            left_ref[i, pl.ds(row, size)] = up
            right_ref[i, pl.ds(row, size)] = down
            return carry

        loop(first - reach, last + stride, states)


def row_faces(left_ref, right_ref, flux_ref, stride, begin, count, normal):
    size = 32

    def faces(k, carry):
        row = pl.multiple_of(begin + k * size, 8)
        left = [left_ref[i, pl.ds(row, size)] for i in range(7)]
        right = [right_ref[i, pl.ds(row + stride, size)] for i in range(7)]
        flux, middle = hllc(left, right, normal)
        for i in range(7):
            flux_ref[i, pl.ds(row, size)] = flux[i]
        flux_ref[7, pl.ds(row, size)] = middle
        return carry

    lax.fori_loop(0, count, faces, 0)


def yz_kernel(
    flow_in, change_in, source_in, z_below_in, z_above_in, y_below_ref, y_above_ref, next_out,
    flow_ref, change_ref, source_ref, cells_z, cells_y, step_ref, curve_ref, left_ref, right_ref, flux_ref,
    flow_sems, side_sems, out_sems,
):
    depth, height = flow_ref.shape[1:3]
    parts = flow_sems.shape[0]
    part = depth // parts
    pitch = height + 8
    first_y = 16
    first_z = 3 * height
    rows_z = depth * height
    loads = []
    for p in range(parts):
        here = pl.ds(p * part, part)
        loads.append(pltpu.make_async_copy(flow_in.at[:, here], flow_ref.at[:, here], flow_sems.at[p]))
    below = pltpu.make_async_copy(z_below_in, cells_z.at[:, pl.ds(0, first_z)], side_sems.at[0])
    above = pltpu.make_async_copy(z_above_in, cells_z.at[:, pl.ds(first_z + rows_z, first_z)], side_sems.at[1])
    change = pltpu.make_async_copy(change_in, change_ref, side_sems.at[2])
    source = pltpu.make_async_copy(source_in, source_ref, side_sems.at[3])
    for copy in loads + [below, above, change, source]:
        copy.start()

    def fill(z, carry):
        base = pl.multiple_of(first_y + z * pitch, 8)
        values = primitives([flow_ref[i, z] for i in range(7)])
        for i, value in enumerate(values):
            cells_z[i, pl.ds(pl.multiple_of(first_z + z * height, 8), height)] = value
            cells_y[i, pl.ds(base, height)] = value
            for j in range(3):
                cells_y[i, pl.ds(base - 3 + j, 1)] = y_below_ref[i, j, pl.ds(z, 1), :]
                cells_y[i, pl.ds(base + height + j, 1)] = y_above_ref[i, j, pl.ds(z, 1), :]
        return carry

    for p in range(parts):
        loads[p].wait()
        lax.fori_loop(p * part, (p + 1) * part, fill, 0)

    last_y = first_y + depth * pitch
    row_states(cells_y, step_ref, curve_ref, left_ref, right_ref, 1, first_y, last_y)
    row_faces(left_ref, right_ref, flux_ref, 1, first_y - 8, -(-(last_y - first_y + 8) // 32), 1)
    change.wait()

    def differences(base, lower, z):
        here, under = pl.ds(base, height), pl.ds(base - lower, height)
        diff = [flux_ref[i, under] - flux_ref[i, here] for i in range(7)]
        fraction = cells_z[6, pl.ds(pl.multiple_of(first_z + z * height, 8), height)]
        diff[6] = diff[6] + fraction * (flux_ref[7, here] - flux_ref[7, under])
        return diff

    def gather(z, carry):
        for i, diff in enumerate(differences(pl.multiple_of(first_y + z * pitch, 8), 1, z)):
            rows = pl.ds(pl.multiple_of(z * height, 8), height)
            change_ref[i, rows] = change_ref[i, rows] + diff
        return carry

    lax.fori_loop(0, depth, gather, 0)

    below.wait()
    above.wait()
    source.wait()
    row_states(cells_z, step_ref, curve_ref, left_ref, right_ref, height, first_z, first_z + rows_z)

    def update(z, carry):
        for i, diff in enumerate(differences(pl.multiple_of(first_z + z * height, 8), height, z)):
            total = change_ref[i, pl.ds(pl.multiple_of(z * height, 8), height)] + diff
            if i == 6:
                total = total - source_ref[z]
            flow_ref[i, z] = flow_ref[i, z] + time_step * total
        return carry

    saves = []
    row_faces(left_ref, right_ref, flux_ref, height, first_z - height, height // 32, 2)
    for p in range(parts):
        row_faces(left_ref, right_ref, flux_ref, height, first_z + p * part * height, part * height // 32, 2)
        lax.fori_loop(p * part, (p + 1) * part, update, 0)
        here = pl.ds(p * part, part)
        saves.append(pltpu.make_async_copy(flow_ref.at[:, here], next_out.at[:, here], out_sems.at[p]))
        saves[-1].start()
    for save in saves:
        save.wait()


def serve_kernel(asked_ref, pressure_ref, served_ref, *, height):
    def one(src, carry):
        for r in range(HB):
            row = jnp.maximum(asked_ref[src, r], 0)
            slot = src * HB + r
            served_ref[slot, pl.ds(0, 2), :] = pressure_ref[pl.ds(row, 2), :]
            served_ref[slot, pl.ds(2, 2), :] = pressure_ref[pl.ds(row + height, 2), :]
        return carry

    lax.fori_loop(0, asked_ref.shape[0], one, 0)


def scatter_kernel(asked_ref, returned_ref, source_ref, *sums):
    depth, height, length = source_ref.shape

    def clear(z, carry):
        for total in sums:
            total[pl.ds(pl.multiple_of(z * height, 8), height)] = jnp.zeros((height, length), F32)
        return carry

    lax.fori_loop(0, depth, clear, 0)

    def one(src, carry):
        for r in range(HB):
            total = sums[r % len(sums)]
            row = asked_ref[src, r]
            row = jnp.where(row < 0, depth * height, row)
            pair = src * PAIRS + 2 * r
            near, far = pl.ds(row, 2), pl.ds(row + height, 2)
            total[near] = total[near] + returned_ref[pair]
            total[far] = total[far] + returned_ref[pair + 1]
        return carry

    lax.fori_loop(0, asked_ref.shape[0], one, 0)

    def collect(z, carry):
        rows = pl.ds(pl.multiple_of(z * height, 8), height)
        value = sums[0][rows]
        for total in sums[1:]:
            value = value + total[rows]
        source_ref[z] = value
        return carry

    lax.fori_loop(0, depth, collect, 0)


def block_weights(place_ref, block, length):
    lateral = lax.broadcasted_iota(jnp.int32, (8, 128), 0) % 4
    shift_z = (lateral // 2).astype(F32) - place_ref[0, pl.ds(block, 1), :]
    shift_y = (lateral % 2).astype(F32) - place_ref[1, pl.ds(block, 1), :]
    across = jnp.exp(-0.5 * (shift_z * shift_z + shift_y * shift_y))
    across_sum = 0.5 * jnp.sum(across, axis=0, keepdims=True)
    offset = place_ref[2, pl.ds(block, 1), :] * float(length - 1)
    shift_x = lax.broadcasted_iota(jnp.int32, (length, 128), 0).astype(F32) - offset
    along = jnp.exp2((-0.5 * math.log2(math.e)) * (shift_x * shift_x))
    return across, across_sum, along


def deposit_kernel(slot_ref, wanted_ref, place_ref, radius_ref, speed_ref, out_ref):
    length = out_ref.shape[2]
    upper = lax.broadcasted_iota(jnp.int32, (8, 128), 0) < 4

    def ask(k, carry):
        for j in range(8):
            home = k * 8 + j
            out_ref[home * PAIRS + 2 * HB, pl.ds(0, 1), :] = wanted_ref[pl.ds(home, 1), :]
        return carry

    lax.fori_loop(0, wanted_ref.shape[0] // 8, ask, 0)

    def one(block):
        across, across_sum, along = block_weights(place_ref, block, length)
        along_sum = jnp.sum(along, axis=0, keepdims=True)
        radius = radius_ref[pl.ds(block, 1), :]
        rate = 4.0 * math.pi * radius * radius * speed_ref[pl.ds(block, 1), :]
        share = across * (rate * inverse(across_sum * along_sum))
        along_hi = along.astype(BF16)
        along_lo = (along - along_hi.astype(F32)).astype(BF16)
        share_hi = share.astype(BF16).astype(F32)
        both = jnp.where(upper, share_hi, share - share_hi).astype(BF16)
        only = jnp.where(upper, share_hi, 0.0).astype(BF16)
        result = dot_nt(both, along_hi) + dot_nt(only, along_lo)
        result = result[0:4] + result[4:8]
        pair = slot_ref[1, block]
        out_ref[pair] = result[0:2]
        out_ref[pair + 1] = result[2:4]

    group = math.gcd(radius_ref.shape[0], 32)

    def several(k, carry):
        for j in range(group):
            one(k * group + j)
        return carry

    lax.fori_loop(0, radius_ref.shape[0] // group, several, 0)


def sample_kernel(slot_ref, place_ref, radius_ref, speed_ref, rest_ref, rows_ref, motion_ref, sampled_ref):
    length = rows_ref.shape[2]
    upper = lax.broadcasted_iota(jnp.int32, (8, 128), 0) < 4

    def one(block):
        across, across_sum, along = block_weights(place_ref, block, length)
        value = rows_ref[slot_ref[0, block]] - pressure_mid
        value = jnp.concatenate([value, value], axis=0)
        high = value.astype(BF16).astype(F32)
        both = jnp.where(upper, high, value - high)
        both = jnp.concatenate([both, jnp.ones_like(both)], axis=0).astype(BF16)
        result = dot_nn(both, along.astype(BF16))
        total = jnp.sum(across * result[0:8], axis=0, keepdims=True)
        sampled_ref[pl.ds(block, 1), :] = pressure_mid + total * inverse(across_sum * result[8:9])

    group = math.gcd(radius_ref.shape[0], 32)

    def several(k, carry):
        for j in range(group):
            one(k * group + j)
        return carry

    lax.fori_loop(0, radius_ref.shape[0] // group, several, 0)

    radius, speed, ratio = radius_ref[...], speed_ref[...], rest_ref[...]
    inv_radius = 1.0 / radius
    gas = (1.0 + 2.0 * surface_tension / (ratio * radius)) * jnp.exp(3.0 * polytropic * jnp.log(ratio))
    wall = gas - (2.0 * surface_tension + 4.0 * liquid_viscosity * speed) * inv_radius
    gas_rate = -3.0 * polytropic * gas * speed * inv_radius
    mach = speed / liquid_sound
    acceleration = (
        (1.0 + mach) * (wall - sampled_ref[...])
        + radius * gas_rate / liquid_sound
        - 1.5 * (1.0 - mach / 3.0) * speed * speed
    ) / ((1.0 - mach) * radius)
    motion_ref[0] = radius + time_step * speed
    motion_ref[1] = speed + time_step * acceleration


def shift_both(low_layers, high_layers, axis):
    count = lax.axis_size(axis)
    below = lax.ppermute(high_layers, axis, [(i, (i + 1) % count) for i in range(count)])
    above = lax.ppermute(low_layers, axis, [((i + 1) % count, i) for i in range(count)])
    return below, above


def exchange(values):
    return lax.all_to_all(values, ("gz", "gy"), split_axis=0, concat_axis=0, tiled=True)


def body(flow_state, block_tiles, bubble_place, bubble_radius, bubble_speed, rest_ratio):
    _, depth, height, length = flow_state.shape
    across_gy = lax.axis_size("gy")
    devices = lax.axis_size("gz") * across_gy
    blocks = block_tiles.shape[0]
    slots = devices * HB
    field = (7, depth, height, length)

    slot, wanted = pl.pallas_call(
        functools.partial(slot_kernel, depth=depth, height=height, across_gy=across_gy),
        out_shape=(shape((2, blocks), jnp.int32), shape((devices, 128))),
        in_specs=[VMEM],
        out_specs=(VMEM, VMEM),
        cost_estimate=cost(2),
        name="slots",
    )(block_tiles.T)
    outgoing = pl.pallas_call(
        deposit_kernel,
        out_shape=shape((devices * PAIRS, 2, length)),
        in_specs=[SMEM] + [VMEM] * 4,
        out_specs=VMEM,
        compiler_params=params(),
        cost_estimate=cost(12),
        name="deposit",
    )(slot, wanted, bubble_place, bubble_radius, bubble_speed)
    returned = exchange(outgoing)

    flow_state, _ = lax.optimization_barrier((flow_state, outgoing))
    rows = depth * height
    groups = rows // 128
    turned = 16 + groups * (length + 8) + 80
    change_x, pressure, z_low, z_high, y_low, y_high = pl.pallas_call(
        x_kernel,
        out_shape=(
            shape((7, rows, length)),
            shape((depth, height, length)),
            shape((7, 3 * height, length)),
            shape((7, 3 * height, length)),
            shape((7, 3, depth, length)),
            shape((7, 3, depth, length)),
        ),
        in_specs=[ANY],
        out_specs=(ANY,) + (VMEM,) * 5,
        scratch_shapes=[
            pltpu.VMEM(field, F32),
            pltpu.VMEM((7, rows, length), F32),
            pltpu.VMEM((7, turned, 128), F32),
            pltpu.VMEM((turned, 128), F32),
            pltpu.VMEM((turned, 128), F32),
            pltpu.VMEM((7, turned, 128), F32),
            pltpu.VMEM((7, turned, 128), F32),
            pltpu.VMEM((8, turned, 128), F32),
            pltpu.SemaphoreType.DMA((groups,)),
            pltpu.SemaphoreType.DMA((groups,)),
        ],
        compiler_params=params(),
        cost_estimate=cost(14),
        name="sweep_x",
    )(flow_state)
    y_below, y_above = shift_both(y_low, y_high, "gy")
    z_below, z_above = shift_both(z_low, z_high, "gz")
    returned, change_x = lax.optimization_barrier((returned, change_x))

    asked = returned.reshape(devices, PAIRS, 2, length)[:, 2 * HB, 0, :HB].astype(jnp.int32)
    served = pl.pallas_call(
        functools.partial(serve_kernel, height=height),
        out_shape=shape((slots, 4, length)),
        in_specs=[SMEM, VMEM],
        out_specs=VMEM,
        compiler_params=params(),
        cost_estimate=cost(5),
        name="serve",
    )(asked, pressure.reshape(rows, length))
    fetched = exchange(served)

    returned, asked, change_x, served = lax.optimization_barrier((returned, asked, change_x, served))
    source = pl.pallas_call(
        scatter_kernel,
        out_shape=shape((depth, height, length)),
        in_specs=[SMEM, VMEM],
        out_specs=VMEM,
        scratch_shapes=[pltpu.VMEM(((depth + 2) * height, length), F32)] * 4,
        compiler_params=params(),
        cost_estimate=cost(6),
        name="scatter",
    )(asked, returned)

    padded = 16 + depth * (height + 8) + 80
    state_next = pl.pallas_call(
        yz_kernel,
        out_shape=shape(field),
        in_specs=[ANY] * 5 + [VMEM] * 2,
        out_specs=ANY,
        scratch_shapes=[
            pltpu.VMEM(field, F32),
            pltpu.VMEM((7, rows, length), F32),
            pltpu.VMEM((depth, height, length), F32),
            pltpu.VMEM((7, rows + 6 * height, length), F32),
            pltpu.VMEM((7, padded, length), F32),
            pltpu.VMEM((padded, length), F32),
            pltpu.VMEM((padded, length), F32),
            pltpu.VMEM((7, padded, length), F32),
            pltpu.VMEM((7, padded, length), F32),
            pltpu.VMEM((8, padded, length), F32),
            pltpu.SemaphoreType.DMA((4,)),
            pltpu.SemaphoreType.DMA((4,)),
            pltpu.SemaphoreType.DMA((4,)),
        ],
        compiler_params=params(),
        cost_estimate=cost(24),
        name="sweep_yz",
    )(flow_state, change_x, source, z_below, z_above, y_below, y_above)

    fetched, state_next = lax.optimization_barrier((fetched, state_next))
    motion = pl.pallas_call(
        sample_kernel,
        out_shape=shape((2, blocks, 128)),
        in_specs=[SMEM] + [VMEM] * 5,
        out_specs=VMEM,
        scratch_shapes=[pltpu.VMEM((blocks, 128), F32)],
        compiler_params=params(),
        cost_estimate=cost(7),
        name="sample",
    )(slot, bubble_place, bubble_radius, bubble_speed, rest_ratio, fetched)
    return state_next, source, motion


def solution(mesh):
    in_specs = (
        P(None, "gz", "gy", None),
        P(("gz", "gy"), None),
        P(None, ("gz", "gy"), None),
        P(("gz", "gy"), None),
        P(("gz", "gy"), None),
        P(("gz", "gy"), None),
    )
    out_specs = (P(None, "gz", "gy", None), P("gz", "gy", None), P(None, ("gz", "gy"), None))
    return jax.shard_map(body, mesh=mesh, in_specs=in_specs, out_specs=out_specs, check_vma=False)
```

```python
import functools
import math

import jax
import jax.numpy as jnp
from jax import lax
from jax.experimental import pallas as pl
from jax.experimental.pallas import tpu as pltpu
from jax.sharding import PartitionSpec as P

HB = 8
PAIRS = 2 * HB + 1
gamma_liquid = 4.4
stiff_liquid = 3.0
gamma_gas = 1.4
time_step = 0.08
liquid_sound = 20.0
surface_tension = 0.01
liquid_viscosity = 0.001
polytropic = 1.4
weno_eps = 1e-06
stiff_base = 1.0 / (gamma_gas - 1.0)
stiff_slope = 1.0 / (gamma_liquid - 1.0) - 1.0 / (gamma_gas - 1.0)
offset_slope = gamma_liquid * stiff_liquid / (gamma_liquid - 1.0)
pressure_mid = 0.9

VMEM = pl.BlockSpec(memory_space=pltpu.VMEM)
SMEM = pl.BlockSpec(memory_space=pltpu.SMEM)
ANY = pl.BlockSpec(memory_space=pl.ANY)
F32 = jnp.float32
BF16 = jnp.bfloat16


def params(mib=63.75):
    return pltpu.CompilerParams(vmem_limit_bytes=int(mib * 2**20))


def shape(dims, dtype=F32):
    return jax.ShapeDtypeStruct(dims, dtype)


def cost(microseconds):
    return pl.CostEstimate(flops=int(microseconds * 1.15e9), bytes_accessed=1000, transcendentals=0)


def inverse(value):
    return pl.reciprocal(value, approx=True)


def dot_nt(left, right):
    return lax.dot_general(left, right, (((1,), (1,)), ((), ())), preferred_element_type=F32)


def dot_nn(left, right):
    return lax.dot_general(left, right, (((1,), (0,)), ((), ())), preferred_element_type=F32)


def find_slots(tiles_ref, devices, depth, height, across_gy):
    blocks = tiles_ref.shape[1]
    anchor = tiles_ref[0:1, :].astype(F32)

    def split(value, size):
        whole = jnp.floor((value + 0.5) * (1.0 / size))
        return whole, value - whole * float(size)

    level, column = split(anchor, height * across_gy)
    home_z, level = split(level, depth)
    home_y, column = split(column, height)
    home = (home_z * float(across_gy) + home_y).astype(jnp.int32)
    onehot = lax.broadcasted_iota(jnp.int32, (devices, blocks), 0) == home
    onehot = jnp.where(onehot, 1.0, 0.0).astype(F32)
    onehot_bf = onehot.astype(BF16)
    earlier = lax.broadcasted_iota(jnp.int32, (blocks, blocks), 0) < lax.broadcasted_iota(
        jnp.int32, (blocks, blocks), 1
    )
    earlier = jnp.where(earlier, 1.0, 0.0).astype(BF16)
    before = dot_nn(onehot_bf, earlier)
    rank = jnp.sum(onehot * before, axis=0, keepdims=True)
    rank = jnp.minimum(rank, HB - 1.0)
    rank_int = rank.astype(jnp.int32)
    slot = jnp.concatenate([home * HB + rank_int, home * PAIRS + 2 * rank_int], axis=0)
    chosen = lax.broadcasted_iota(jnp.int32, (128, blocks), 0).astype(F32) == rank
    level = jnp.where(chosen, level + 1.0, 0.0).astype(BF16)
    column = jnp.where(chosen, column, 0.0).astype(BF16)
    level = dot_nt(onehot_bf, level)
    column = dot_nt(onehot_bf, column)
    row = (level - 1.0) * float(height) + column
    return slot, jnp.where(level > 0.0, row, -1.0)


def primitives(value):
    first, second = value[0], value[1]
    density = first + second
    inv_density = inverse(density)
    vel = [value[2 + i] * inv_density for i in range(3)]
    kinetic = 0.5 * (value[2] * vel[0] + value[3] * vel[1] + value[4] * vel[2])
    fraction = value[6]
    stiffness = stiff_base + stiff_slope * fraction
    pressure = (value[5] - kinetic - offset_slope * fraction) * inverse(stiffness)
    return [first, second] + vel + [pressure, fraction]


def weno_pair(cell, dm2, dm1, d0, dp1, zm, z0, zp):
    qm = dm1 + d0
    ql = 3.0 * dm1 - dm2
    qh = dp1 - 3.0 * d0
    tl = zm + ql * ql
    tm = z0 + qm * qm
    th = zp + qh * qh
    tl = tl * tl
    tm = tm * tm
    th = th * th
    low = tm * th
    mid = 6.0 * (tl * th)
    high = tl * tm
    low3 = 3.0 * low
    high3 = 3.0 * high
    den_up = 6.0 * (low + mid + high3)
    den_down = 6.0 * (low3 + mid + high)
    num_up = low * (2.0 * ql - dm1) + mid * (qm + d0) + high3 * (d0 - qh)
    num_down = low3 * (ql + dm1) + mid * (qm + dm1) - high * (2.0 * qh + d0)
    return cell + num_up * inverse(den_up), cell - num_down * inverse(den_down)


def curvature(step):
    return (13.0 / 3.0) * (step * step) + 4.0 * weno_eps


def sound_terms(state):
    density = state[0] + state[1]
    stiff_one = (stiff_base + 1.0) + stiff_slope * state[6]
    enthalpy = state[5] * stiff_one + offset_slope * state[6]
    sound = enthalpy * lax.rsqrt(enthalpy * ((stiff_one - 1.0) * density))
    return density, enthalpy, sound


def hllc(left, right, normal):
    density_l, enthalpy_l, sound_l = sound_terms(left)
    density_r, enthalpy_r, sound_r = sound_terms(right)
    speed_l, speed_r = left[2 + normal], right[2 + normal]
    wave_l = jnp.minimum(speed_l - sound_l, speed_r - sound_r)
    wave_r = jnp.maximum(speed_l + sound_l, speed_r + sound_r)
    mass_l = density_l * (wave_l - speed_l)
    mass_r = density_r * (wave_r - speed_r)
    middle = (right[5] - left[5] + mass_l * speed_l - mass_r * speed_r) * inverse(mass_l - mass_r)
    forward = middle >= 0.0
    use_left = (wave_l >= 0.0) | forward
    one = [jnp.where(use_left, a, b) for a, b in zip(left[:6], right[:6])]
    density = jnp.where(use_left, density_l, density_r)
    enthalpy = jnp.where(use_left, enthalpy_l, enthalpy_r)
    wave = jnp.where(use_left, jnp.minimum(wave_l, 0.0), jnp.maximum(wave_r, 0.0))
    speed, pressure = one[2 + normal], one[5]
    ratio = jnp.where(wave != 0.0, wave * inverse(wave - middle), 0.0)
    extra = ratio * (middle - speed)
    carried = speed + extra
    push = density * (extra * (wave - speed))
    mass = density * carried
    kinetic = 0.5 * density * (one[2] * one[2] + one[3] * one[3] + one[4] * one[4])
    flux = [one[0] * carried, one[1] * carried]
    for i in range(3):
        flow = mass * one[2 + i]
        flux.append(flow + (push + pressure) if i == normal else flow)
    flux.append((enthalpy + kinetic) * carried + push * middle)
    flux.append(middle * jnp.where(forward, left[6], right[6]))
    return flux, middle


def x_kernel(
    flow_in, change_out, pressure_ref, z_low_ref, z_high_ref, y_low_ref, y_high_ref,
    flow_ref, prim_ref, cells_ref, step_ref, curve_ref, left_ref, right_ref, flux_ref, load_sems, save_sems,
):
    depth, height, length = flow_ref.shape[1:]
    groups = load_sems.shape[0]
    slabs = depth // groups
    width = slabs * height
    pitch = length + 8
    first = 16
    loads = []
    for g in range(groups):
        here = pl.ds(g * slabs, slabs)
        loads.append(pltpu.make_async_copy(flow_in.at[:, here], flow_ref.at[:, here], load_sems.at[g]))
        loads[-1].start()

    def slab(z, carry):
        rows = pl.ds(pl.multiple_of(z * height, 8), height)
        values = primitives([flow_ref[i, z] for i in range(7)])
        pressure_ref[z] = values[5]
        for i, value in enumerate(values):
            prim_ref[i, rows] = value
            for j in range(3):
                y_low_ref[i, j, pl.ds(z, 1), :] = value[j : j + 1]
                y_high_ref[i, j, pl.ds(z, 1), :] = value[height - 3 + j : height - 2 + j]
        return carry

    for g in range(groups):
        loads[g].wait()
        lax.fori_loop(g * slabs, (g + 1) * slabs, slab, 0)
        base = first + g * pitch
        for i in range(7):
            tile = prim_ref[i, pl.ds(g * width, width)].T
            cells_ref[i, pl.ds(base, length)] = tile
            cells_ref[i, pl.ds(base - 3, 3)] = tile[length - 3 :]
            cells_ref[i, pl.ds(base + length, 3)] = tile[:3]
    for i in range(7):
        z_low_ref[i] = prim_ref[i, pl.ds(0, 3 * height)]
        z_high_ref[i] = prim_ref[i, pl.ds((depth - 3) * height, 3 * height)]

    last = first + groups * pitch
    row_states(cells_ref, step_ref, curve_ref, left_ref, right_ref, 1, first, last)
    row_faces(left_ref, right_ref, flux_ref, 1, first - 8, -(-(last - first + 8) // 32), 0)

    saves = []
    for g in range(groups):
        here, under = pl.ds(first + g * pitch, length), pl.ds(first + g * pitch - 1, length)
        out = pl.ds(g * width, width)
        for i in range(7):
            diff = flux_ref[i, under] - flux_ref[i, here]
            if i == 6:
                diff = diff + cells_ref[6, here] * (flux_ref[7, here] - flux_ref[7, under])
            prim_ref[i, out] = diff.T
        saves.append(pltpu.make_async_copy(prim_ref.at[:, out], change_out.at[:, out], save_sems.at[g]))
        saves[-1].start()
    for save in saves:
        save.wait()


def row_states(cells_ref, step_ref, curve_ref, left_ref, right_ref, stride, first, last):
    size = 64
    reach = -(-stride // 8) * 8

    def loop(begin, end, step):
        count = -(-(end - begin) // size)
        lax.fori_loop(0, count, lambda k, c: step(pl.multiple_of(begin + k * size, 8), c), 0, unroll=4)

    for i in range(7):

        def prepare(row, carry, i=i):
            mid = cells_ref[i, pl.ds(row, size)]
            d0 = cells_ref[i, pl.ds(row + stride, size)] - mid
            dm1 = mid - cells_ref[i, pl.ds(row - stride, size)]
            step_ref[pl.ds(row, size)] = d0
            curve_ref[pl.ds(row, size)] = curvature(d0 - dm1)
            return carry

        if stride == reach:
            edge = pl.ds(first - 3 * stride, size)
            step_ref[edge] = cells_ref[i, pl.ds(first - 2 * stride, size)] - cells_ref[i, edge]
            loop(first - 2 * stride, last + 2 * stride, prepare)
        else:
            loop(first - reach, last + 2 * stride, prepare)

        def states(row, carry, i=i):
            def take(ref, shift):
                return ref[pl.ds(row + shift * stride, size)]

            up, down = weno_pair(
                cells_ref[i, pl.ds(row, size)],
                take(step_ref, -2), take(step_ref, -1), take(step_ref, 0), take(step_ref, 1),
                take(curve_ref, -1), take(curve_ref, 0), take(curve_ref, 1),
            )
            left_ref[i, pl.ds(row, size)] = up
            right_ref[i, pl.ds(row, size)] = down
            return carry

        loop(first - reach, last + stride, states)


def row_faces(left_ref, right_ref, flux_ref, stride, begin, count, normal):
    size = 32

    def faces(k, carry):
        row = pl.multiple_of(begin + k * size, 8)
        left = [left_ref[i, pl.ds(row, size)] for i in range(7)]
        right = [right_ref[i, pl.ds(row + stride, size)] for i in range(7)]
        flux, middle = hllc(left, right, normal)
        for i in range(7):
            flux_ref[i, pl.ds(row, size)] = flux[i]
        flux_ref[7, pl.ds(row, size)] = middle
        return carry

    lax.fori_loop(0, count, faces, 0, unroll=2)


def yz_kernel(
    flow_in, change_in, source_in, z_below_in, z_above_in, y_below_in, y_above_in, next_out,
    y_below_ref, y_above_ref, flow_ref, change_ref, source_ref, cells_z, cells_y, step_ref, curve_ref, left_ref, right_ref, flux_ref,
    flow_sems, side_sems, out_sems,
):
    depth, height = flow_ref.shape[1:3]
    parts = flow_sems.shape[0]
    part = depth // parts
    pitch = height + 8
    first_y = 16
    first_z = 3 * height
    rows_z = depth * height
    loads = []
    for p in range(parts):
        here = pl.ds(p * part, part)
        loads.append(pltpu.make_async_copy(flow_in.at[:, here], flow_ref.at[:, here], flow_sems.at[p]))
    below = pltpu.make_async_copy(z_below_in, cells_z.at[:, pl.ds(0, first_z)], side_sems.at[0])
    above = pltpu.make_async_copy(z_above_in, cells_z.at[:, pl.ds(first_z + rows_z, first_z)], side_sems.at[1])
    change = pltpu.make_async_copy(change_in, change_ref, side_sems.at[2])
    source = pltpu.make_async_copy(source_in, source_ref, side_sems.at[3])
    y_below = pltpu.make_async_copy(y_below_in, y_below_ref, side_sems.at[4])
    y_above = pltpu.make_async_copy(y_above_in, y_above_ref, side_sems.at[5])
    for copy in [y_below, y_above] + loads + [below, above, change, source]:
        copy.start()
    y_below.wait()
    y_above.wait()

    def fill(z, carry):
        base = pl.multiple_of(first_y + z * pitch, 8)
        values = primitives([flow_ref[i, z] for i in range(7)])
        for i, value in enumerate(values):
            cells_z[i, pl.ds(pl.multiple_of(first_z + z * height, 8), height)] = value
            cells_y[i, pl.ds(base, height)] = value
            for j in range(3):
                cells_y[i, pl.ds(base - 3 + j, 1)] = y_below_ref[i, j, pl.ds(z, 1), :]
                cells_y[i, pl.ds(base + height + j, 1)] = y_above_ref[i, j, pl.ds(z, 1), :]
        return carry

    for p in range(parts):
        loads[p].wait()
        lax.fori_loop(p * part, (p + 1) * part, fill, 0)

    last_y = first_y + depth * pitch
    row_states(cells_y, step_ref, curve_ref, left_ref, right_ref, 1, first_y, last_y)
    row_faces(left_ref, right_ref, flux_ref, 1, first_y - 8, -(-(last_y - first_y + 8) // 32), 1)
    change.wait()

    def differences(base, lower, z):
        here, under = pl.ds(base, height), pl.ds(base - lower, height)
        diff = [flux_ref[i, under] - flux_ref[i, here] for i in range(7)]
        fraction = cells_z[6, pl.ds(pl.multiple_of(first_z + z * height, 8), height)]
        diff[6] = diff[6] + fraction * (flux_ref[7, here] - flux_ref[7, under])
        return diff

    def gather(z, carry):
        for i, diff in enumerate(differences(pl.multiple_of(first_y + z * pitch, 8), 1, z)):
            rows = pl.ds(pl.multiple_of(z * height, 8), height)
            change_ref[i, rows] = change_ref[i, rows] + diff
        return carry

    lax.fori_loop(0, depth, gather, 0)

    below.wait()
    above.wait()
    source.wait()
    row_states(cells_z, step_ref, curve_ref, left_ref, right_ref, height, first_z, first_z + rows_z)

    def update(z, carry):
        for i, diff in enumerate(differences(pl.multiple_of(first_z + z * height, 8), height, z)):
            total = change_ref[i, pl.ds(pl.multiple_of(z * height, 8), height)] + diff
            if i == 6:
                total = total - source_ref[z]
            flow_ref[i, z] = flow_ref[i, z] + time_step * total
        return carry

    saves = []
    row_faces(left_ref, right_ref, flux_ref, height, first_z - height, height // 32, 2)
    for p in range(parts):
        row_faces(left_ref, right_ref, flux_ref, height, first_z + p * part * height, part * height // 32, 2)
        lax.fori_loop(p * part, (p + 1) * part, update, 0)
        here = pl.ds(p * part, part)
        saves.append(pltpu.make_async_copy(flow_ref.at[:, here], next_out.at[:, here], out_sems.at[p]))
        saves[-1].start()
    for save in saves:
        save.wait()


def serve_kernel(asked_ref, pressure_ref, served_out, served_ref, sems, *, height):
    parts = sems.shape[0]
    sources = asked_ref.shape[0] // parts

    def one(src, carry):
        for r in range(HB):
            row = jnp.maximum(asked_ref[src, r], 0)
            slot = src * HB + r
            served_ref[slot, pl.ds(0, 2), :] = pressure_ref[pl.ds(row, 2), :]
            served_ref[slot, pl.ds(2, 2), :] = pressure_ref[pl.ds(row + height, 2), :]
        return carry

    saves = []
    for p in range(parts):
        lax.fori_loop(p * sources, (p + 1) * sources, one, 0, unroll=4)
        here = pl.ds(p * sources * HB, sources * HB)
        saves.append(pltpu.make_async_copy(served_ref.at[here], served_out.at[here], sems.at[p]))
        saves[-1].start()
    for save in saves:
        save.wait()


def scatter_kernel(asked_ref, returned_ref, source_ref, *sums):
    depth, height, length = source_ref.shape

    def clear(z, carry):
        for total in sums:
            total[pl.ds(pl.multiple_of(z * height, 8), height)] = jnp.zeros((height, length), F32)
        return carry

    lax.fori_loop(0, depth, clear, 0)

    def one(src, carry):
        for r in range(HB):
            total = sums[r % len(sums)]
            row = asked_ref[src, r]
            row = jnp.where(row < 0, depth * height, row)
            pair = src * PAIRS + 2 * r
            near, far = pl.ds(row, 2), pl.ds(row + height, 2)
            total[near] = total[near] + returned_ref[pair]
            total[far] = total[far] + returned_ref[pair + 1]
        return carry

    lax.fori_loop(0, asked_ref.shape[0], one, 0, unroll=4)

    def collect(z, carry):
        rows = pl.ds(pl.multiple_of(z * height, 8), height)
        value = sums[0][rows]
        for total in sums[1:]:
            value = value + total[rows]
        source_ref[z] = value
        return carry

    lax.fori_loop(0, depth, collect, 0)


def block_weights(place_ref, block, length):
    lateral = lax.broadcasted_iota(jnp.int32, (8, 128), 0) % 4
    shift_z = (lateral // 2).astype(F32) - place_ref[0, pl.ds(block, 1), :]
    shift_y = (lateral % 2).astype(F32) - place_ref[1, pl.ds(block, 1), :]
    across = jnp.exp(-0.5 * (shift_z * shift_z + shift_y * shift_y))
    across_sum = 0.5 * jnp.sum(across, axis=0, keepdims=True)
    offset = place_ref[2, pl.ds(block, 1), :] * float(length - 1)
    shift_x = lax.broadcasted_iota(jnp.int32, (length, 128), 0).astype(F32) - offset
    along = jnp.exp2((-0.5 * math.log2(math.e)) * (shift_x * shift_x))
    return across, across_sum, along


def deposit_kernel(
    tiles_ref, place_ref, radius_ref, speed_ref, slot_out, out_ref, slot_ref, wanted_ref, sem, *, depth, height, across_gy
):
    length = out_ref.shape[2]
    slot, wanted = find_slots(tiles_ref, wanted_ref.shape[0], depth, height, across_gy)
    slot_out[...] = slot
    wanted_ref[...] = wanted
    move = pltpu.make_async_copy(slot_out, slot_ref, sem)
    move.start()
    upper = lax.broadcasted_iota(jnp.int32, (8, 128), 0) < 4

    def ask(k, carry):
        for j in range(8):
            home = k * 8 + j
            out_ref[home * PAIRS + 2 * HB, pl.ds(0, 1), :] = wanted_ref[pl.ds(home, 1), :]
        return carry

    lax.fori_loop(0, wanted_ref.shape[0] // 8, ask, 0)
    move.wait()

    def one(block):
        across, across_sum, along = block_weights(place_ref, block, length)
        along_sum = jnp.sum(along, axis=0, keepdims=True)
        radius = radius_ref[pl.ds(block, 1), :]
        rate = 4.0 * math.pi * radius * radius * speed_ref[pl.ds(block, 1), :]
        share = across * (rate * inverse(across_sum * along_sum))
        along_hi = along.astype(BF16)
        along_lo = (along - along_hi.astype(F32)).astype(BF16)
        share_hi = share.astype(BF16).astype(F32)
        both = jnp.where(upper, share_hi, share - share_hi).astype(BF16)
        only = jnp.where(upper, share_hi, 0.0).astype(BF16)
        result = dot_nt(
            jnp.concatenate([both, only], axis=1), jnp.concatenate([along_hi, along_lo], axis=1)
        )
        result = result[0:4] + result[4:8]
        pair = slot_ref[1, block]
        out_ref[pair] = result[0:2]
        out_ref[pair + 1] = result[2:4]

    group = math.gcd(radius_ref.shape[0], 64)

    def several(k, carry):
        for j in range(group):
            one(k * group + j)
        return carry

    lax.fori_loop(0, radius_ref.shape[0] // group, several, 0)


def sample_kernel(
    slot_ref, place_ref, radius_ref, speed_ref, rest_ref, fetched_in, motion_ref, sampled_ref, scale_ref, rows_ref, sem
):
    length = rows_ref.shape[2]
    load = pltpu.make_async_copy(fetched_in, rows_ref, sem)
    load.start()
    upper = lax.broadcasted_iota(jnp.int32, (8, 128), 0) < 4

    radius, speed, ratio = radius_ref[...], speed_ref[...], rest_ref[...]
    inv_radius = 1.0 / radius
    gas = (1.0 + 2.0 * surface_tension / (ratio * radius)) * jnp.exp(3.0 * polytropic * jnp.log(ratio))
    wall = gas - (2.0 * surface_tension + 4.0 * liquid_viscosity * speed) * inv_radius
    gas_rate = -3.0 * polytropic * gas * speed * inv_radius
    mach = speed / liquid_sound
    scale = time_step / ((1.0 - mach) * radius)
    motion_ref[0] = radius + time_step * speed
    motion_ref[1] = speed + scale * (
        (1.0 + mach) * wall + radius * gas_rate / liquid_sound - 1.5 * (1.0 - mach / 3.0) * speed * speed
    )
    scale_ref[...] = scale * (1.0 + mach)
    load.wait()

    def one(block):
        across, across_sum, along = block_weights(place_ref, block, length)
        value = rows_ref[slot_ref[0, block]] - pressure_mid
        value = jnp.concatenate([value, value], axis=0)
        high = value.astype(BF16).astype(F32)
        both = jnp.where(upper, high, value - high)
        both = jnp.concatenate([both, jnp.ones_like(both)], axis=0).astype(BF16)
        result = dot_nn(both, along.astype(BF16))
        total = jnp.sum(across * result[0:8], axis=0, keepdims=True)
        sampled_ref[pl.ds(block, 1), :] = pressure_mid + total * inverse(across_sum * result[8:9])

    group = math.gcd(radius_ref.shape[0], 64)

    def several(k, carry):
        for j in range(group):
            one(k * group + j)
        return carry

    lax.fori_loop(0, radius_ref.shape[0] // group, several, 0)
    motion_ref[1] = motion_ref[1] - scale_ref[...] * sampled_ref[...]


def shift_both(low_layers, high_layers, axis):
    count = lax.axis_size(axis)
    below = lax.ppermute(high_layers, axis, [(i, (i + 1) % count) for i in range(count)])
    above = lax.ppermute(low_layers, axis, [((i + 1) % count, i) for i in range(count)])
    return below, above


def exchange(values):
    return lax.all_to_all(values, ("gz", "gy"), split_axis=0, concat_axis=0, tiled=True)


def body(flow_state, block_tiles, bubble_place, bubble_radius, bubble_speed, rest_ratio):
    _, depth, height, length = flow_state.shape
    across_gy = lax.axis_size("gy")
    devices = lax.axis_size("gz") * across_gy
    blocks = block_tiles.shape[0]
    slots = devices * HB
    field = (7, depth, height, length)

    slot, outgoing = pl.pallas_call(
        functools.partial(deposit_kernel, depth=depth, height=height, across_gy=across_gy),
        out_shape=(shape((2, blocks), jnp.int32), shape((devices * PAIRS, 2, length))),
        in_specs=[VMEM] * 4,
        out_specs=(VMEM, VMEM),
        scratch_shapes=[
            pltpu.SMEM((2, blocks), jnp.int32),
            pltpu.VMEM((devices, 128), F32),
            pltpu.SemaphoreType.DMA,
        ],
        compiler_params=params(),
        cost_estimate=cost(10),
        name="deposit",
    )(block_tiles.T, bubble_place, bubble_radius, bubble_speed)
    returned = exchange(outgoing)

    flow_state, _ = lax.optimization_barrier((flow_state, outgoing))
    rows = depth * height
    groups = rows // 128
    turned = 16 + groups * (length + 8) + 80
    change_x, pressure, z_low, z_high, y_low, y_high = pl.pallas_call(
        x_kernel,
        out_shape=(
            shape((7, rows, length)),
            shape((depth, height, length)),
            shape((7, 3 * height, length)),
            shape((7, 3 * height, length)),
            shape((7, 3, depth, length)),
            shape((7, 3, depth, length)),
        ),
        in_specs=[ANY],
        out_specs=(ANY,) + (VMEM,) * 5,
        scratch_shapes=[
            pltpu.VMEM(field, F32),
            pltpu.VMEM((7, rows, length), F32),
            pltpu.VMEM((7, turned, 128), F32),
            pltpu.VMEM((turned, 128), F32),
            pltpu.VMEM((turned, 128), F32),
            pltpu.VMEM((7, turned, 128), F32),
            pltpu.VMEM((7, turned, 128), F32),
            pltpu.VMEM((8, turned, 128), F32),
            pltpu.SemaphoreType.DMA((groups,)),
            pltpu.SemaphoreType.DMA((groups,)),
        ],
        compiler_params=params(),
        cost_estimate=cost(14),
        name="sweep_x",
    )(flow_state)
    y_below, y_above = shift_both(y_low, y_high, "gy")
    z_below, z_above = shift_both(z_low, z_high, "gz")
    returned, change_x = lax.optimization_barrier((returned, change_x))

    asked = returned.reshape(devices, PAIRS, 2, length)[:, 2 * HB, 0, :HB].astype(jnp.int32)
    served = pl.pallas_call(
        functools.partial(serve_kernel, height=height),
        out_shape=shape((slots, 4, length)),
        in_specs=[SMEM, VMEM],
        out_specs=ANY,
        scratch_shapes=[pltpu.VMEM((slots, 4, length), F32), pltpu.SemaphoreType.DMA((4,))],
        compiler_params=params(56),
        cost_estimate=cost(5),
        name="serve",
    )(asked, pressure.reshape(rows, length))
    fetched = exchange(served)

    returned, asked, change_x, served = lax.optimization_barrier((returned, asked, change_x, served))
    source = pl.pallas_call(
        scatter_kernel,
        out_shape=shape((depth, height, length)),
        in_specs=[SMEM, VMEM],
        out_specs=VMEM,
        scratch_shapes=[pltpu.VMEM(((depth + 2) * height, length), F32)] * 4,
        compiler_params=params(56),
        cost_estimate=cost(6),
        name="scatter",
    )(asked, returned)

    padded = 16 + depth * (height + 8) + 80
    state_next = pl.pallas_call(
        yz_kernel,
        out_shape=shape(field),
        in_specs=[ANY] * 7,
        out_specs=ANY,
        scratch_shapes=[
            pltpu.VMEM((7, 3, depth, length), F32),
            pltpu.VMEM((7, 3, depth, length), F32),
            pltpu.VMEM(field, F32),
            pltpu.VMEM((7, rows, length), F32),
            pltpu.VMEM((depth, height, length), F32),
            pltpu.VMEM((7, rows + 6 * height, length), F32),
            pltpu.VMEM((7, padded, length), F32),
            pltpu.VMEM((padded, length), F32),
            pltpu.VMEM((padded, length), F32),
            pltpu.VMEM((7, padded, length), F32),
            pltpu.VMEM((7, padded, length), F32),
            pltpu.VMEM((8, padded, length), F32),
            pltpu.SemaphoreType.DMA((4,)),
            pltpu.SemaphoreType.DMA((6,)),
            pltpu.SemaphoreType.DMA((4,)),
        ],
        compiler_params=params(),
        cost_estimate=cost(24),
        name="sweep_yz",
    )(flow_state, change_x, source, z_below, z_above, y_below, y_above)

    fetched, state_next = lax.optimization_barrier((fetched, state_next))
    motion = pl.pallas_call(
        sample_kernel,
        out_shape=shape((2, blocks, 128)),
        in_specs=[SMEM] + [VMEM] * 4 + [ANY],
        out_specs=VMEM,
        scratch_shapes=[
            pltpu.VMEM((blocks, 128), F32),
            pltpu.VMEM((blocks, 128), F32),
            pltpu.VMEM((slots, 4, length), F32),
            pltpu.SemaphoreType.DMA,
        ],
        compiler_params=params(),
        cost_estimate=cost(7),
        name="sample",
    )(slot, bubble_place, bubble_radius, bubble_speed, rest_ratio, fetched)
    return state_next, source, motion


def solution(mesh):
    in_specs = (
        P(None, "gz", "gy", None),
        P(("gz", "gy"), None),
        P(None, ("gz", "gy"), None),
        P(("gz", "gy"), None),
        P(("gz", "gy"), None),
        P(("gz", "gy"), None),
    )
    out_specs = (P(None, "gz", "gy", None), P("gz", "gy", None), P(None, ("gz", "gy"), None))
    return jax.shard_map(body, mesh=mesh, in_specs=in_specs, out_specs=out_specs, check_vma=False)
```

```python
import functools
import math

import jax
import jax.numpy as jnp
from jax import lax
from jax.experimental import pallas as pl
from jax.experimental.pallas import tpu as pltpu
from jax.sharding import PartitionSpec as P

HB = 8
PAIRS = 2 * HB + 1
gamma_liquid = 4.4
stiff_liquid = 3.0
gamma_gas = 1.4
time_step = 0.08
liquid_sound = 20.0
surface_tension = 0.01
liquid_viscosity = 0.001
polytropic = 1.4
weno_eps = 1e-06
stiff_base = 1.0 / (gamma_gas - 1.0)
stiff_slope = 1.0 / (gamma_liquid - 1.0) - 1.0 / (gamma_gas - 1.0)
offset_slope = gamma_liquid * stiff_liquid / (gamma_liquid - 1.0)
pressure_mid = 0.9

VMEM = pl.BlockSpec(memory_space=pltpu.VMEM)
SMEM = pl.BlockSpec(memory_space=pltpu.SMEM)
ANY = pl.BlockSpec(memory_space=pl.ANY)
F32 = jnp.float32
BF16 = jnp.bfloat16


def params(mib=63.75):
    return pltpu.CompilerParams(vmem_limit_bytes=int(mib * 2**20))


def shape(dims, dtype=F32):
    return jax.ShapeDtypeStruct(dims, dtype)


def cost(microseconds):
    return pl.CostEstimate(flops=int(microseconds * 1.15e9), bytes_accessed=1000, transcendentals=0)


def inverse(value):
    return pl.reciprocal(value, approx=True)


def dot_nt(left, right):
    return lax.dot_general(left, right, (((1,), (1,)), ((), ())), preferred_element_type=F32)


def dot_nn(left, right):
    return lax.dot_general(left, right, (((1,), (0,)), ((), ())), preferred_element_type=F32)


def find_slots(tiles_ref, devices, depth, height, across_gy):
    blocks = tiles_ref.shape[1]
    anchor = tiles_ref[0:1, :].astype(F32)

    def split(value, size):
        whole = jnp.floor((value + 0.5) * (1.0 / size))
        return whole, value - whole * float(size)

    level, column = split(anchor, height * across_gy)
    home_z, level = split(level, depth)
    home_y, column = split(column, height)
    home = (home_z * float(across_gy) + home_y).astype(jnp.int32)
    onehot = lax.broadcasted_iota(jnp.int32, (devices, blocks), 0) == home
    onehot = jnp.where(onehot, 1.0, 0.0).astype(F32)
    onehot_bf = onehot.astype(BF16)
    earlier = lax.broadcasted_iota(jnp.int32, (blocks, blocks), 0) < lax.broadcasted_iota(
        jnp.int32, (blocks, blocks), 1
    )
    earlier = jnp.where(earlier, 1.0, 0.0).astype(BF16)
    before = dot_nn(onehot_bf, earlier)
    rank = jnp.sum(onehot * before, axis=0, keepdims=True)
    rank = jnp.minimum(rank, HB - 1.0)
    rank_int = rank.astype(jnp.int32)
    slot = jnp.concatenate([home * HB + rank_int, home * PAIRS + 2 * rank_int], axis=0)
    chosen = lax.broadcasted_iota(jnp.int32, (128, blocks), 0).astype(F32) == rank
    level = jnp.where(chosen, level + 1.0, 0.0).astype(BF16)
    column = jnp.where(chosen, column, 0.0).astype(BF16)
    level = dot_nt(onehot_bf, level)
    column = dot_nt(onehot_bf, column)
    row = (level - 1.0) * float(height) + column
    return slot, jnp.where(level > 0.0, row, -1.0)


def primitives(value):
    first, second = value[0], value[1]
    density = first + second
    inv_density = inverse(density)
    vel = [value[2 + i] * inv_density for i in range(3)]
    kinetic = 0.5 * (value[2] * vel[0] + value[3] * vel[1] + value[4] * vel[2])
    fraction = value[6]
    stiffness = stiff_base + stiff_slope * fraction
    pressure = (value[5] - kinetic - offset_slope * fraction) * inverse(stiffness)
    return [first, second] + vel + [pressure, fraction]


def weno_pair(cell, dm2, dm1, d0, dp1, zm, z0, zp):
    qm = dm1 + d0
    ql = 3.0 * dm1 - dm2
    qh = dp1 - 3.0 * d0
    tl = zm + ql * ql
    tm = z0 + qm * qm
    th = zp + qh * qh
    tl = tl * tl
    tm = tm * tm
    th = th * th
    low = tm * th
    mid = 6.0 * (tl * th)
    high = tl * tm
    low3 = 3.0 * low
    high3 = 3.0 * high
    den_up = 6.0 * (low + mid + high3)
    den_down = 6.0 * (low3 + mid + high)
    num_up = low * (2.0 * ql - dm1) + mid * (qm + d0) + high3 * (d0 - qh)
    num_down = low3 * (ql + dm1) + mid * (qm + dm1) - high * (2.0 * qh + d0)
    return cell + num_up * inverse(den_up), cell - num_down * inverse(den_down)


def curvature(step):
    return (13.0 / 3.0) * (step * step) + 4.0 * weno_eps


def sound_terms(state):
    density = state[0] + state[1]
    stiff_one = (stiff_base + 1.0) + stiff_slope * state[6]
    enthalpy = state[5] * stiff_one + offset_slope * state[6]
    sound = enthalpy * lax.rsqrt(enthalpy * ((stiff_one - 1.0) * density))
    return density, enthalpy, sound


def hllc(left, right, normal):
    density_l, enthalpy_l, sound_l = sound_terms(left)
    density_r, enthalpy_r, sound_r = sound_terms(right)
    speed_l, speed_r = left[2 + normal], right[2 + normal]
    wave_l = jnp.minimum(speed_l - sound_l, speed_r - sound_r)
    wave_r = jnp.maximum(speed_l + sound_l, speed_r + sound_r)
    mass_l = density_l * (wave_l - speed_l)
    mass_r = density_r * (wave_r - speed_r)
    middle = (right[5] - left[5] + mass_l * speed_l - mass_r * speed_r) * inverse(mass_l - mass_r)
    forward = middle >= 0.0
    use_left = (wave_l >= 0.0) | forward
    one = [jnp.where(use_left, a, b) for a, b in zip(left[:6], right[:6])]
    density = jnp.where(use_left, density_l, density_r)
    enthalpy = jnp.where(use_left, enthalpy_l, enthalpy_r)
    wave = jnp.where(use_left, jnp.minimum(wave_l, 0.0), jnp.maximum(wave_r, 0.0))
    speed, pressure = one[2 + normal], one[5]
    ratio = jnp.where(wave != 0.0, wave * inverse(wave - middle), 0.0)
    extra = ratio * (middle - speed)
    carried = speed + extra
    push = density * (extra * (wave - speed))
    mass = density * carried
    kinetic = 0.5 * density * (one[2] * one[2] + one[3] * one[3] + one[4] * one[4])
    flux = [one[0] * carried, one[1] * carried]
    for i in range(3):
        flow = mass * one[2 + i]
        flux.append(flow + (push + pressure) if i == normal else flow)
    flux.append((enthalpy + kinetic) * carried + push * middle)
    flux.append(middle * jnp.where(forward, left[6], right[6]))
    return flux, middle


def x_kernel(
    flow_in, change_out, pressure_ref, z_low_ref, z_high_ref, y_low_ref, y_high_ref,
    flow_ref, prim_ref, cells_ref, step_ref, curve_ref, left_ref, right_ref, flux_ref, load_sems, save_sems,
):
    depth, height, length = flow_ref.shape[1:]
    groups = load_sems.shape[0]
    slabs = depth // groups
    width = slabs * height
    pitch = length + 8
    first = 16
    loads = []
    for g in range(groups):
        here = pl.ds(g * slabs, slabs)
        loads.append(pltpu.make_async_copy(flow_in.at[:, here], flow_ref.at[:, here], load_sems.at[g]))
        loads[-1].start()

    def slab(z, carry):
        rows = pl.ds(pl.multiple_of(z * height, 8), height)
        values = primitives([flow_ref[i, z] for i in range(7)])
        pressure_ref[z] = values[5]
        for i, value in enumerate(values):
            prim_ref[i, rows] = value
            for j in range(3):
                y_low_ref[i, j, pl.ds(z, 1), :] = value[j : j + 1]
                y_high_ref[i, j, pl.ds(z, 1), :] = value[height - 3 + j : height - 2 + j]
        return carry

    for g in range(groups):
        loads[g].wait()
        lax.fori_loop(g * slabs, (g + 1) * slabs, slab, 0)
        base = first + g * pitch
        for i in range(7):
            tile = prim_ref[i, pl.ds(g * width, width)].T
            cells_ref[i, pl.ds(base, length)] = tile
            cells_ref[i, pl.ds(base - 3, 3)] = tile[length - 3 :]
            cells_ref[i, pl.ds(base + length, 3)] = tile[:3]
    for i in range(7):
        z_low_ref[i] = prim_ref[i, pl.ds(0, 3 * height)]
        z_high_ref[i] = prim_ref[i, pl.ds((depth - 3) * height, 3 * height)]

    last = first + groups * pitch
    row_states(cells_ref, step_ref, curve_ref, left_ref, right_ref, 1, first, last)
    row_faces(left_ref, right_ref, flux_ref, 1, first - 8, -(-(last - first + 8) // 32), 0)

    saves = []
    for g in range(groups):
        here, under = pl.ds(first + g * pitch, length), pl.ds(first + g * pitch - 1, length)
        out = pl.ds(g * width, width)
        for i in range(7):
            diff = flux_ref[i, under] - flux_ref[i, here]
            if i == 6:
                diff = diff + cells_ref[6, here] * (flux_ref[7, here] - flux_ref[7, under])
            prim_ref[i, out] = diff.T
        saves.append(pltpu.make_async_copy(prim_ref.at[:, out], change_out.at[:, out], save_sems.at[g]))
        saves[-1].start()
    for save in saves:
        save.wait()


def row_states(cells_ref, step_ref, curve_ref, left_ref, right_ref, stride, first, last):
    size = 64
    reach = -(-stride // 8) * 8

    def loop(begin, end, step):
        count = -(-(end - begin) // size)
        lax.fori_loop(0, count, lambda k, c: step(pl.multiple_of(begin + k * size, 8), c), 0, unroll=4)

    for i in range(7):

        def prepare(row, carry, i=i):
            mid = cells_ref[i, pl.ds(row, size)]
            d0 = cells_ref[i, pl.ds(row + stride, size)] - mid
            dm1 = mid - cells_ref[i, pl.ds(row - stride, size)]
            step_ref[pl.ds(row, size)] = d0
            curve_ref[pl.ds(row, size)] = curvature(d0 - dm1)
            return carry

        if stride == reach:
            edge = pl.ds(first - 3 * stride, size)
            step_ref[edge] = cells_ref[i, pl.ds(first - 2 * stride, size)] - cells_ref[i, edge]
            loop(first - 2 * stride, last + 2 * stride, prepare)
        else:
            loop(first - reach, last + 2 * stride, prepare)

        def states(row, carry, i=i):
            def take(ref, shift):
                return ref[pl.ds(row + shift * stride, size)]

            up, down = weno_pair(
                cells_ref[i, pl.ds(row, size)],
                take(step_ref, -2), take(step_ref, -1), take(step_ref, 0), take(step_ref, 1),
                take(curve_ref, -1), take(curve_ref, 0), take(curve_ref, 1),
            )
            left_ref[i, pl.ds(row, size)] = up
            right_ref[i, pl.ds(row, size)] = down
            return carry

        loop(first - reach, last + stride, states)


def row_faces(left_ref, right_ref, flux_ref, stride, begin, count, normal):
    size = 32

    def faces(k, carry):
        row = pl.multiple_of(begin + k * size, 8)
        left = [left_ref[i, pl.ds(row, size)] for i in range(7)]
        right = [right_ref[i, pl.ds(row + stride, size)] for i in range(7)]
        flux, middle = hllc(left, right, normal)
        for i in range(7):
            flux_ref[i, pl.ds(row, size)] = flux[i]
        flux_ref[7, pl.ds(row, size)] = middle
        return carry

    lax.fori_loop(0, count, faces, 0, unroll=2)


def yz_kernel(
    flow_in, change_in, source_in, z_below_in, z_above_in, y_below_in, y_above_in, next_out,
    y_below_ref, y_above_ref, flow_ref, change_ref, source_ref, cells_z, cells_y, step_ref, curve_ref, left_ref, right_ref, flux_ref,
    flow_sems, side_sems, out_sems,
):
    depth, height = flow_ref.shape[1:3]
    parts = flow_sems.shape[0]
    part = depth // parts
    pitch = height + 8
    first_y = 16
    first_z = 3 * height
    rows_z = depth * height
    loads = []
    for p in range(parts):
        here = pl.ds(p * part, part)
        loads.append(pltpu.make_async_copy(flow_in.at[:, here], flow_ref.at[:, here], flow_sems.at[p]))
    below = pltpu.make_async_copy(z_below_in, cells_z.at[:, pl.ds(0, first_z)], side_sems.at[0])
    above = pltpu.make_async_copy(z_above_in, cells_z.at[:, pl.ds(first_z + rows_z, first_z)], side_sems.at[1])
    change = pltpu.make_async_copy(change_in, change_ref, side_sems.at[2])
    source = pltpu.make_async_copy(source_in, source_ref, side_sems.at[3])
    y_below = pltpu.make_async_copy(y_below_in, y_below_ref, side_sems.at[4])
    y_above = pltpu.make_async_copy(y_above_in, y_above_ref, side_sems.at[5])
    for copy in [y_below, y_above] + loads + [below, above, change, source]:
        copy.start()
    y_below.wait()
    y_above.wait()

    def fill(z, carry):
        base = pl.multiple_of(first_y + z * pitch, 8)
        values = primitives([flow_ref[i, z] for i in range(7)])
        for i, value in enumerate(values):
            cells_z[i, pl.ds(pl.multiple_of(first_z + z * height, 8), height)] = value
            cells_y[i, pl.ds(base, height)] = value
            for j in range(3):
                cells_y[i, pl.ds(base - 3 + j, 1)] = y_below_ref[i, j, pl.ds(z, 1), :]
                cells_y[i, pl.ds(base + height + j, 1)] = y_above_ref[i, j, pl.ds(z, 1), :]
        return carry

    for p in range(parts):
        loads[p].wait()
        lax.fori_loop(p * part, (p + 1) * part, fill, 0)

    last_y = first_y + depth * pitch
    row_states(cells_y, step_ref, curve_ref, left_ref, right_ref, 1, first_y, last_y)
    row_faces(left_ref, right_ref, flux_ref, 1, first_y - 8, -(-(last_y - first_y + 8) // 32), 1)
    change.wait()

    def differences(base, lower, z):
        here, under = pl.ds(base, height), pl.ds(base - lower, height)
        diff = [flux_ref[i, under] - flux_ref[i, here] for i in range(7)]
        fraction = cells_z[6, pl.ds(pl.multiple_of(first_z + z * height, 8), height)]
        diff[6] = diff[6] + fraction * (flux_ref[7, here] - flux_ref[7, under])
        return diff

    def gather(z, carry):
        for i, diff in enumerate(differences(pl.multiple_of(first_y + z * pitch, 8), 1, z)):
            rows = pl.ds(pl.multiple_of(z * height, 8), height)
            change_ref[i, rows] = change_ref[i, rows] + diff
        return carry

    lax.fori_loop(0, depth, gather, 0)

    below.wait()
    above.wait()
    source.wait()
    row_states(cells_z, step_ref, curve_ref, left_ref, right_ref, height, first_z, first_z + rows_z)

    def update(z, carry):
        for i, diff in enumerate(differences(pl.multiple_of(first_z + z * height, 8), height, z)):
            total = change_ref[i, pl.ds(pl.multiple_of(z * height, 8), height)] + diff
            if i == 6:
                total = total - source_ref[z]
            flow_ref[i, z] = flow_ref[i, z] + time_step * total
        return carry

    saves = []
    row_faces(left_ref, right_ref, flux_ref, height, first_z - height, height // 32, 2)
    for p in range(parts):
        row_faces(left_ref, right_ref, flux_ref, height, first_z + p * part * height, part * height // 32, 2)
        lax.fori_loop(p * part, (p + 1) * part, update, 0)
        here = pl.ds(p * part, part)
        saves.append(pltpu.make_async_copy(flow_ref.at[:, here], next_out.at[:, here], out_sems.at[p]))
        saves[-1].start()
    for save in saves:
        save.wait()


def serve_kernel(asked_ref, pressure_ref, served_out, served_ref, sems, *, height):
    parts = sems.shape[0]
    sources = asked_ref.shape[0] // parts

    def one(src, carry):
        for r in range(HB):
            row = jnp.maximum(asked_ref[src, r], 0)
            slot = src * HB + r
            served_ref[slot, pl.ds(0, 2), :] = pressure_ref[pl.ds(row, 2), :]
            served_ref[slot, pl.ds(2, 2), :] = pressure_ref[pl.ds(row + height, 2), :]
        return carry

    saves = []
    for p in range(parts):
        lax.fori_loop(p * sources, (p + 1) * sources, one, 0, unroll=4)
        here = pl.ds(p * sources * HB, sources * HB)
        saves.append(pltpu.make_async_copy(served_ref.at[here], served_out.at[here], sems.at[p]))
        saves[-1].start()
    for save in saves:
        save.wait()


def scatter_kernel(asked_ref, returned_ref, source_ref, *sums):
    depth, height, length = source_ref.shape

    def clear(z, carry):
        for total in sums:
            total[pl.ds(pl.multiple_of(z * height, 8), height)] = jnp.zeros((height, length), F32)
        return carry

    lax.fori_loop(0, depth, clear, 0)

    def one(src, carry):
        for r in range(HB):
            total = sums[r % len(sums)]
            row = asked_ref[src, r]
            row = jnp.where(row < 0, depth * height, row)
            pair = src * PAIRS + 2 * r
            near, far = pl.ds(row, 2), pl.ds(row + height, 2)
            total[near] = total[near] + returned_ref[pair]
            total[far] = total[far] + returned_ref[pair + 1]
        return carry

    lax.fori_loop(0, asked_ref.shape[0], one, 0, unroll=4)

    def collect(z, carry):
        rows = pl.ds(pl.multiple_of(z * height, 8), height)
        value = sums[0][rows]
        for total in sums[1:]:
            value = value + total[rows]
        source_ref[z] = value
        return carry

    lax.fori_loop(0, depth, collect, 0)


half_log2e = 0.5 * math.log2(math.e)


def gaussian(distance):
    return jnp.exp2(-half_log2e * (distance * distance))


def across_rows(place_ref, block):
    lateral = lax.broadcasted_iota(jnp.int32, (8, 128), 0) % 4
    shift_z = (lateral // 2).astype(F32) - place_ref[0, pl.ds(block, 1), :]
    shift_y = (lateral % 2).astype(F32) - place_ref[1, pl.ds(block, 1), :]
    return jnp.exp2(-half_log2e * (shift_z * shift_z + shift_y * shift_y))


def across_total(place_ref):
    place_z, place_y = place_ref[0], place_ref[1]
    return (gaussian(place_z) + gaussian(1.0 - place_z)) * (gaussian(place_y) + gaussian(1.0 - place_y))


def deposit_kernel(
    tiles_ref, place_ref, radius_ref, speed_ref, slot_out, out_ref,
    slot_ref, wanted_ref, rate_ref, sem, *, depth, height, across_gy,
):
    length = out_ref.shape[2]
    blocks = radius_ref.shape[0]
    slot, wanted = find_slots(tiles_ref, wanted_ref.shape[0], depth, height, across_gy)
    slot_out[...] = slot
    wanted_ref[...] = wanted
    move = pltpu.make_async_copy(slot_out, slot_ref, sem)
    move.start()
    radius = radius_ref[...]
    rate_ref[...] = 4.0 * math.pi * radius * radius * speed_ref[...] * inverse(across_total(place_ref))
    upper = lax.broadcasted_iota(jnp.int32, (8, 128), 0) < 4

    def ask(k, carry):
        for j in range(8):
            home = k * 8 + j
            out_ref[home * PAIRS + 2 * HB, pl.ds(0, 1), :] = wanted_ref[pl.ds(home, 1), :]
        return carry

    lax.fori_loop(0, wanted_ref.shape[0] // 8, ask, 0)
    move.wait()

    def one(block):
        across = across_rows(place_ref, block)
        offset = place_ref[2, pl.ds(block, 1), :] * float(length - 1)
        along = gaussian(lax.broadcasted_iota(jnp.int32, (length, 128), 0).astype(F32) - offset)
        along_sum = jnp.sum(along, axis=0, keepdims=True)
        share = across * (rate_ref[pl.ds(block, 1), :] * inverse(along_sum))
        along_hi = along.astype(BF16)
        along_lo = (along - along_hi.astype(F32)).astype(BF16)
        share_hi = share.astype(BF16).astype(F32)
        both = jnp.where(upper, share_hi, share - share_hi).astype(BF16)
        only = jnp.where(upper, share_hi, 0.0).astype(BF16)
        result = dot_nt(
            jnp.concatenate([both, only], axis=1), jnp.concatenate([along_hi, along_lo], axis=1)
        )
        result = result[0:4] + result[4:8]
        pair = slot_ref[1, block]
        out_ref[pair] = result[0:2]
        out_ref[pair + 1] = result[2:4]

    size = math.gcd(blocks, 64)

    def several(k, carry):
        for j in range(size):
            one(k * size + j)
        return carry

    lax.fori_loop(0, blocks // size, several, 0)


def sample_kernel(
    slot_ref, place_ref, radius_ref, speed_ref, rest_ref, fetched_in, motion_ref,
    total_ref, width_ref, scale_ref, across_ref, rows_ref, sem,
):
    blocks = radius_ref.shape[0]
    length = rows_ref.shape[2]
    load = pltpu.make_async_copy(fetched_in, rows_ref, sem)
    load.start()
    upper = lax.broadcasted_iota(jnp.int32, (8, 128), 0) < 4

    radius, speed, ratio = radius_ref[...], speed_ref[...], rest_ref[...]
    inv_radius = 1.0 / radius
    gas = (1.0 + 2.0 * surface_tension / (ratio * radius)) * jnp.exp(3.0 * polytropic * jnp.log(ratio))
    wall = gas - (2.0 * surface_tension + 4.0 * liquid_viscosity * speed) * inv_radius
    gas_rate = -3.0 * polytropic * gas * speed * inv_radius
    mach = speed / liquid_sound
    scale = time_step / ((1.0 - mach) * radius)
    motion_ref[0] = radius + time_step * speed
    motion_ref[1] = speed + scale * (
        (1.0 + mach) * (wall - pressure_mid)
        + radius * gas_rate / liquid_sound
        - 1.5 * (1.0 - mach / 3.0) * speed * speed
    )
    scale_ref[...] = scale * (1.0 + mach)
    across_ref[...] = across_total(place_ref)
    load.wait()

    def one(block):
        value = rows_ref[slot_ref[0, block]] - pressure_mid
        value = jnp.concatenate([value, value], axis=0)
        high = value.astype(BF16).astype(F32)
        both = jnp.where(upper, high, value - high)
        both = jnp.concatenate([both, jnp.ones_like(both)], axis=0).astype(BF16)
        offset = place_ref[2, pl.ds(block, 1), :] * float(length - 1)
        along = gaussian(lax.broadcasted_iota(jnp.int32, (length, 128), 0).astype(F32) - offset)
        result = dot_nn(both, along.astype(BF16))
        total_ref[pl.ds(pl.multiple_of(block * 8, 8), 8)] = across_rows(place_ref, block) * result[0:8]
        width_ref[pl.ds(block, 1), :] = result[8:9]

    size = math.gcd(blocks, 64)

    def several(k, carry):
        for j in range(size):
            one(k * size + j)
        return carry

    lax.fori_loop(0, blocks // size, several, 0)
    total = total_ref[pl.ds(0, blocks, stride=8), :]
    for row in range(1, 8):
        total = total + total_ref[pl.ds(row, blocks, stride=8), :]
    motion_ref[1] = motion_ref[1] - scale_ref[...] * (total * inverse(across_ref[...] * width_ref[...]))


def shift_both(low_layers, high_layers, axis):
    count = lax.axis_size(axis)
    below = lax.ppermute(high_layers, axis, [(i, (i + 1) % count) for i in range(count)])
    above = lax.ppermute(low_layers, axis, [((i + 1) % count, i) for i in range(count)])
    return below, above


def exchange(values):
    return lax.all_to_all(values, ("gz", "gy"), split_axis=0, concat_axis=0, tiled=True)


def body(flow_state, block_tiles, bubble_place, bubble_radius, bubble_speed, rest_ratio):
    _, depth, height, length = flow_state.shape
    across_gy = lax.axis_size("gy")
    devices = lax.axis_size("gz") * across_gy
    blocks = block_tiles.shape[0]
    slots = devices * HB
    field = (7, depth, height, length)

    slot, outgoing = pl.pallas_call(
        functools.partial(deposit_kernel, depth=depth, height=height, across_gy=across_gy),
        out_shape=(
            shape((2, blocks), jnp.int32),
            shape((devices * PAIRS, 2, length)),
        ),
        in_specs=[VMEM] * 4,
        out_specs=(VMEM, VMEM),
        scratch_shapes=[
            pltpu.SMEM((2, blocks), jnp.int32),
            pltpu.VMEM((devices, 128), F32),
            pltpu.VMEM((blocks, 128), F32),
            pltpu.SemaphoreType.DMA,
        ],
        compiler_params=params(),
        cost_estimate=cost(10),
        name="deposit",
    )(block_tiles.T, bubble_place, bubble_radius, bubble_speed)
    returned = exchange(outgoing)

    flow_state, _ = lax.optimization_barrier((flow_state, outgoing))
    rows = depth * height
    groups = rows // 128
    turned = 16 + groups * (length + 8) + 80
    change_x, pressure, z_low, z_high, y_low, y_high = pl.pallas_call(
        x_kernel,
        out_shape=(
            shape((7, rows, length)),
            shape((depth, height, length)),
            shape((7, 3 * height, length)),
            shape((7, 3 * height, length)),
            shape((7, 3, depth, length)),
            shape((7, 3, depth, length)),
        ),
        in_specs=[ANY],
        out_specs=(ANY,) + (VMEM,) * 5,
        scratch_shapes=[
            pltpu.VMEM(field, F32),
            pltpu.VMEM((7, rows, length), F32),
            pltpu.VMEM((7, turned, 128), F32),
            pltpu.VMEM((turned, 128), F32),
            pltpu.VMEM((turned, 128), F32),
            pltpu.VMEM((7, turned, 128), F32),
            pltpu.VMEM((7, turned, 128), F32),
            pltpu.VMEM((8, turned, 128), F32),
            pltpu.SemaphoreType.DMA((groups,)),
            pltpu.SemaphoreType.DMA((groups,)),
        ],
        compiler_params=params(56),
        cost_estimate=cost(14),
        name="sweep_x",
    )(flow_state)
    y_below, y_above = shift_both(y_low, y_high, "gy")
    z_below, z_above = shift_both(z_low, z_high, "gz")
    returned, change_x = lax.optimization_barrier((returned, change_x))

    asked = returned.reshape(devices, PAIRS, 2, length)[:, 2 * HB, 0, :HB].astype(jnp.int32)
    served = pl.pallas_call(
        functools.partial(serve_kernel, height=height),
        out_shape=shape((slots, 4, length)),
        in_specs=[SMEM, VMEM],
        out_specs=ANY,
        scratch_shapes=[pltpu.VMEM((slots, 4, length), F32), pltpu.SemaphoreType.DMA((4,))],
        compiler_params=params(56),
        cost_estimate=cost(5),
        name="serve",
    )(asked, pressure.reshape(rows, length))
    fetched = exchange(served)

    returned, asked, change_x, served = lax.optimization_barrier((returned, asked, change_x, served))
    source = pl.pallas_call(
        scatter_kernel,
        out_shape=shape((depth, height, length)),
        in_specs=[SMEM, VMEM],
        out_specs=VMEM,
        scratch_shapes=[pltpu.VMEM(((depth + 2) * height, length), F32)] * 4,
        compiler_params=params(56),
        cost_estimate=cost(6),
        name="scatter",
    )(asked, returned)

    padded = 16 + depth * (height + 8) + 80
    state_next = pl.pallas_call(
        yz_kernel,
        out_shape=shape(field),
        in_specs=[ANY] * 7,
        out_specs=ANY,
        scratch_shapes=[
            pltpu.VMEM((7, 3, depth, length), F32),
            pltpu.VMEM((7, 3, depth, length), F32),
            pltpu.VMEM(field, F32),
            pltpu.VMEM((7, rows, length), F32),
            pltpu.VMEM((depth, height, length), F32),
            pltpu.VMEM((7, rows + 6 * height, length), F32),
            pltpu.VMEM((7, padded, length), F32),
            pltpu.VMEM((padded, length), F32),
            pltpu.VMEM((padded, length), F32),
            pltpu.VMEM((7, padded, length), F32),
            pltpu.VMEM((7, padded, length), F32),
            pltpu.VMEM((8, padded, length), F32),
            pltpu.SemaphoreType.DMA((4,)),
            pltpu.SemaphoreType.DMA((6,)),
            pltpu.SemaphoreType.DMA((4,)),
        ],
        compiler_params=params(),
        cost_estimate=cost(24),
        name="sweep_yz",
    )(flow_state, change_x, source, z_below, z_above, y_below, y_above)

    fetched, state_next = lax.optimization_barrier((fetched, state_next))
    motion = pl.pallas_call(
        sample_kernel,
        out_shape=shape((2, blocks, 128)),
        in_specs=[SMEM] + [VMEM] * 4 + [ANY],
        out_specs=VMEM,
        scratch_shapes=[
            pltpu.VMEM((blocks * 8, 128), F32),
            pltpu.VMEM((blocks, 128), F32),
            pltpu.VMEM((blocks, 128), F32),
            pltpu.VMEM((blocks, 128), F32),
            pltpu.VMEM((slots, 4, length), F32),
            pltpu.SemaphoreType.DMA,
        ],
        compiler_params=params(),
        cost_estimate=cost(7),
        name="sample",
    )(slot, bubble_place, bubble_radius, bubble_speed, rest_ratio, fetched)
    return state_next, source, motion


def solution(mesh):
    in_specs = (
        P(None, "gz", "gy", None),
        P(("gz", "gy"), None),
        P(None, ("gz", "gy"), None),
        P(("gz", "gy"), None),
        P(("gz", "gy"), None),
        P(("gz", "gy"), None),
    )
    out_specs = (P(None, "gz", "gy", None), P("gz", "gy", None), P(None, ("gz", "gy"), None))
    return jax.shard_map(body, mesh=mesh, in_specs=in_specs, out_specs=out_specs, check_vma=False)
```

```python
import functools
import math

import jax
import jax.numpy as jnp
from jax import lax
from jax.experimental import pallas as pl
from jax.experimental.pallas import tpu as pltpu
from jax.sharding import PartitionSpec as P

HB = 8
PAIRS = 2 * HB + 1
gamma_liquid = 4.4
stiff_liquid = 3.0
gamma_gas = 1.4
time_step = 0.08
liquid_sound = 20.0
surface_tension = 0.01
liquid_viscosity = 0.001
polytropic = 1.4
weno_eps = 1e-06
stiff_base = 1.0 / (gamma_gas - 1.0)
stiff_slope = 1.0 / (gamma_liquid - 1.0) - 1.0 / (gamma_gas - 1.0)
offset_slope = gamma_liquid * stiff_liquid / (gamma_liquid - 1.0)
pressure_mid = 0.9

VMEM = pl.BlockSpec(memory_space=pltpu.VMEM)
SMEM = pl.BlockSpec(memory_space=pltpu.SMEM)
ANY = pl.BlockSpec(memory_space=pl.ANY)
F32 = jnp.float32
BF16 = jnp.bfloat16


def params(mib=63.75):
    return pltpu.CompilerParams(vmem_limit_bytes=int(mib * 2**20))


def shape(dims, dtype=F32):
    return jax.ShapeDtypeStruct(dims, dtype)


def cost(microseconds):
    return pl.CostEstimate(flops=int(microseconds * 1.15e9), bytes_accessed=1000, transcendentals=0)


def inverse(value):
    return pl.reciprocal(value, approx=True)


def dot_nt(left, right):
    return lax.dot_general(left, right, (((1,), (1,)), ((), ())), preferred_element_type=F32)


def dot_nn(left, right):
    return lax.dot_general(left, right, (((1,), (0,)), ((), ())), preferred_element_type=F32)


def find_slots(tiles_ref, devices, depth, height, across_gy):
    blocks = tiles_ref.shape[1]
    anchor = tiles_ref[0:1, :].astype(F32)

    def split(value, size):
        whole = jnp.floor((value + 0.5) * (1.0 / size))
        return whole, value - whole * float(size)

    level, column = split(anchor, height * across_gy)
    home_z, level = split(level, depth)
    home_y, column = split(column, height)
    home = (home_z * float(across_gy) + home_y).astype(jnp.int32)
    onehot = lax.broadcasted_iota(jnp.int32, (devices, blocks), 0) == home
    onehot = jnp.where(onehot, 1.0, 0.0).astype(F32)
    onehot_bf = onehot.astype(BF16)
    earlier = lax.broadcasted_iota(jnp.int32, (blocks, blocks), 0) < lax.broadcasted_iota(
        jnp.int32, (blocks, blocks), 1
    )
    earlier = jnp.where(earlier, 1.0, 0.0).astype(BF16)
    before = dot_nn(onehot_bf, earlier)
    rank = jnp.sum(onehot * before, axis=0, keepdims=True)
    rank = jnp.minimum(rank, HB - 1.0)
    rank_int = rank.astype(jnp.int32)
    slot = jnp.concatenate([home * HB + rank_int, home * PAIRS + 2 * rank_int], axis=0)
    chosen = lax.broadcasted_iota(jnp.int32, (128, blocks), 0).astype(F32) == rank
    level = jnp.where(chosen, level + 1.0, 0.0).astype(BF16)
    column = jnp.where(chosen, column, 0.0).astype(BF16)
    level = dot_nt(onehot_bf, level)
    column = dot_nt(onehot_bf, column)
    row = (level - 1.0) * float(height) + column
    return slot, jnp.where(level > 0.0, row, -1.0)


def primitives(value):
    first, second = value[0], value[1]
    density = first + second
    inv_density = inverse(density)
    vel = [value[2 + i] * inv_density for i in range(3)]
    kinetic = 0.5 * (value[2] * vel[0] + value[3] * vel[1] + value[4] * vel[2])
    fraction = value[6]
    stiffness = stiff_base + stiff_slope * fraction
    pressure = (value[5] - kinetic - offset_slope * fraction) * inverse(stiffness)
    return [first, second] + vel + [pressure, fraction]


def weno_pair(cell, dm2, dm1, d0, dp1, zm, z0, zp):
    qm = dm1 + d0
    ql = 3.0 * dm1 - dm2
    qh = dp1 - 3.0 * d0
    tl = zm + ql * ql
    tm = z0 + qm * qm
    th = zp + qh * qh
    tl = tl * tl
    tm = tm * tm
    th = th * th
    low = tm * th
    mid = 6.0 * (tl * th)
    high = tl * tm
    low3 = 3.0 * low
    high3 = 3.0 * high
    den_up = 6.0 * (low + mid + high3)
    den_down = 6.0 * (low3 + mid + high)
    num_up = low * (2.0 * ql - dm1) + mid * (qm + d0) + high3 * (d0 - qh)
    num_down = low3 * (ql + dm1) + mid * (qm + dm1) - high * (2.0 * qh + d0)
    return cell + num_up * inverse(den_up), cell - num_down * inverse(den_down)


def curvature(step):
    return (13.0 / 3.0) * (step * step) + 4.0 * weno_eps


def sound_terms(state):
    density = state[0] + state[1]
    stiff_one = (stiff_base + 1.0) + stiff_slope * state[6]
    enthalpy = state[5] * stiff_one + offset_slope * state[6]
    sound = enthalpy * lax.rsqrt(enthalpy * ((stiff_one - 1.0) * density))
    return density, enthalpy, sound


def hllc(left, right, normal):
    density_l, enthalpy_l, sound_l = sound_terms(left)
    density_r, enthalpy_r, sound_r = sound_terms(right)
    speed_l, speed_r = left[2 + normal], right[2 + normal]
    wave_l = jnp.minimum(speed_l - sound_l, speed_r - sound_r)
    wave_r = jnp.maximum(speed_l + sound_l, speed_r + sound_r)
    mass_l = density_l * (wave_l - speed_l)
    mass_r = density_r * (wave_r - speed_r)
    middle = (right[5] - left[5] + mass_l * speed_l - mass_r * speed_r) * inverse(mass_l - mass_r)
    forward = middle >= 0.0
    use_left = (wave_l >= 0.0) | forward
    one = [jnp.where(use_left, a, b) for a, b in zip(left[:6], right[:6])]
    density = jnp.where(use_left, density_l, density_r)
    enthalpy = jnp.where(use_left, enthalpy_l, enthalpy_r)
    wave = jnp.where(use_left, jnp.minimum(wave_l, 0.0), jnp.maximum(wave_r, 0.0))
    speed, pressure = one[2 + normal], one[5]
    ratio = jnp.where(wave != 0.0, wave * inverse(wave - middle), 0.0)
    extra = ratio * (middle - speed)
    carried = speed + extra
    push = density * (extra * (wave - speed))
    mass = density * carried
    kinetic = 0.5 * density * (one[2] * one[2] + one[3] * one[3] + one[4] * one[4])
    flux = [one[0] * carried, one[1] * carried]
    for i in range(3):
        flow = mass * one[2 + i]
        flux.append(flow + (push + pressure) if i == normal else flow)
    flux.append((enthalpy + kinetic) * carried + push * middle)
    flux.append(middle * jnp.where(forward, left[6], right[6]))
    return flux, middle


def x_kernel(
    flow_in, change_out, pressure_ref, z_low_ref, z_high_ref, y_low_ref, y_high_ref,
    flow_ref, prim_ref, cells_ref, step_ref, curve_ref, left_ref, right_ref, flux_ref, load_sems, save_sems,
):
    depth, height, length = flow_ref.shape[1:]
    groups = load_sems.shape[0]
    slabs = depth // groups
    width = slabs * height
    pitch = length + 8
    first = 16
    loads = []
    for g in range(groups):
        here = pl.ds(g * slabs, slabs)
        loads.append(pltpu.make_async_copy(flow_in.at[:, here], flow_ref.at[:, here], load_sems.at[g]))
        loads[-1].start()

    def slab(z, carry):
        rows = pl.ds(pl.multiple_of(z * height, 8), height)
        values = primitives([flow_ref[i, z] for i in range(7)])
        pressure_ref[z] = values[5]
        for i, value in enumerate(values):
            prim_ref[i, rows] = value
            for j in range(3):
                y_low_ref[i, j, pl.ds(z, 1), :] = value[j : j + 1]
                y_high_ref[i, j, pl.ds(z, 1), :] = value[height - 3 + j : height - 2 + j]
        return carry

    for g in range(groups):
        loads[g].wait()
        lax.fori_loop(g * slabs, (g + 1) * slabs, slab, 0)
        base = first + g * pitch
        for i in range(7):
            tile = prim_ref[i, pl.ds(g * width, width)].T
            cells_ref[i, pl.ds(base, length)] = tile
            cells_ref[i, pl.ds(base - 3, 3)] = tile[length - 3 :]
            cells_ref[i, pl.ds(base + length, 3)] = tile[:3]
    for i in range(7):
        z_low_ref[i] = prim_ref[i, pl.ds(0, 3 * height)]
        z_high_ref[i] = prim_ref[i, pl.ds((depth - 3) * height, 3 * height)]

    last = first + groups * pitch
    row_states(cells_ref, step_ref, curve_ref, left_ref, right_ref, 1, first, last)
    row_faces(left_ref, right_ref, flux_ref, 1, first - 8, -(-(last - first + 8) // 32), 0)

    saves = []
    for g in range(groups):
        here, under = pl.ds(first + g * pitch, length), pl.ds(first + g * pitch - 1, length)
        out = pl.ds(g * width, width)
        for i in range(7):
            diff = flux_ref[i, under] - flux_ref[i, here]
            if i == 6:
                diff = diff + cells_ref[6, here] * (flux_ref[7, here] - flux_ref[7, under])
            prim_ref[i, out] = diff.T
        saves.append(pltpu.make_async_copy(prim_ref.at[:, out], change_out.at[:, out], save_sems.at[g]))
        saves[-1].start()
    for save in saves:
        save.wait()


def row_states(cells_ref, step_ref, curve_ref, left_ref, right_ref, stride, first, last):
    size = 64
    reach = -(-stride // 8) * 8

    def loop(begin, end, step):
        count = -(-(end - begin) // size)
        lax.fori_loop(0, count, lambda k, c: step(pl.multiple_of(begin + k * size, 8), c), 0, unroll=4)

    for i in range(7):

        def prepare(row, carry, i=i):
            mid = cells_ref[i, pl.ds(row, size)]
            d0 = cells_ref[i, pl.ds(row + stride, size)] - mid
            dm1 = mid - cells_ref[i, pl.ds(row - stride, size)]
            step_ref[pl.ds(row, size)] = d0
            curve_ref[pl.ds(row, size)] = curvature(d0 - dm1)
            return carry

        if stride == reach:
            edge = pl.ds(first - 3 * stride, size)
            step_ref[edge] = cells_ref[i, pl.ds(first - 2 * stride, size)] - cells_ref[i, edge]
            loop(first - 2 * stride, last + 2 * stride, prepare)
        else:
            loop(first - reach, last + 2 * stride, prepare)

        def states(row, carry, i=i):
            def take(ref, shift):
                return ref[pl.ds(row + shift * stride, size)]

            up, down = weno_pair(
                cells_ref[i, pl.ds(row, size)],
                take(step_ref, -2), take(step_ref, -1), take(step_ref, 0), take(step_ref, 1),
                take(curve_ref, -1), take(curve_ref, 0), take(curve_ref, 1),
            )
            left_ref[i, pl.ds(row, size)] = up
            right_ref[i, pl.ds(row, size)] = down
            return carry

        loop(first - reach, last + stride, states)


def row_faces(left_ref, right_ref, flux_ref, stride, begin, count, normal):
    size = 32

    def faces(k, carry):
        row = pl.multiple_of(begin + k * size, 8)
        left = [left_ref[i, pl.ds(row, size)] for i in range(7)]
        right = [right_ref[i, pl.ds(row + stride, size)] for i in range(7)]
        flux, middle = hllc(left, right, normal)
        for i in range(7):
            flux_ref[i, pl.ds(row, size)] = flux[i]
        flux_ref[7, pl.ds(row, size)] = middle
        return carry

    lax.fori_loop(0, count, faces, 0, unroll=2)


def yz_kernel(
    flow_in, change_in, source_in, z_below_in, z_above_in, y_below_in, y_above_in, next_out,
    y_below_ref, y_above_ref, flow_ref, change_ref, source_ref, cells_z, cells_y, step_ref, curve_ref, left_ref, right_ref, flux_ref,
    flow_sems, side_sems, out_sems,
):
    depth, height = flow_ref.shape[1:3]
    parts = flow_sems.shape[0]
    part = depth // parts
    pitch = height + 8
    first_y = 16
    first_z = 3 * height
    rows_z = depth * height
    loads = []
    for p in range(parts):
        here = pl.ds(p * part, part)
        loads.append(pltpu.make_async_copy(flow_in.at[:, here], flow_ref.at[:, here], flow_sems.at[p]))
    below = pltpu.make_async_copy(z_below_in, cells_z.at[:, pl.ds(0, first_z)], side_sems.at[0])
    above = pltpu.make_async_copy(z_above_in, cells_z.at[:, pl.ds(first_z + rows_z, first_z)], side_sems.at[1])
    change = pltpu.make_async_copy(change_in, change_ref, side_sems.at[2])
    source = pltpu.make_async_copy(source_in, source_ref, side_sems.at[3])
    y_below = pltpu.make_async_copy(y_below_in, y_below_ref, side_sems.at[4])
    y_above = pltpu.make_async_copy(y_above_in, y_above_ref, side_sems.at[5])
    for copy in [y_below, y_above] + loads + [below, above, change, source]:
        copy.start()
    y_below.wait()
    y_above.wait()

    def fill(z, carry):
        base = pl.multiple_of(first_y + z * pitch, 8)
        values = primitives([flow_ref[i, z] for i in range(7)])
        for i, value in enumerate(values):
            cells_z[i, pl.ds(pl.multiple_of(first_z + z * height, 8), height)] = value
            cells_y[i, pl.ds(base, height)] = value
            for j in range(3):
                cells_y[i, pl.ds(base - 3 + j, 1)] = y_below_ref[i, j, pl.ds(z, 1), :]
                cells_y[i, pl.ds(base + height + j, 1)] = y_above_ref[i, j, pl.ds(z, 1), :]
        return carry

    for p in range(parts):
        loads[p].wait()
        lax.fori_loop(p * part, (p + 1) * part, fill, 0)

    last_y = first_y + depth * pitch
    row_states(cells_y, step_ref, curve_ref, left_ref, right_ref, 1, first_y, last_y)
    row_faces(left_ref, right_ref, flux_ref, 1, first_y - 8, -(-(last_y - first_y + 8) // 32), 1)
    change.wait()

    def differences(base, lower, z):
        here, under = pl.ds(base, height), pl.ds(base - lower, height)
        diff = [flux_ref[i, under] - flux_ref[i, here] for i in range(7)]
        fraction = cells_z[6, pl.ds(pl.multiple_of(first_z + z * height, 8), height)]
        diff[6] = diff[6] + fraction * (flux_ref[7, here] - flux_ref[7, under])
        return diff

    def gather(z, carry):
        for i, diff in enumerate(differences(pl.multiple_of(first_y + z * pitch, 8), 1, z)):
            rows = pl.ds(pl.multiple_of(z * height, 8), height)
            change_ref[i, rows] = change_ref[i, rows] + diff
        return carry

    lax.fori_loop(0, depth, gather, 0)

    below.wait()
    above.wait()
    source.wait()
    row_states(cells_z, step_ref, curve_ref, left_ref, right_ref, height, first_z, first_z + rows_z)

    def update(z, carry):
        for i, diff in enumerate(differences(pl.multiple_of(first_z + z * height, 8), height, z)):
            total = change_ref[i, pl.ds(pl.multiple_of(z * height, 8), height)] + diff
            if i == 6:
                total = total - source_ref[z]
            flow_ref[i, z] = flow_ref[i, z] + time_step * total
        return carry

    saves = []
    row_faces(left_ref, right_ref, flux_ref, height, first_z - height, height // 32, 2)
    for p in range(parts):
        row_faces(left_ref, right_ref, flux_ref, height, first_z + p * part * height, part * height // 32, 2)
        lax.fori_loop(p * part, (p + 1) * part, update, 0)
        here = pl.ds(p * part, part)
        saves.append(pltpu.make_async_copy(flow_ref.at[:, here], next_out.at[:, here], out_sems.at[p]))
        saves[-1].start()
    for save in saves:
        save.wait()


def serve_kernel(asked_ref, pressure_ref, served_out, served_ref, sems, *, height):
    parts = sems.shape[0]
    sources = asked_ref.shape[0] // parts

    def one(src, carry):
        for r in range(HB):
            row = jnp.maximum(asked_ref[src, r], 0)
            slot = src * HB + r
            served_ref[slot, pl.ds(0, 2), :] = pressure_ref[pl.ds(row, 2), :]
            served_ref[slot, pl.ds(2, 2), :] = pressure_ref[pl.ds(row + height, 2), :]
        return carry

    saves = []
    for p in range(parts):
        lax.fori_loop(p * sources, (p + 1) * sources, one, 0, unroll=4)
        here = pl.ds(p * sources * HB, sources * HB)
        saves.append(pltpu.make_async_copy(served_ref.at[here], served_out.at[here], sems.at[p]))
        saves[-1].start()
    for save in saves:
        save.wait()


def scatter_kernel(asked_ref, returned_ref, source_ref, *sums):
    depth, height, length = source_ref.shape

    def clear(z, carry):
        for total in sums:
            total[pl.ds(pl.multiple_of(z * height, 8), height)] = jnp.zeros((height, length), F32)
        return carry

    lax.fori_loop(0, depth, clear, 0)

    def one(src, carry):
        for r in range(HB):
            total = sums[r % len(sums)]
            row = asked_ref[src, r]
            row = jnp.where(row < 0, depth * height, row)
            pair = src * PAIRS + 2 * r
            near, far = pl.ds(row, 2), pl.ds(row + height, 2)
            total[near] = total[near] + returned_ref[pair]
            total[far] = total[far] + returned_ref[pair + 1]
        return carry

    lax.fori_loop(0, asked_ref.shape[0], one, 0, unroll=4)

    def collect(z, carry):
        rows = pl.ds(pl.multiple_of(z * height, 8), height)
        value = sums[0][rows]
        for total in sums[1:]:
            value = value + total[rows]
        source_ref[z] = value
        return carry

    lax.fori_loop(0, depth, collect, 0)


half_log2e = 0.5 * math.log2(math.e)


def gaussian(distance):
    return jnp.exp2(-half_log2e * (distance * distance))


def across_rows(place_ref, block):
    lateral = lax.broadcasted_iota(jnp.int32, (8, 128), 0) % 4
    shift_z = (lateral // 2).astype(F32) - place_ref[0, pl.ds(block, 1), :]
    shift_y = (lateral % 2).astype(F32) - place_ref[1, pl.ds(block, 1), :]
    return jnp.exp2(-half_log2e * (shift_z * shift_z + shift_y * shift_y))


def across_total(place_ref):
    place_z, place_y = place_ref[0], place_ref[1]
    return (gaussian(place_z) + gaussian(1.0 - place_z)) * (gaussian(place_y) + gaussian(1.0 - place_y))


def deposit_kernel(
    tiles_ref, place_ref, radius_ref, speed_ref, slot_out, out_ref,
    slot_ref, wanted_ref, rate_ref, sem, *, depth, height, across_gy,
):
    length = out_ref.shape[2]
    blocks = radius_ref.shape[0]
    slot, wanted = find_slots(tiles_ref, wanted_ref.shape[0], depth, height, across_gy)
    slot_out[...] = slot
    wanted_ref[...] = wanted
    move = pltpu.make_async_copy(slot_out, slot_ref, sem)
    move.start()
    radius = radius_ref[...]
    rate_ref[...] = 4.0 * math.pi * radius * radius * speed_ref[...] * inverse(across_total(place_ref))
    upper = lax.broadcasted_iota(jnp.int32, (8, 128), 0) < 4

    def ask(k, carry):
        for j in range(8):
            home = k * 8 + j
            out_ref[home * PAIRS + 2 * HB, pl.ds(0, 1), :] = wanted_ref[pl.ds(home, 1), :]
        return carry

    lax.fori_loop(0, wanted_ref.shape[0] // 8, ask, 0)
    move.wait()

    def one(block):
        across = across_rows(place_ref, block)
        offset = place_ref[2, pl.ds(block, 1), :] * float(length - 1)
        along = gaussian(lax.broadcasted_iota(jnp.int32, (length, 128), 0).astype(F32) - offset)
        along_sum = jnp.sum(along, axis=0, keepdims=True)
        share = across * (rate_ref[pl.ds(block, 1), :] * inverse(along_sum))
        along_hi = along.astype(BF16)
        along_lo = (along - along_hi.astype(F32)).astype(BF16)
        share_hi = share.astype(BF16).astype(F32)
        both = jnp.where(upper, share_hi, share - share_hi).astype(BF16)
        only = jnp.where(upper, share_hi, 0.0).astype(BF16)
        result = dot_nt(
            jnp.concatenate([both, only], axis=1), jnp.concatenate([along_hi, along_lo], axis=1)
        )
        result = result[0:4] + result[4:8]
        pair = slot_ref[1, block]
        out_ref[pair] = result[0:2]
        out_ref[pair + 1] = result[2:4]

    size = math.gcd(blocks, 64)

    def several(k, carry):
        for j in range(size):
            one(k * size + j)
        return carry

    lax.fori_loop(0, blocks // size, several, 0)


def ready_kernel(place_ref, radius_ref, speed_ref, rest_ref, ready_ref):
    radius, speed, ratio = radius_ref[...], speed_ref[...], rest_ref[...]
    inv_radius = 1.0 / radius
    gas = (1.0 + 2.0 * surface_tension / (ratio * radius)) * jnp.exp(3.0 * polytropic * jnp.log(ratio))
    wall = gas - (2.0 * surface_tension + 4.0 * liquid_viscosity * speed) * inv_radius
    gas_rate = -3.0 * polytropic * gas * speed * inv_radius
    mach = speed / liquid_sound
    scale = time_step / ((1.0 - mach) * radius)
    ready_ref[0] = radius + time_step * speed
    ready_ref[1] = speed + scale * (
        (1.0 + mach) * (wall - pressure_mid)
        + radius * gas_rate / liquid_sound
        - 1.5 * (1.0 - mach / 3.0) * speed * speed
    )
    ready_ref[2] = scale * (1.0 + mach) * inverse(across_total(place_ref))


def sample_kernel(slot_ref, place_ref, ready_ref, rows_ref, motion_ref, total_ref, width_ref):
    blocks = width_ref.shape[0]
    length = rows_ref.shape[2]
    upper = lax.broadcasted_iota(jnp.int32, (8, 128), 0) < 4
    motion_ref[0] = ready_ref[0]

    def one(block):
        value = rows_ref[slot_ref[0, block]] - pressure_mid
        value = jnp.concatenate([value, value], axis=0)
        high = value.astype(BF16).astype(F32)
        both = jnp.where(upper, high, value - high)
        both = jnp.concatenate([both, jnp.ones_like(both)], axis=0).astype(BF16)
        offset = place_ref[2, pl.ds(block, 1), :] * float(length - 1)
        along = gaussian(lax.broadcasted_iota(jnp.int32, (length, 128), 0).astype(F32) - offset)
        result = dot_nn(both, along.astype(BF16))
        total_ref[pl.ds(pl.multiple_of(block * 8, 8), 8)] = across_rows(place_ref, block) * result[0:8]
        width_ref[pl.ds(block, 1), :] = result[8:9]

    size = math.gcd(blocks, 64)

    def several(k, carry):
        for j in range(size):
            one(k * size + j)
        return carry

    lax.fori_loop(0, blocks // size, several, 0)
    total = total_ref[pl.ds(0, blocks, stride=8), :]
    for row in range(1, 8):
        total = total + total_ref[pl.ds(row, blocks, stride=8), :]
    motion_ref[1] = ready_ref[1] - ready_ref[2] * (total * inverse(width_ref[...]))


def shift_both(low_layers, high_layers, axis):
    count = lax.axis_size(axis)
    below = lax.ppermute(high_layers, axis, [(i, (i + 1) % count) for i in range(count)])
    above = lax.ppermute(low_layers, axis, [((i + 1) % count, i) for i in range(count)])
    return below, above


def exchange(values):
    return lax.all_to_all(values, ("gz", "gy"), split_axis=0, concat_axis=0, tiled=True)


def body(flow_state, block_tiles, bubble_place, bubble_radius, bubble_speed, rest_ratio):
    _, depth, height, length = flow_state.shape
    across_gy = lax.axis_size("gy")
    devices = lax.axis_size("gz") * across_gy
    blocks = block_tiles.shape[0]
    slots = devices * HB
    field = (7, depth, height, length)

    slot, outgoing = pl.pallas_call(
        functools.partial(deposit_kernel, depth=depth, height=height, across_gy=across_gy),
        out_shape=(
            shape((2, blocks), jnp.int32),
            shape((devices * PAIRS, 2, length)),
        ),
        in_specs=[VMEM] * 4,
        out_specs=(VMEM, VMEM),
        scratch_shapes=[
            pltpu.SMEM((2, blocks), jnp.int32),
            pltpu.VMEM((devices, 128), F32),
            pltpu.VMEM((blocks, 128), F32),
            pltpu.SemaphoreType.DMA,
        ],
        compiler_params=params(),
        cost_estimate=cost(10),
        name="deposit",
    )(block_tiles.T, bubble_place, bubble_radius, bubble_speed)
    returned = exchange(outgoing)

    flow_state, rest_ratio, _ = lax.optimization_barrier((flow_state, rest_ratio, outgoing))
    rows = depth * height
    groups = rows // 128
    turned = 16 + groups * (length + 8) + 80
    change_x, pressure, z_low, z_high, y_low, y_high = pl.pallas_call(
        x_kernel,
        out_shape=(
            shape((7, rows, length)),
            shape((depth, height, length)),
            shape((7, 3 * height, length)),
            shape((7, 3 * height, length)),
            shape((7, 3, depth, length)),
            shape((7, 3, depth, length)),
        ),
        in_specs=[ANY],
        out_specs=(ANY,) + (VMEM,) * 5,
        scratch_shapes=[
            pltpu.VMEM(field, F32),
            pltpu.VMEM((7, rows, length), F32),
            pltpu.VMEM((7, turned, 128), F32),
            pltpu.VMEM((turned, 128), F32),
            pltpu.VMEM((turned, 128), F32),
            pltpu.VMEM((7, turned, 128), F32),
            pltpu.VMEM((7, turned, 128), F32),
            pltpu.VMEM((8, turned, 128), F32),
            pltpu.SemaphoreType.DMA((groups,)),
            pltpu.SemaphoreType.DMA((groups,)),
        ],
        compiler_params=params(56),
        cost_estimate=cost(14),
        name="sweep_x",
    )(flow_state)
    y_below, y_above = shift_both(y_low, y_high, "gy")
    z_below, z_above = shift_both(z_low, z_high, "gz")
    ready = pl.pallas_call(
        ready_kernel,
        out_shape=shape((3, blocks, 128)),
        in_specs=[VMEM] * 4,
        out_specs=VMEM,
        compiler_params=params(56),
        cost_estimate=cost(2),
        name="ready",
    )(bubble_place, bubble_radius, bubble_speed, rest_ratio)
    returned, change_x, ready = lax.optimization_barrier((returned, change_x, ready))

    asked = returned.reshape(devices, PAIRS, 2, length)[:, 2 * HB, 0, :HB].astype(jnp.int32)
    served = pl.pallas_call(
        functools.partial(serve_kernel, height=height),
        out_shape=shape((slots, 4, length)),
        in_specs=[SMEM, VMEM],
        out_specs=ANY,
        scratch_shapes=[pltpu.VMEM((slots, 4, length), F32), pltpu.SemaphoreType.DMA((4,))],
        compiler_params=params(56),
        cost_estimate=cost(5),
        name="serve",
    )(asked, pressure.reshape(rows, length))
    fetched = exchange(served)

    returned, asked, change_x, served = lax.optimization_barrier((returned, asked, change_x, served))
    source = pl.pallas_call(
        scatter_kernel,
        out_shape=shape((depth, height, length)),
        in_specs=[SMEM, VMEM],
        out_specs=VMEM,
        scratch_shapes=[pltpu.VMEM(((depth + 2) * height, length), F32)] * 4,
        compiler_params=params(56),
        cost_estimate=cost(6),
        name="scatter",
    )(asked, returned)

    padded = 16 + depth * (height + 8) + 80
    state_next = pl.pallas_call(
        yz_kernel,
        out_shape=shape(field),
        in_specs=[ANY] * 7,
        out_specs=ANY,
        scratch_shapes=[
            pltpu.VMEM((7, 3, depth, length), F32),
            pltpu.VMEM((7, 3, depth, length), F32),
            pltpu.VMEM(field, F32),
            pltpu.VMEM((7, rows, length), F32),
            pltpu.VMEM((depth, height, length), F32),
            pltpu.VMEM((7, rows + 6 * height, length), F32),
            pltpu.VMEM((7, padded, length), F32),
            pltpu.VMEM((padded, length), F32),
            pltpu.VMEM((padded, length), F32),
            pltpu.VMEM((7, padded, length), F32),
            pltpu.VMEM((7, padded, length), F32),
            pltpu.VMEM((8, padded, length), F32),
            pltpu.SemaphoreType.DMA((4,)),
            pltpu.SemaphoreType.DMA((6,)),
            pltpu.SemaphoreType.DMA((4,)),
        ],
        compiler_params=params(),
        cost_estimate=cost(24),
        name="sweep_yz",
    )(flow_state, change_x, source, z_below, z_above, y_below, y_above)

    fetched, state_next = lax.optimization_barrier((fetched, state_next))
    motion = pl.pallas_call(
        sample_kernel,
        out_shape=shape((2, blocks, 128)),
        in_specs=[SMEM] + [VMEM] * 3,
        out_specs=VMEM,
        scratch_shapes=[pltpu.VMEM((blocks * 8, 128), F32), pltpu.VMEM((blocks, 128), F32)],
        compiler_params=params(),
        cost_estimate=cost(7),
        name="sample",
    )(slot, bubble_place, ready, fetched)
    return state_next, source, motion


def solution(mesh):
    in_specs = (
        P(None, "gz", "gy", None),
        P(("gz", "gy"), None),
        P(None, ("gz", "gy"), None),
        P(("gz", "gy"), None),
        P(("gz", "gy"), None),
        P(("gz", "gy"), None),
    )
    out_specs = (P(None, "gz", "gy", None), P("gz", "gy", None), P(None, ("gz", "gy"), None))
    return jax.shard_map(body, mesh=mesh, in_specs=in_specs, out_specs=out_specs, check_vma=False)
```

```python
import functools
import math

import jax
import jax.numpy as jnp
from jax import lax
from jax.experimental import pallas as pl
from jax.experimental.pallas import tpu as pltpu
from jax.sharding import PartitionSpec as P

HB = 8
PAIRS = 2 * HB + 1
gamma_liquid = 4.4
stiff_liquid = 3.0
gamma_gas = 1.4
time_step = 0.08
liquid_sound = 20.0
surface_tension = 0.01
liquid_viscosity = 0.001
polytropic = 1.4
weno_eps = 1e-06
stiff_base = 1.0 / (gamma_gas - 1.0)
stiff_slope = 1.0 / (gamma_liquid - 1.0) - 1.0 / (gamma_gas - 1.0)
offset_slope = gamma_liquid * stiff_liquid / (gamma_liquid - 1.0)
pressure_mid = 0.9

VMEM = pl.BlockSpec(memory_space=pltpu.VMEM)
SMEM = pl.BlockSpec(memory_space=pltpu.SMEM)
ANY = pl.BlockSpec(memory_space=pl.ANY)
F32 = jnp.float32
BF16 = jnp.bfloat16


def params(mib=63.75):
    return pltpu.CompilerParams(vmem_limit_bytes=int(mib * 2**20))


def shape(dims, dtype=F32):
    return jax.ShapeDtypeStruct(dims, dtype)


def cost(microseconds):
    return pl.CostEstimate(flops=int(microseconds * 1.15e9), bytes_accessed=1000, transcendentals=0)


def inverse(value):
    return pl.reciprocal(value, approx=True)


def dot_nt(left, right):
    return lax.dot_general(left, right, (((1,), (1,)), ((), ())), preferred_element_type=F32)


def dot_nn(left, right):
    return lax.dot_general(left, right, (((1,), (0,)), ((), ())), preferred_element_type=F32)


def find_slots(tiles_ref, devices, depth, height, across_gy):
    blocks = tiles_ref.shape[1]
    anchor = tiles_ref[0:1, :].astype(F32)

    def split(value, size):
        whole = jnp.floor((value + 0.5) * (1.0 / size))
        return whole, value - whole * float(size)

    level, column = split(anchor, height * across_gy)
    home_z, level = split(level, depth)
    home_y, column = split(column, height)
    home = (home_z * float(across_gy) + home_y).astype(jnp.int32)
    onehot = lax.broadcasted_iota(jnp.int32, (devices, blocks), 0) == home
    onehot = jnp.where(onehot, 1.0, 0.0).astype(F32)
    onehot_bf = onehot.astype(BF16)
    earlier = lax.broadcasted_iota(jnp.int32, (blocks, blocks), 0) < lax.broadcasted_iota(
        jnp.int32, (blocks, blocks), 1
    )
    earlier = jnp.where(earlier, 1.0, 0.0).astype(BF16)
    before = dot_nn(onehot_bf, earlier)
    rank = jnp.sum(onehot * before, axis=0, keepdims=True)
    rank = jnp.minimum(rank, HB - 1.0)
    rank_int = rank.astype(jnp.int32)
    slot = jnp.concatenate([home * HB + rank_int, home * PAIRS + 2 * rank_int], axis=0)
    chosen = lax.broadcasted_iota(jnp.int32, (128, blocks), 0).astype(F32) == rank
    level = jnp.where(chosen, level + 1.0, 0.0).astype(BF16)
    column = jnp.where(chosen, column, 0.0).astype(BF16)
    level = dot_nt(onehot_bf, level)
    column = dot_nt(onehot_bf, column)
    row = (level - 1.0) * float(height) + column
    return slot, jnp.where(level > 0.0, row, -1.0)


def primitives(value):
    first, second = value[0], value[1]
    density = first + second
    inv_density = inverse(density)
    vel = [value[2 + i] * inv_density for i in range(3)]
    kinetic = 0.5 * (value[2] * vel[0] + value[3] * vel[1] + value[4] * vel[2])
    fraction = value[6]
    stiffness = stiff_base + stiff_slope * fraction
    pressure = (value[5] - kinetic - offset_slope * fraction) * inverse(stiffness)
    return [first, second] + vel + [pressure, fraction]


def weno_pair(cell, dm2, dm1, d0, dp1, zm, z0, zp):
    qm = dm1 + d0
    ql = 3.0 * dm1 - dm2
    qh = dp1 - 3.0 * d0
    tl = zm + ql * ql
    tm = z0 + qm * qm
    th = zp + qh * qh
    tl = tl * tl
    tm = tm * tm
    th = th * th
    low = tm * th
    mid = 6.0 * (tl * th)
    high = tl * tm
    low3 = 3.0 * low
    high3 = 3.0 * high
    den_up = 6.0 * (low + mid + high3)
    den_down = 6.0 * (low3 + mid + high)
    num_up = low * (2.0 * ql - dm1) + mid * (qm + d0) + high3 * (d0 - qh)
    num_down = low3 * (ql + dm1) + mid * (qm + dm1) - high * (2.0 * qh + d0)
    return cell + num_up * inverse(den_up), cell - num_down * inverse(den_down)


def curvature(step):
    return (13.0 / 3.0) * (step * step) + 4.0 * weno_eps


def sound_terms(state):
    density = state[0] + state[1]
    stiff_one = (stiff_base + 1.0) + stiff_slope * state[6]
    enthalpy = state[5] * stiff_one + offset_slope * state[6]
    sound = enthalpy * lax.rsqrt(enthalpy * ((stiff_one - 1.0) * density))
    return density, enthalpy, sound


def hllc(left, right, normal):
    density_l, enthalpy_l, sound_l = sound_terms(left)
    density_r, enthalpy_r, sound_r = sound_terms(right)
    speed_l, speed_r = left[2 + normal], right[2 + normal]
    wave_l = jnp.minimum(speed_l - sound_l, speed_r - sound_r)
    wave_r = jnp.maximum(speed_l + sound_l, speed_r + sound_r)
    mass_l = density_l * (wave_l - speed_l)
    mass_r = density_r * (wave_r - speed_r)
    middle = (right[5] - left[5] + mass_l * speed_l - mass_r * speed_r) * inverse(mass_l - mass_r)
    forward = middle >= 0.0
    use_left = (wave_l >= 0.0) | forward
    one = [jnp.where(use_left, a, b) for a, b in zip(left[:6], right[:6])]
    density = jnp.where(use_left, density_l, density_r)
    enthalpy = jnp.where(use_left, enthalpy_l, enthalpy_r)
    wave = jnp.where(use_left, jnp.minimum(wave_l, 0.0), jnp.maximum(wave_r, 0.0))
    speed, pressure = one[2 + normal], one[5]
    ratio = jnp.where(wave != 0.0, wave * inverse(wave - middle), 0.0)
    extra = ratio * (middle - speed)
    carried = speed + extra
    push = density * (extra * (wave - speed))
    mass = density * carried
    kinetic = 0.5 * density * (one[2] * one[2] + one[3] * one[3] + one[4] * one[4])
    flux = [one[0] * carried, one[1] * carried]
    for i in range(3):
        flow = mass * one[2 + i]
        flux.append(flow + (push + pressure) if i == normal else flow)
    flux.append((enthalpy + kinetic) * carried + push * middle)
    flux.append(middle * jnp.where(forward, left[6], right[6]))
    return flux, middle


def x_kernel(
    flow_in, change_out, pressure_ref, z_low_ref, z_high_ref, y_low_ref, y_high_ref,
    flow_ref, prim_ref, cells_ref, step_ref, curve_ref, left_ref, right_ref, flux_ref, load_sems, save_sems,
):
    depth, height, length = flow_ref.shape[1:]
    groups = load_sems.shape[0]
    slabs = depth // groups
    width = slabs * height
    pitch = length + 8
    first = 16
    loads = []
    for g in range(groups):
        here = pl.ds(g * slabs, slabs)
        loads.append(pltpu.make_async_copy(flow_in.at[:, here], flow_ref.at[:, here], load_sems.at[g]))
        loads[-1].start()

    def slab(z, carry):
        rows = pl.ds(pl.multiple_of(z * height, 8), height)
        values = primitives([flow_ref[i, z] for i in range(7)])
        pressure_ref[z] = values[5]
        for i, value in enumerate(values):
            prim_ref[i, rows] = value
            for j in range(3):
                y_low_ref[i, j, pl.ds(z, 1), :] = value[j : j + 1]
                y_high_ref[i, j, pl.ds(z, 1), :] = value[height - 3 + j : height - 2 + j]
        return carry

    for g in range(groups):
        loads[g].wait()
        lax.fori_loop(g * slabs, (g + 1) * slabs, slab, 0)
        base = first + g * pitch
        for i in range(7):
            tile = prim_ref[i, pl.ds(g * width, width)].T
            cells_ref[i, pl.ds(base, length)] = tile
            cells_ref[i, pl.ds(base - 3, 3)] = tile[length - 3 :]
            cells_ref[i, pl.ds(base + length, 3)] = tile[:3]
    for i in range(7):
        z_low_ref[i] = prim_ref[i, pl.ds(0, 3 * height)]
        z_high_ref[i] = prim_ref[i, pl.ds((depth - 3) * height, 3 * height)]

    last = first + groups * pitch
    row_states(cells_ref, step_ref, curve_ref, left_ref, right_ref, 1, first, last)
    row_faces(left_ref, right_ref, flux_ref, 1, first - 8, -(-(last - first + 8) // 32), 0)

    saves = []
    for g in range(groups):
        here, under = pl.ds(first + g * pitch, length), pl.ds(first + g * pitch - 1, length)
        out = pl.ds(g * width, width)
        for i in range(7):
            diff = flux_ref[i, under] - flux_ref[i, here]
            if i == 6:
                diff = diff + cells_ref[6, here] * (flux_ref[7, here] - flux_ref[7, under])
            prim_ref[i, out] = diff.T
        saves.append(pltpu.make_async_copy(prim_ref.at[:, out], change_out.at[:, out], save_sems.at[g]))
        saves[-1].start()
    for save in saves:
        save.wait()


def row_states(cells_ref, step_ref, curve_ref, left_ref, right_ref, stride, first, last):
    size = 64
    reach = -(-stride // 8) * 8

    def loop(begin, end, step):
        count = -(-(end - begin) // size)
        lax.fori_loop(0, count, lambda k, c: step(pl.multiple_of(begin + k * size, 8), c), 0, unroll=4)

    for i in range(7):

        def prepare(row, carry, i=i):
            mid = cells_ref[i, pl.ds(row, size)]
            d0 = cells_ref[i, pl.ds(row + stride, size)] - mid
            dm1 = mid - cells_ref[i, pl.ds(row - stride, size)]
            step_ref[pl.ds(row, size)] = d0
            curve_ref[pl.ds(row, size)] = curvature(d0 - dm1)
            return carry

        if stride == reach:
            edge = pl.ds(first - 3 * stride, size)
            step_ref[edge] = cells_ref[i, pl.ds(first - 2 * stride, size)] - cells_ref[i, edge]
            loop(first - 2 * stride, last + 2 * stride, prepare)
        else:
            loop(first - reach, last + 2 * stride, prepare)

        def states(row, carry, i=i):
            def take(ref, shift):
                return ref[pl.ds(row + shift * stride, size)]

            up, down = weno_pair(
                cells_ref[i, pl.ds(row, size)],
                take(step_ref, -2), take(step_ref, -1), take(step_ref, 0), take(step_ref, 1),
                take(curve_ref, -1), take(curve_ref, 0), take(curve_ref, 1),
            )
            left_ref[i, pl.ds(row, size)] = up
            right_ref[i, pl.ds(row, size)] = down
            return carry

        loop(first - reach, last + stride, states)


def row_faces(left_ref, right_ref, flux_ref, stride, begin, count, normal):
    size = 32

    def faces(k, carry):
        row = pl.multiple_of(begin + k * size, 8)
        left = [left_ref[i, pl.ds(row, size)] for i in range(7)]
        right = [right_ref[i, pl.ds(row + stride, size)] for i in range(7)]
        flux, middle = hllc(left, right, normal)
        for i in range(7):
            flux_ref[i, pl.ds(row, size)] = flux[i]
        flux_ref[7, pl.ds(row, size)] = middle
        return carry

    lax.fori_loop(0, count, faces, 0, unroll=2)


def yz_kernel(
    flow_in, change_in, source_in, z_below_in, z_above_in, y_below_in, y_above_in, next_out,
    y_below_ref, y_above_ref, flow_ref, change_ref, source_ref, cells_z, cells_y, step_ref, curve_ref, left_ref, right_ref, flux_ref,
    flow_sems, side_sems, out_sems,
):
    depth, height = flow_ref.shape[1:3]
    parts = flow_sems.shape[0]
    part = depth // parts
    pitch = height + 8
    first_y = 16
    first_z = 3 * height
    rows_z = depth * height
    loads = []
    for p in range(parts):
        here = pl.ds(p * part, part)
        loads.append(pltpu.make_async_copy(flow_in.at[:, here], flow_ref.at[:, here], flow_sems.at[p]))
    below = pltpu.make_async_copy(z_below_in, cells_z.at[:, pl.ds(0, first_z)], side_sems.at[0])
    above = pltpu.make_async_copy(z_above_in, cells_z.at[:, pl.ds(first_z + rows_z, first_z)], side_sems.at[1])
    change = pltpu.make_async_copy(change_in, change_ref, side_sems.at[2])
    source = pltpu.make_async_copy(source_in, source_ref, side_sems.at[3])
    y_below = pltpu.make_async_copy(y_below_in, y_below_ref, side_sems.at[4])
    y_above = pltpu.make_async_copy(y_above_in, y_above_ref, side_sems.at[5])
    for copy in [y_below, y_above] + loads + [below, above, change, source]:
        copy.start()
    y_below.wait()
    y_above.wait()

    def fill(z, carry):
        base = pl.multiple_of(first_y + z * pitch, 8)
        values = primitives([flow_ref[i, z] for i in range(7)])
        for i, value in enumerate(values):
            cells_z[i, pl.ds(pl.multiple_of(first_z + z * height, 8), height)] = value
            cells_y[i, pl.ds(base, height)] = value
            for j in range(3):
                cells_y[i, pl.ds(base - 3 + j, 1)] = y_below_ref[i, j, pl.ds(z, 1), :]
                cells_y[i, pl.ds(base + height + j, 1)] = y_above_ref[i, j, pl.ds(z, 1), :]
        return carry

    for p in range(parts):
        loads[p].wait()
        lax.fori_loop(p * part, (p + 1) * part, fill, 0)

    last_y = first_y + depth * pitch
    row_states(cells_y, step_ref, curve_ref, left_ref, right_ref, 1, first_y, last_y)
    row_faces(left_ref, right_ref, flux_ref, 1, first_y - 8, -(-(last_y - first_y + 8) // 32), 1)
    change.wait()

    def differences(base, lower, z):
        here, under = pl.ds(base, height), pl.ds(base - lower, height)
        diff = [flux_ref[i, under] - flux_ref[i, here] for i in range(7)]
        fraction = cells_z[6, pl.ds(pl.multiple_of(first_z + z * height, 8), height)]
        diff[6] = diff[6] + fraction * (flux_ref[7, here] - flux_ref[7, under])
        return diff

    def gather(z, carry):
        for i, diff in enumerate(differences(pl.multiple_of(first_y + z * pitch, 8), 1, z)):
            rows = pl.ds(pl.multiple_of(z * height, 8), height)
            change_ref[i, rows] = change_ref[i, rows] + diff
        return carry

    lax.fori_loop(0, depth, gather, 0)

    below.wait()
    above.wait()
    source.wait()
    row_states(cells_z, step_ref, curve_ref, left_ref, right_ref, height, first_z, first_z + rows_z)

    def update(z, carry):
        for i, diff in enumerate(differences(pl.multiple_of(first_z + z * height, 8), height, z)):
            total = change_ref[i, pl.ds(pl.multiple_of(z * height, 8), height)] + diff
            if i == 6:
                total = total - source_ref[z]
            flow_ref[i, z] = flow_ref[i, z] + time_step * total
        return carry

    saves = []
    row_faces(left_ref, right_ref, flux_ref, height, first_z - height, height // 32, 2)
    for p in range(parts):
        row_faces(left_ref, right_ref, flux_ref, height, first_z + p * part * height, part * height // 32, 2)
        lax.fori_loop(p * part, (p + 1) * part, update, 0)
        here = pl.ds(p * part, part)
        saves.append(pltpu.make_async_copy(flow_ref.at[:, here], next_out.at[:, here], out_sems.at[p]))
        saves[-1].start()
    for save in saves:
        save.wait()


def serve_kernel(asked_ref, pressure_ref, served_out, served_ref, sems, *, height):
    parts = sems.shape[0]
    sources = asked_ref.shape[0] // parts

    def one(src, carry):
        for r in range(HB):
            row = jnp.maximum(asked_ref[src, r], 0)
            slot = src * HB + r
            served_ref[slot, pl.ds(0, 2), :] = pressure_ref[pl.ds(row, 2), :]
            served_ref[slot, pl.ds(2, 2), :] = pressure_ref[pl.ds(row + height, 2), :]
        return carry

    saves = []
    for p in range(parts):
        lax.fori_loop(p * sources, (p + 1) * sources, one, 0, unroll=4)
        here = pl.ds(p * sources * HB, sources * HB)
        saves.append(pltpu.make_async_copy(served_ref.at[here], served_out.at[here], sems.at[p]))
        saves[-1].start()
    for save in saves:
        save.wait()


def scatter_kernel(asked_ref, returned_ref, source_ref, *sums):
    depth, height, length = source_ref.shape

    def clear(z, carry):
        for total in sums:
            total[pl.ds(pl.multiple_of(z * height, 8), height)] = jnp.zeros((height, length), F32)
        return carry

    lax.fori_loop(0, depth, clear, 0)

    def one(src, carry):
        for r in range(HB):
            total = sums[r % len(sums)]
            row = asked_ref[src, r]
            row = jnp.where(row < 0, depth * height, row)
            pair = src * PAIRS + 2 * r
            near, far = pl.ds(row, 2), pl.ds(row + height, 2)
            total[near] = total[near] + returned_ref[pair]
            total[far] = total[far] + returned_ref[pair + 1]
        return carry

    lax.fori_loop(0, asked_ref.shape[0], one, 0, unroll=4)

    def collect(z, carry):
        rows = pl.ds(pl.multiple_of(z * height, 8), height)
        value = sums[0][rows]
        for total in sums[1:]:
            value = value + total[rows]
        source_ref[z] = value
        return carry

    lax.fori_loop(0, depth, collect, 0)


half_log2e = 0.5 * math.log2(math.e)


def gaussian(distance):
    return jnp.exp2(-half_log2e * (distance * distance))


def across_rows(place_ref, block):
    lateral = lax.broadcasted_iota(jnp.int32, (8, 128), 0) % 4
    shift_z = (lateral // 2).astype(F32) - place_ref[0, pl.ds(block, 1), :]
    shift_y = (lateral % 2).astype(F32) - place_ref[1, pl.ds(block, 1), :]
    return jnp.exp2(-half_log2e * (shift_z * shift_z + shift_y * shift_y))


def across_total(place_ref):
    place_z, place_y = place_ref[0], place_ref[1]
    return (gaussian(place_z) + gaussian(1.0 - place_z)) * (gaussian(place_y) + gaussian(1.0 - place_y))


def deposit_kernel(
    tiles_ref, place_ref, radius_ref, speed_ref, slot_out, out_ref,
    slot_ref, wanted_ref, rate_ref, sem, *, depth, height, across_gy,
):
    length = out_ref.shape[2]
    blocks = radius_ref.shape[0]
    slot, wanted = find_slots(tiles_ref, wanted_ref.shape[0], depth, height, across_gy)
    slot_out[...] = slot
    wanted_ref[...] = wanted
    move = pltpu.make_async_copy(slot_out, slot_ref, sem)
    move.start()
    radius = radius_ref[...]
    rate_ref[...] = 4.0 * math.pi * radius * radius * speed_ref[...] * inverse(across_total(place_ref))
    upper = lax.broadcasted_iota(jnp.int32, (8, 128), 0) < 4

    def ask(k, carry):
        for j in range(8):
            home = k * 8 + j
            out_ref[home * PAIRS + 2 * HB, pl.ds(0, 1), :] = wanted_ref[pl.ds(home, 1), :]
        return carry

    lax.fori_loop(0, wanted_ref.shape[0] // 8, ask, 0)
    move.wait()

    def one(block):
        across = across_rows(place_ref, block)
        offset = place_ref[2, pl.ds(block, 1), :] * float(length - 1)
        along = gaussian(lax.broadcasted_iota(jnp.int32, (length, 128), 0).astype(F32) - offset)
        along_sum = jnp.sum(along, axis=0, keepdims=True)
        share = across * (rate_ref[pl.ds(block, 1), :] * inverse(along_sum))
        along_hi = along.astype(BF16)
        along_lo = (along - along_hi.astype(F32)).astype(BF16)
        share_hi = share.astype(BF16).astype(F32)
        both = jnp.where(upper, share_hi, share - share_hi).astype(BF16)
        only = jnp.where(upper, share_hi, 0.0).astype(BF16)
        result = dot_nt(
            jnp.concatenate([both, only], axis=1), jnp.concatenate([along_hi, along_lo], axis=1)
        )
        result = result[0:4] + result[4:8]
        pair = slot_ref[1, block]
        out_ref[pair] = result[0:2]
        out_ref[pair + 1] = result[2:4]

    size = math.gcd(blocks, 128)

    def several(k, carry):
        for j in range(size):
            one(k * size + j)
        return carry

    lax.fori_loop(0, blocks // size, several, 0)


def ready_kernel(place_ref, radius_ref, speed_ref, rest_ref, ready_ref):
    radius, speed, ratio = radius_ref[...], speed_ref[...], rest_ref[...]
    inv_radius = 1.0 / radius
    gas = (1.0 + 2.0 * surface_tension / (ratio * radius)) * jnp.exp(3.0 * polytropic * jnp.log(ratio))
    wall = gas - (2.0 * surface_tension + 4.0 * liquid_viscosity * speed) * inv_radius
    gas_rate = -3.0 * polytropic * gas * speed * inv_radius
    mach = speed / liquid_sound
    scale = time_step / ((1.0 - mach) * radius)
    ready_ref[0] = radius + time_step * speed
    ready_ref[1] = speed + scale * (
        (1.0 + mach) * (wall - pressure_mid)
        + radius * gas_rate / liquid_sound
        - 1.5 * (1.0 - mach / 3.0) * speed * speed
    )
    ready_ref[2] = scale * (1.0 + mach) * inverse(across_total(place_ref))


def sample_kernel(slot_ref, place_ref, ready_ref, rows_ref, motion_ref, total_ref, width_ref):
    blocks = width_ref.shape[0]
    length = rows_ref.shape[2]
    upper = lax.broadcasted_iota(jnp.int32, (8, 128), 0) < 4
    motion_ref[0] = ready_ref[0]

    def one(block):
        value = rows_ref[slot_ref[0, block]] - pressure_mid
        value = jnp.concatenate([value, value], axis=0)
        high = value.astype(BF16).astype(F32)
        both = jnp.where(upper, high, value - high)
        both = jnp.concatenate([both, jnp.ones_like(both)], axis=0).astype(BF16)
        offset = place_ref[2, pl.ds(block, 1), :] * float(length - 1)
        along = gaussian(lax.broadcasted_iota(jnp.int32, (length, 128), 0).astype(F32) - offset)
        result = dot_nn(both, along.astype(BF16))
        total_ref[pl.ds(pl.multiple_of(block * 8, 8), 8)] = across_rows(place_ref, block) * result[0:8]
        width_ref[pl.ds(block, 1), :] = result[8:9]

    size = math.gcd(blocks, 256)

    def several(k, carry):
        for j in range(size):
            one(k * size + j)
        return carry

    lax.fori_loop(0, blocks // size, several, 0)
    total = total_ref[pl.ds(0, blocks, stride=8), :]
    for row in range(1, 8):
        total = total + total_ref[pl.ds(row, blocks, stride=8), :]
    motion_ref[1] = ready_ref[1] - ready_ref[2] * (total * inverse(width_ref[...]))


def shift_both(low_layers, high_layers, axis):
    count = lax.axis_size(axis)
    below = lax.ppermute(high_layers, axis, [(i, (i + 1) % count) for i in range(count)])
    above = lax.ppermute(low_layers, axis, [((i + 1) % count, i) for i in range(count)])
    return below, above


def exchange(values):
    return lax.all_to_all(values, ("gz", "gy"), split_axis=0, concat_axis=0, tiled=True)


def body(flow_state, block_tiles, bubble_place, bubble_radius, bubble_speed, rest_ratio):
    _, depth, height, length = flow_state.shape
    across_gy = lax.axis_size("gy")
    devices = lax.axis_size("gz") * across_gy
    blocks = block_tiles.shape[0]
    slots = devices * HB
    field = (7, depth, height, length)

    slot, outgoing = pl.pallas_call(
        functools.partial(deposit_kernel, depth=depth, height=height, across_gy=across_gy),
        out_shape=(
            shape((2, blocks), jnp.int32),
            shape((devices * PAIRS, 2, length)),
        ),
        in_specs=[VMEM] * 4,
        out_specs=(VMEM, VMEM),
        scratch_shapes=[
            pltpu.SMEM((2, blocks), jnp.int32),
            pltpu.VMEM((devices, 128), F32),
            pltpu.VMEM((blocks, 128), F32),
            pltpu.SemaphoreType.DMA,
        ],
        compiler_params=params(),
        cost_estimate=cost(10),
        name="deposit",
    )(block_tiles.T, bubble_place, bubble_radius, bubble_speed)
    returned = exchange(outgoing)

    flow_state, rest_ratio, _ = lax.optimization_barrier((flow_state, rest_ratio, outgoing))
    rows = depth * height
    groups = rows // 128
    turned = 16 + groups * (length + 8) + 80
    change_x, pressure, z_low, z_high, y_low, y_high = pl.pallas_call(
        x_kernel,
        out_shape=(
            shape((7, rows, length)),
            shape((depth, height, length)),
            shape((7, 3 * height, length)),
            shape((7, 3 * height, length)),
            shape((7, 3, depth, length)),
            shape((7, 3, depth, length)),
        ),
        in_specs=[ANY],
        out_specs=(ANY,) + (VMEM,) * 5,
        scratch_shapes=[
            pltpu.VMEM(field, F32),
            pltpu.VMEM((7, rows, length), F32),
            pltpu.VMEM((7, turned, 128), F32),
            pltpu.VMEM((turned, 128), F32),
            pltpu.VMEM((turned, 128), F32),
            pltpu.VMEM((7, turned, 128), F32),
            pltpu.VMEM((7, turned, 128), F32),
            pltpu.VMEM((8, turned, 128), F32),
            pltpu.SemaphoreType.DMA((groups,)),
            pltpu.SemaphoreType.DMA((groups,)),
        ],
        compiler_params=params(56),
        cost_estimate=cost(14),
        name="sweep_x",
    )(flow_state)
    y_below, y_above = shift_both(y_low, y_high, "gy")
    z_below, z_above = shift_both(z_low, z_high, "gz")
    ready = pl.pallas_call(
        ready_kernel,
        out_shape=shape((3, blocks, 128)),
        in_specs=[VMEM] * 4,
        out_specs=VMEM,
        compiler_params=params(56),
        cost_estimate=cost(2),
        name="ready",
    )(bubble_place, bubble_radius, bubble_speed, rest_ratio)
    returned, change_x, ready = lax.optimization_barrier((returned, change_x, ready))

    asked = returned.reshape(devices, PAIRS, 2, length)[:, 2 * HB, 0, :HB].astype(jnp.int32)
    served = pl.pallas_call(
        functools.partial(serve_kernel, height=height),
        out_shape=shape((slots, 4, length)),
        in_specs=[SMEM, VMEM],
        out_specs=ANY,
        scratch_shapes=[pltpu.VMEM((slots, 4, length), F32), pltpu.SemaphoreType.DMA((4,))],
        compiler_params=params(56),
        cost_estimate=cost(5),
        name="serve",
    )(asked, pressure.reshape(rows, length))
    fetched = exchange(served)

    returned, asked, change_x, served = lax.optimization_barrier((returned, asked, change_x, served))
    source = pl.pallas_call(
        scatter_kernel,
        out_shape=shape((depth, height, length)),
        in_specs=[SMEM, VMEM],
        out_specs=VMEM,
        scratch_shapes=[pltpu.VMEM(((depth + 2) * height, length), F32)] * 4,
        compiler_params=params(56),
        cost_estimate=cost(6),
        name="scatter",
    )(asked, returned)

    padded = 16 + depth * (height + 8) + 80
    state_next = pl.pallas_call(
        yz_kernel,
        out_shape=shape(field),
        in_specs=[ANY] * 7,
        out_specs=ANY,
        scratch_shapes=[
            pltpu.VMEM((7, 3, depth, length), F32),
            pltpu.VMEM((7, 3, depth, length), F32),
            pltpu.VMEM(field, F32),
            pltpu.VMEM((7, rows, length), F32),
            pltpu.VMEM((depth, height, length), F32),
            pltpu.VMEM((7, rows + 6 * height, length), F32),
            pltpu.VMEM((7, padded, length), F32),
            pltpu.VMEM((padded, length), F32),
            pltpu.VMEM((padded, length), F32),
            pltpu.VMEM((7, padded, length), F32),
            pltpu.VMEM((7, padded, length), F32),
            pltpu.VMEM((8, padded, length), F32),
            pltpu.SemaphoreType.DMA((4,)),
            pltpu.SemaphoreType.DMA((6,)),
            pltpu.SemaphoreType.DMA((4,)),
        ],
        compiler_params=params(),
        cost_estimate=cost(24),
        name="sweep_yz",
    )(flow_state, change_x, source, z_below, z_above, y_below, y_above)

    fetched, state_next = lax.optimization_barrier((fetched, state_next))
    motion = pl.pallas_call(
        sample_kernel,
        out_shape=shape((2, blocks, 128)),
        in_specs=[SMEM] + [VMEM] * 3,
        out_specs=VMEM,
        scratch_shapes=[pltpu.VMEM((blocks * 8, 128), F32), pltpu.VMEM((blocks, 128), F32)],
        compiler_params=params(),
        cost_estimate=cost(7),
        name="sample",
    )(slot, bubble_place, ready, fetched)
    return state_next, source, motion


def solution(mesh):
    in_specs = (
        P(None, "gz", "gy", None),
        P(("gz", "gy"), None),
        P(None, ("gz", "gy"), None),
        P(("gz", "gy"), None),
        P(("gz", "gy"), None),
        P(("gz", "gy"), None),
    )
    out_specs = (P(None, "gz", "gy", None), P("gz", "gy", None), P(None, ("gz", "gy"), None))
    return jax.shard_map(body, mesh=mesh, in_specs=in_specs, out_specs=out_specs, check_vma=False)
```
